32 devices in a mesh: dp: 4 (over y, x), ctx: 8 (over z, core).
Axes of the slice: x: 2, y: 2, z: 4, core: 2. Of those that a mesh axis runs over, the one named last changes fastest.
Arguments:
- queries: bfloat16 [4, 1024, 4096], P('dp', 'ctx'), may hold values from -80 to 80
- key_tokens: bfloat16 [4, 1024, 1024], P('dp', 'ctx'), may hold values from -80 to 80
- value_tokens: bfloat16 [4, 1024, 1024], P('dp', 'ctx'), may hold values from -6 to 6
- cotangent: bfloat16 [4, 1024, 4096], P('dp', 'ctx'), may hold values from -6 to 6
- query_map: bfloat16 [32, 128, 64], replicated, may hold values from -4 to 4
- key_map: bfloat16 [32, 128, 64], replicated, may hold values from -4 to 4
Outputs:
- attended: bfloat16 [4, 1024, 4096], P('dp', 'ctx')
- grad_query_map: float32 [32, 128, 64], replicated
- grad_key_map: float32 [32, 128, 64], replicated
The draws below stay inside these ranges and needn't reach their ends.
All inputs are finite; a program needn't handle non-finite values.
Results may differ from the reference program's by a relative error of at most 0.015.
Values sent between devices are 32-bit elements; how exact they have to be, the bound alone decides.
No kernel may reach another device: no remote copies, remote signals or barrier semaphores. Data moves between devices by JAX's collectives and lax.ppermute only.
A program may use at most 320 MiB of HBM per device.

```python
import math
import jax
import jax.numpy as jnp
from jax import lax

HEADS = 32
KV_HEADS = 8
HEAD_DIM = 128
HALF_FEAT = 64
TOK_DEV = 128
LENGTH = 1024
SEQS = 4
N_CTX = 8


def token_rows(key, width):
    shape = (SEQS, LENGTH, width)
    return jax.random.truncated_normal(key, -6.0, 6.0, shape, jnp.float32)


def map_rows(key):
    shape = (HEADS, HEAD_DIM, HALF_FEAT)
    return jax.random.truncated_normal(key, -4.0, 4.0, shape, jnp.float32) / math.sqrt(HEAD_DIM)


def draw_queries(key, part):
    return token_rows(jax.random.fold_in(key, 11), HEADS * HEAD_DIM).astype(jnp.bfloat16)


def draw_key_tokens(key, part):
    return token_rows(jax.random.fold_in(key, 23), KV_HEADS * HEAD_DIM).astype(jnp.bfloat16)


def draw_query_map(key, part):
    return map_rows(jax.random.fold_in(key, 37)).astype(jnp.bfloat16)


def draw_key_map(key, part):
    return map_rows(jax.random.fold_in(key, 41)).astype(jnp.bfloat16)


def block_levels(own_key, dims, cuts, smallest, top_value):
    def one(dim, shards_of):
        heights = jax.random.uniform(jax.random.fold_in(jax.random.fold_in(own_key, 6), dim), (shards_of,), jnp.float32, smallest / len(cuts), top_value / len(cuts))
        return jnp.repeat(jnp.exp(heights), dims[dim] // shards_of).reshape((-1,) + (1,) * (len(dims) - dim - 1))

    loudness = one(*cuts[0])
    for cut in cuts[1:]:
        loudness = loudness * one(*cut)
    return loudness


def noise(own_key, extent, scale, limit, cuts=(), dtype=jnp.bfloat16):
    level = block_levels(own_key, extent, cuts, -0.22, 0.18) if cuts else 1.0
    array = jax.random.normal(own_key, extent, jnp.float32) * scale * level
    return jnp.minimum(jnp.maximum(array, -limit), limit).astype(dtype)


def setup_inputs(seed: int = 0) -> dict:
    key_list = jax.random.split(jax.random.key(seed), 7)
    queries = draw_queries(jax.random.fold_in(key_list[6], 71), 0)
    key_tokens = draw_key_tokens(jax.random.fold_in(key_list[6], 71), 0)
    value_tokens = noise(key_list[2], (SEQS, LENGTH, KV_HEADS * HEAD_DIM), 1.0, 6.0, ((0, 4), (1, 8)))
    cotangent = noise(key_list[3], (SEQS, LENGTH, HEADS * HEAD_DIM), 1.0, 6.0, ((0, 4), (1, 8)))
    query_map = draw_query_map(jax.random.fold_in(key_list[6], 71), 0)
    key_map = draw_key_map(jax.random.fold_in(key_list[6], 71), 0)
    return dict(queries=queries, key_tokens=key_tokens, value_tokens=value_tokens, cotangent=cotangent, query_map=query_map, key_map=key_map)


PRECISE = lax.Precision.HIGHEST


def feature_map(block_rows, weight):
    scores = jnp.einsum('lhe,hef->lhf', block_rows.astype(jnp.float32), weight.astype(jnp.float32))
    positive = jax.nn.softmax(scores, axis=-1)
    negative = jax.nn.softmax(-scores, axis=-1)
    return positive, negative, jnp.concatenate([positive, negative], axis=-1).astype(jnp.bfloat16)


def feature_back(positive, negative, upstream):
    split_at = positive.shape[-1]
    upper_half = upstream[..., :split_at]
    lower_half = upstream[..., split_at:]
    result = positive * (upper_half - jnp.sum(positive * upper_half, axis=-1, keepdims=True))
    result = result - negative * (lower_half - jnp.sum(negative * lower_half, axis=-1, keepdims=True))
    return result.astype(jnp.bfloat16)


def causal_mask(length):
    row_index = lax.broadcasted_iota(jnp.int32, (length, length), 0)
    col_index = lax.broadcasted_iota(jnp.int32, (length, length), 1)
    return row_index >= col_index


def attend(query_feat, key_feat, value_block, prefix_state, prefix_norm, causal):
    scores = jnp.einsum('thf,shf->hts', query_feat.astype(jnp.float32), key_feat.astype(jnp.float32))
    weights = jnp.where(causal[None], scores, 0.0).astype(jnp.bfloat16)
    numerator = jnp.einsum('hts,she->the', weights.astype(jnp.float32), value_block.astype(jnp.float32))
    numerator = numerator + jnp.einsum('thf,hfe->the', query_feat.astype(jnp.float32), prefix_state, precision=PRECISE)
    denominator = jnp.sum(weights.astype(jnp.float32), axis=-1).T
    denominator = denominator + jnp.einsum('thf,hf->th', query_feat.astype(jnp.float32), prefix_norm, precision=PRECISE)
    return numerator, denominator


def reference(queries, key_tokens, value_tokens, cotangent, query_map, key_map):
    causal = causal_mask(TOK_DEV)
    block_shape = (N_CTX, TOK_DEV, HEADS, HEAD_DIM)
    shared_shape = (N_CTX, TOK_DEV, KV_HEADS, HEAD_DIM)
    features = 2 * HALF_FEAT
    group_size = HEADS // KV_HEADS

    def one_sequence(inputs):
        query_seq, key_seq, value_seq, grad_seq = inputs
        query_blocks = query_seq.reshape(block_shape)
        key_blocks = jnp.repeat(key_seq.reshape(shared_shape), group_size, axis=2)
        value_blocks = jnp.repeat(value_seq.reshape(shared_shape), group_size, axis=2)
        grad_blocks = grad_seq.reshape(block_shape)

        def forward_step(carry, pieces):
            prefix_state, prefix_norm = carry
            query_block, key_block, value_block = pieces
            query_pos, query_neg, query_feat = feature_map(query_block, query_map)
            key_pos, key_neg, key_feat = feature_map(key_block, key_map)
            numerator, denominator = attend(query_feat, key_feat, value_block, prefix_state, prefix_norm, causal)
            attended = (numerator / denominator[..., None]).astype(jnp.bfloat16)
            next_state = prefix_state + jnp.einsum('shf,she->hfe', key_feat.astype(jnp.float32), value_block.astype(jnp.float32))
            next_norm = prefix_norm + jnp.sum(key_feat.astype(jnp.float32), axis=0)
            return (next_state, next_norm), (attended, prefix_state, prefix_norm)

        start = (jnp.zeros((HEADS, features, HEAD_DIM), jnp.float32), jnp.zeros((HEADS, features), jnp.float32))
        unused_carry, (attended, states, norms) = lax.scan(forward_step, start, (query_blocks, key_blocks, value_blocks))

        def backward_step(carry, pieces):
            suffix_state, suffix_norm, query_grad, key_grad = carry
            query_block, key_block, value_block, grad_block, prefix_state, prefix_norm = pieces
            query_pos, query_neg, query_feat = feature_map(query_block, query_map)
            key_pos, key_neg, key_feat = feature_map(key_block, key_map)
            numerator, denominator = attend(query_feat, key_feat, value_block, prefix_state, prefix_norm, causal)
            upstream = grad_block.astype(jnp.float32)
            scaled = (upstream / denominator[..., None]).astype(jnp.bfloat16)
            norm_grad = -jnp.sum(upstream * numerator, axis=-1) / (denominator * denominator)
            mixed = jnp.einsum('the,she->hts', scaled.astype(jnp.float32), value_block.astype(jnp.float32)) + norm_grad.T[:, :, None]
            block_grads = jnp.where(causal[None], mixed, 0.0).astype(jnp.bfloat16)
            query_feat_grad = jnp.einsum('hts,shf->thf', block_grads.astype(jnp.float32), key_feat.astype(jnp.float32))
            query_feat_grad = query_feat_grad + jnp.einsum('hfe,the->thf', prefix_state, scaled.astype(jnp.float32), precision=PRECISE)
            query_feat_grad = query_feat_grad + prefix_norm[None] * norm_grad[..., None]
            key_feat_grad = jnp.einsum('hts,thf->shf', block_grads.astype(jnp.float32), query_feat.astype(jnp.float32))
            key_feat_grad = key_feat_grad + jnp.einsum('hfe,she->shf', suffix_state, value_block.astype(jnp.float32), precision=PRECISE)
            key_feat_grad = key_feat_grad + suffix_norm[None]
            query_score_grad = feature_back(query_pos, query_neg, query_feat_grad)
            key_score_grad = feature_back(key_pos, key_neg, key_feat_grad)
            query_grad = query_grad + jnp.einsum('lhe,lhf->hef', query_block.astype(jnp.float32), query_score_grad.astype(jnp.float32))
            key_grad = key_grad + jnp.einsum('lhe,lhf->hef', key_block.astype(jnp.float32), key_score_grad.astype(jnp.float32))
            next_state = suffix_state + jnp.einsum('thf,the->hfe', query_feat.astype(jnp.float32), scaled.astype(jnp.float32))
            next_norm = suffix_norm + jnp.einsum('thf,th->hf', query_feat.astype(jnp.float32), norm_grad, precision=PRECISE)
            return (next_state, next_norm, query_grad, key_grad), None

        grad_start = (jnp.zeros((HEADS, features, HEAD_DIM), jnp.float32), jnp.zeros((HEADS, features), jnp.float32),
                      jnp.zeros((HEADS, HEAD_DIM, HALF_FEAT), jnp.float32), jnp.zeros((HEADS, HEAD_DIM, HALF_FEAT), jnp.float32))
        final, unused_out = lax.scan(backward_step, grad_start,
                                     (query_blocks, key_blocks, value_blocks, grad_blocks, states, norms), reverse=True)
        return attended.reshape(LENGTH, HEADS * HEAD_DIM), final[2], final[3]

    attended, query_grads, key_grads = lax.map(one_sequence, (queries, key_tokens, value_tokens, cotangent))
    return attended, jnp.sum(query_grads, axis=0), jnp.sum(key_grads, axis=0)
```

```python
import jax
import jax.numpy as jnp
from jax import lax
from jax.experimental import pallas as pl
from jax.experimental.pallas import tpu as pltpu
from jax.sharding import PartitionSpec as P

BF = jnp.bfloat16
F32 = jnp.float32
VMEM_LIMIT = 40 * 1024 * 1024


def mm(a, b):
    return jnp.dot(a, b, preferred_element_type=F32)


def mm_nt(a, b):
    return lax.dot_general(a, b, (((1,), (1,)), ((), ())), preferred_element_type=F32)


def mm_tn(a, b):
    return lax.dot_general(a, b, (((0,), (0,)), ((), ())), preferred_element_type=F32)


def split(x):
    high = x.astype(BF)
    return high, (x - high.astype(F32)).astype(BF)


def soft(scores):
    top = jnp.max(scores, axis=0, keepdims=True)
    raised = jnp.exp(scores - top)
    return raised * (1.0 / jnp.sum(raised, axis=0, keepdims=True))


def both_soft(scores):
    return jnp.concatenate([soft(scores), soft(-scores)], axis=0)


def soft_back(probs, upstream):
    half = probs.shape[0] // 2
    p, n = probs[:half], probs[half:]
    gp, gn = upstream[:half], upstream[half:]
    result = p * (gp - jnp.sum(p * gp, axis=0, keepdims=True))
    result = result - n * (gn - jnp.sum(n * gn, axis=0, keepdims=True))
    return result.astype(BF)


def causal_mask(length):
    rows = lax.broadcasted_iota(jnp.int32, (length, length), 0)
    cols = lax.broadcasted_iota(jnp.int32, (length, length), 1)
    return rows >= cols


def outer(row_a, row_b):
    ah, al = split(row_a)
    bh, bl = split(row_b)
    zero_a = jnp.zeros((13, row_a.shape[1]), F32)
    zero_b = jnp.zeros((13, row_b.shape[1]), F32)
    a = jnp.concatenate([ah.astype(F32), al.astype(F32), ah.astype(F32), zero_a], axis=0).astype(BF)
    b = jnp.concatenate([bh.astype(F32), bh.astype(F32), bl.astype(F32), zero_b], axis=0).astype(BF)
    return mm_tn(a, b)


def denominators(weights, query_rows, norm_row):
    lanes = weights.shape[1]
    high, low = split(jnp.broadcast_to(norm_row, (lanes, norm_row.shape[1])))
    ones = jnp.ones((lanes, lanes), BF)
    return mm(weights, ones) + mm_nt(query_rows, high) + mm_nt(query_rows, low)


def put_half(own_ref, other_ref, value):
    half = pl.program_id(1)

    @pl.when(half == 0)
    def _():
        own_ref[...] = value

    @pl.when(half == 1)
    def _():
        other_ref[...] = value


def key_kernel(order, k_ref, v_ref, w_ref, kp_ref, own_ref, other_ref, norm_ref):
    group, dim, width = w_ref.shape
    length = k_ref.shape[0]
    maps = jnp.concatenate([w_ref[i].T for i in range(group)], axis=0)
    scores = mm_nt(maps, k_ref[...])
    probs = jnp.concatenate(
        [both_soft(scores[i * width : (i + 1) * width]) for i in range(group)], axis=0
    )
    kp_ref[0, 0] = probs
    features = probs.astype(BF)
    put_half(own_ref, other_ref, mm(features, v_ref[...]))
    norm_ref[0, 0] = mm_nt(jnp.ones((16, length), BF), features)[:1]


def query_kernel(order, q_ref, c_ref, w_ref, kp_ref, pn_ref, qp_ref, wt_ref, own_ref, other_ref):
    group, dim, width = w_ref.shape
    length = q_ref.shape[0]
    causal = causal_mask(length)
    sums = []
    for i in range(group):
        cols = slice(i * dim, (i + 1) * dim)
        rows = slice(i * 2 * width, (i + 1) * 2 * width)
        probs = both_soft(mm_nt(w_ref[i].T, q_ref[:, cols]))
        qp_ref[0, 0, rows] = probs
        query_t = probs.astype(BF)
        query_rows = query_t.T
        key_t = kp_ref[0, 0, rows].astype(BF)
        weights = jnp.where(causal, mm(query_rows, key_t), 0.0).astype(BF)
        wt_ref[0, 0, i] = weights
        den = denominators(weights, query_rows, pn_ref[0, 0, :, rows])
        scaled = (c_ref[:, cols].astype(F32) * (1.0 / den)).astype(BF)
        sums.append(mm(query_t, scaled))
    put_half(own_ref, other_ref, jnp.concatenate(sums, axis=0))


def middle_kernel(
    order, q_ref, c_ref, v_ref, kp_ref, qp_ref, wt_ref, pn_ref, so_ref, st_ref,
    att_ref, own_ref, other_ref, gk_ref, sn_ref,
):
    group, length = wt_ref.shape[2], wt_ref.shape[3]
    dim = v_ref.shape[1]
    causal = causal_mask(length)
    half = pl.program_id(1)
    values = v_ref[...]
    ones = jnp.ones((2 * dim, length), BF)
    ones_rows = jnp.ones((16, 2 * dim), BF)
    feats = qp_ref.shape[2] // group
    grads = []
    for i in range(group):
        cols = slice(i * dim, (i + 1) * dim)
        rows = slice(i * feats, (i + 1) * feats)
        state = jnp.where(half == 0, so_ref[rows], st_ref[rows])
        high, low = split(state)
        norm_row = pn_ref[0, 0, :, rows]
        probs = qp_ref[0, 0, rows]
        query_t = probs.astype(BF)
        query_rows = query_t.T
        key_t = kp_ref[0, 0, rows].astype(BF)
        weights = wt_ref[0, 0, i]
        inverse = 1.0 / denominators(weights, query_rows, norm_row)
        numerator = mm(
            jnp.concatenate([weights, query_rows], axis=1),
            jnp.concatenate([values, high], axis=0),
        ) + mm(query_rows, low)
        att_ref[:, cols] = (numerator * inverse).astype(BF)
        upstream = c_ref[:, cols].astype(F32)
        scaled_wide = upstream * inverse
        scaled = scaled_wide.astype(BF)
        product = jnp.concatenate(split(-(scaled_wide * inverse) * numerator), axis=1)
        norm_grad = mm(product, ones)
        norm_grad_row = mm_nt(ones_rows, product)[:1]
        mixed = mm_nt(scaled, values) + norm_grad
        block = jnp.where(causal, mixed, 0.0).astype(BF)
        upstream_q = mm_nt(
            jnp.concatenate([key_t, high], axis=1), jnp.concatenate([block, scaled], axis=1)
        )
        upstream_q = upstream_q + mm_nt(low, scaled) + outer(norm_row, norm_grad_row)
        grads.append(mm(soft_back(probs, upstream_q), q_ref[:, cols]))
        gk_ref[0, 0, rows] = mm(query_t, block)
        grad_high, grad_low = split(jnp.broadcast_to(norm_grad_row, (16, length)))
        sn_ref[0, 0, :, rows] = (mm(grad_high, query_rows) + mm(grad_low, query_rows))[:1]
    put_half(own_ref, other_ref, jnp.concatenate(grads, axis=0))


def last_kernel(
    order, k_ref, v_ref, kp_ref, gk_ref, sn_ref, to_ref, tt_ref, own_ref, other_ref
):
    half = pl.program_id(1)
    rows = kp_ref.shape[2]
    length = k_ref.shape[0]
    state = jnp.where(half == 0, to_ref[...], tt_ref[...])
    high, low = split(state)
    values = v_ref[...]
    upstream = gk_ref[0, 0] + mm_nt(
        jnp.concatenate([high, low], axis=1), jnp.concatenate([values, values], axis=1)
    )
    upstream = upstream + outer(sn_ref[0, 0], jnp.ones((1, length), F32))
    probs = kp_ref[0, 0]
    dim = k_ref.shape[1]
    feats = dim
    back = [
        soft_back(probs[a : a + feats], upstream[a : a + feats]) for a in range(0, rows, feats)
    ]
    put_half(own_ref, other_ref, mm(jnp.concatenate(back, axis=0), k_ref[...]))


def out_kernel(order, x_ref, o_ref):
    group, dim, width = o_ref.shape
    for i in range(group):
        o_ref[i] = x_ref[0, i * width : (i + 1) * width].T


def core_swap(x):
    size = lax.axis_size("ctx")
    return lax.ppermute(x, "ctx", [(i, i ^ 1) for i in range(size)])


def chip_move(x, pairs):
    return lax.ppermute(x, "ctx", [(2 * a + c, 2 * b + c) for a, b in pairs for c in (0, 1)])


def chip_before(x, chip, chips, forward):
    turn = (lambda a: a) if forward else (lambda a: chips - 1 - a)
    place = chip if forward else chips - 1 - chip

    def move(y, pairs):
        return chip_move(y, [(turn(a), turn(b)) for a, b in pairs])

    if chips == 4:
        rows = x.shape[0] // 2
        a, b = x[:rows], x[rows:]
        near = move(jnp.where(place == 1, b, a), [(0, 1), (1, 2), (2, 3)])
        far = move(b, [(0, 2)])
        second = jnp.where(place == 1, a + near, jnp.where(place == 2, b + near + far, b))
        near2 = move(second, [(0, 1), (1, 2), (2, 3)])
        far2 = move(second, [(1, 3)])
        first_half = jnp.where(place == 2, near2, near + far2)
        second_half = jnp.where(place == 2, near + far, near2)
        return jnp.concatenate([first_half, second_half], axis=0)
    total = move(x, [(i, i + 1) for i in range(chips - 1)])
    step = 1
    while step < chips:
        total = total + move(total, [(i, i + step) for i in range(chips - step)])
        step *= 2
    return total


def scan_states(own, other, chip, core, chips, forward):
    got = core_swap(other)
    before = chip_before(own + got, chip, chips, forward)
    second = core == 1 if forward else core == 0
    mine = before + jnp.where(second, got, 0.0)
    sent = before + jnp.where(second, 0.0, own)
    return mine, core_swap(sent)


def scan_norms(norm, chip, core, chips, forward):
    got = core_swap(norm)[:, ::-1]
    second = core == 1 if forward else core == 0
    base = jnp.where(second, got, 0.0)
    total = norm + got
    if chips & (chips - 1):
        before = chip_before(total.reshape(-1, total.shape[-1]), chip, chips, forward)
        return base + before.reshape(total.shape)
    bit = 1
    while bit < chips:
        moved = chip_move(total, [(i, i ^ bit) for i in range(chips)])
        upper = (chip & bit) != 0 if forward else (chip & bit) == 0
        base = base + jnp.where(upper, moved, 0.0)
        total = total + moved
        bit *= 2
    return base


def sum_all(own, other, chips):
    mine = own + core_swap(other)
    dp = lax.axis_size("dp")
    parts = mine.shape[0]
    if dp & (dp - 1) or parts % dp or chips & (chips - 1) or parts & (parts - 1):
        mine = lax.psum(mine, "dp")
        total = sum_chips(mine, chips)
        return jnp.concatenate([total, core_swap(total)], axis=0)
    share = parts // dp
    got = [
        lax.ppermute(mine[k * share : (k + 1) * share], "dp", [(i, i ^ k) for i in range(dp)])
        for k in range(1, dp)
    ]
    total = mine[:share]
    for piece in got:
        total = total + piece
    total = sum_chips(total, chips)
    pieces = [total] + [
        lax.ppermute(total, "dp", [(i, i ^ k) for i in range(dp)]) for k in range(1, dp)
    ]
    full = jnp.concatenate(pieces, axis=0)
    return jnp.concatenate([full, core_swap(full)], axis=0)


def sum_chips(total, chips):
    if chips & (chips - 1):
        size = 2 * chips
        return lax.psum(
            total, "ctx", axis_index_groups=[list(range(c, size, 2)) for c in (0, 1)]
        )
    bit = 1
    while bit < chips:
        total = total + chip_move(total, [(i, i ^ bit) for i in range(chips)])
        bit *= 2
    return total


def shards(queries, key_tokens, value_tokens, cotangent, query_map, key_map):
    length = queries.shape[1]
    head_count, dim, width = query_map.shape
    shared = key_tokens.shape[2] // dim
    group = head_count // shared
    feats = 2 * width
    n = shared // 2
    wide = group * feats
    queries = queries.reshape(length, head_count * dim)
    cotangent = cotangent.reshape(length, head_count * dim)
    keys = key_tokens.reshape(length, shared * dim)
    values = value_tokens.reshape(length, shared * dim)

    ctx = lax.axis_index("ctx")
    chips = lax.axis_size("ctx") // 2
    chip, core = ctx // 2, ctx % 2
    dp = lax.axis_size("dp")
    turn = lax.axis_index("dp") * (n // dp) if n % dp == 0 and n & (n - 1) == 0 else 0
    part = jnp.arange(n, dtype=jnp.int32) ^ turn
    order = jnp.concatenate([part + n * core, part + n * (1 - core)]).astype(jnp.int32)
    heads = jnp.arange(shared, dtype=jnp.int32)
    back = jnp.where(heads // n == core, 0, n) + ((heads % n) ^ turn)
    back = back.astype(jnp.int32)

    def head_cols(rows, cols):
        return pl.BlockSpec((rows, cols), lambda i, s, order: (0, order[s * n + i]))

    map_spec = pl.BlockSpec((group, dim, width), lambda i, s, order: (order[s * n + i], 0, 0))
    kept_spec = pl.BlockSpec((1, 1, wide, length), lambda i, s, order: (i, s, 0, 0))
    kept = jax.ShapeDtypeStruct((n, 2, wide, length), F32)
    row_spec = pl.BlockSpec((1, 1, 1, wide), lambda i, s, order: (i, s, 0, 0))
    row = jax.ShapeDtypeStruct((n, 2, 1, wide), F32)
    weight_spec = pl.BlockSpec((1, 1, group, length, length), lambda i, s, order: (i, s, 0, 0, 0))
    weight = jax.ShapeDtypeStruct((n, 2, group, length, length), BF)

    def half_spec(rows):
        return pl.BlockSpec((rows, dim), lambda i, s, order: (i, 0))

    def call(name, body, in_specs, out_specs, out_shape):
        return pl.pallas_call(
            body,
            name=name,
            out_shape=out_shape,
            grid_spec=pltpu.PrefetchScalarGridSpec(
                num_scalar_prefetch=1, grid=(n, 2), in_specs=in_specs, out_specs=out_specs
            ),
            compiler_params=pltpu.CompilerParams(vmem_limit_bytes=VMEM_LIMIT),
        )

    state = jax.ShapeDtypeStruct((n * wide, dim), F32)
    grad = jax.ShapeDtypeStruct((n * group * width, dim), F32)
    token = head_cols(length, dim)
    wide_token = head_cols(length, group * dim)

    key_probs, own, other, norm = call(
        "key_features",
        key_kernel,
        [token, token, map_spec],
        [kept_spec, half_spec(wide), half_spec(wide), row_spec],
        [kept, state, state, row],
    )(order, keys, values, key_map)
    prefix_norm = scan_norms(norm, chip, core, chips, True)
    prefix_own, prefix_other = scan_states(own, other, chip, core, chips, True)

    query_probs, weights, own, other = call(
        "query_features",
        query_kernel,
        [wide_token, wide_token, map_spec, kept_spec, row_spec],
        [kept_spec, weight_spec, half_spec(wide), half_spec(wide)],
        [kept, weight, state, state],
    )(order, queries, cotangent, query_map, key_probs, prefix_norm)
    suffix_own, suffix_other = scan_states(own, other, chip, core, chips, False)

    attended, query_own, query_other, key_up, norm = call(
        "attend",
        middle_kernel,
        [wide_token, wide_token, token, kept_spec, kept_spec, weight_spec, row_spec]
        + [half_spec(wide)] * 2,
        [wide_token, half_spec(group * width), half_spec(group * width), kept_spec, row_spec],
        [jax.ShapeDtypeStruct((length, head_count * dim), BF), grad, grad, kept, row],
    )(order, queries, cotangent, values, key_probs, query_probs, weights, prefix_norm, prefix_own, prefix_other)
    suffix_norm = scan_norms(norm, chip, core, chips, False)

    key_own, key_other = call(
        "key_grads",
        last_kernel,
        [token, token, kept_spec, kept_spec, row_spec] + [half_spec(wide)] * 2,
        [half_spec(group * width)] * 2,
        [grad, grad],
    )(order, keys, values, key_probs, key_up, suffix_norm, suffix_own, suffix_other)

    def finish(name, own, other):
        shape = (n, group * width, dim)
        total = sum_all(own.reshape(shape), other.reshape(shape), chips)
        return pl.pallas_call(
            out_kernel,
            name=name,
            out_shape=jax.ShapeDtypeStruct((head_count, dim, width), F32),
            grid_spec=pltpu.PrefetchScalarGridSpec(
                num_scalar_prefetch=1,
                grid=(shared,),
                in_specs=[pl.BlockSpec((1, group * width, dim), lambda i, back: (back[i], 0, 0))],
                out_specs=pl.BlockSpec((group, dim, width), lambda i, back: (i, 0, 0)),
            ),
            compiler_params=pltpu.CompilerParams(vmem_limit_bytes=VMEM_LIMIT),
        )(back, total)

    query_grad = finish("query_out", query_own, query_other)
    key_grad = finish("key_out", key_own, key_other)
    return attended.reshape(1, length, head_count * dim), query_grad, key_grad


def solution(mesh):
    in_specs = (
        P("dp", "ctx", None),
        P("dp", "ctx", None),
        P("dp", "ctx", None),
        P("dp", "ctx", None),
        P(),
        P(),
    )
    out_specs = (P("dp", "ctx", None), P(), P())
    return jax.shard_map(shards, mesh=mesh, in_specs=in_specs, out_specs=out_specs, check_vma=False)
```

```python
import jax
import jax.numpy as jnp
from jax import lax
from jax.experimental import pallas as pl
from jax.experimental.pallas import tpu as pltpu
from jax.sharding import PartitionSpec as P

BF = jnp.bfloat16
F32 = jnp.float32
VMEM_LIMIT = 16 * 1024 * 1024


def mm(a, b):
    return jnp.dot(a, b, preferred_element_type=F32)


def mm_nt(a, b):
    return lax.dot_general(a, b, (((1,), (1,)), ((), ())), preferred_element_type=F32)


def split(x):
    high = x.astype(BF)
    return high, (x - high.astype(F32)).astype(BF)


def soft(scores):
    top = jnp.max(scores, axis=0, keepdims=True)
    raised = jnp.exp(scores - top)
    return raised * (1.0 / jnp.sum(raised, axis=0, keepdims=True))


def both_soft(scores):
    return jnp.concatenate([soft(scores), soft(-scores)], axis=0)


def soft_back(probs, upstream):
    half = probs.shape[0] // 2
    p, n = probs[:half], probs[half:]
    gp, gn = upstream[:half], upstream[half:]
    result = p * (gp - jnp.sum(p * gp, axis=0, keepdims=True))
    result = result - n * (gn - jnp.sum(n * gn, axis=0, keepdims=True))
    return result.astype(BF)


def causal_mask(length):
    rows = lax.broadcasted_iota(jnp.int32, (length, length), 0)
    cols = lax.broadcasted_iota(jnp.int32, (length, length), 1)
    return rows >= cols


def column(row):
    return jnp.broadcast_to(row, (8, row.shape[1])).T[:, :1]


def three_lanes(wide, order):
    lane = lax.broadcasted_iota(jnp.int32, wide.shape, 1)
    high = wide.astype(BF).astype(F32)
    parts = {"h": high, "l": wide - high}
    result = jnp.where(lane == 2, parts[order[2]], 0.0)
    result = jnp.where(lane == 1, parts[order[1]], result)
    return jnp.where(lane == 0, parts[order[0]], result).astype(BF)


def cat(*pieces):
    return jnp.concatenate(pieces, axis=1)


def stack(*pieces):
    return jnp.concatenate(pieces, axis=0)


def put_half(own_ref, other_ref, value):
    half = pl.program_id(1)

    @pl.when(half == 0)
    def _():
        own_ref[...] = value

    @pl.when(half == 1)
    def _():
        other_ref[...] = value


def key_kernel(order, k_ref, v_ref, w_ref, kp_ref, own_ref, other_ref, norm_ref):
    group, width, dim = w_ref.shape
    length = k_ref.shape[0]
    scores = mm_nt(w_ref[...].reshape(group * width, dim), k_ref[...])
    probs = stack(*[both_soft(scores[i * width : (i + 1) * width]) for i in range(group)])
    kp_ref[0, 0] = probs
    features = probs.astype(BF)
    put_half(own_ref, other_ref, mm(features, v_ref[...]))
    norm_ref[0, 0] = mm_nt(jnp.ones((16, length), BF), features)[:1]


def query_kernel(
    order, q_ref, c_ref, w_ref, kp_ref, pn_ref, qp_ref, qr_ref, wt_ref, inv_ref, own_ref, other_ref
):
    group, width, dim = w_ref.shape
    length = q_ref.shape[0]
    causal = causal_mask(length)
    heads = range(group)
    cols = [slice(i * dim, (i + 1) * dim) for i in heads]
    rows = [slice(i * 2 * width, (i + 1) * 2 * width) for i in heads]
    scores = [mm_nt(w_ref[i], q_ref[:, cols[i]]) for i in heads]
    probs = [both_soft(x) for x in scores]
    query_t = [x.astype(BF) for x in probs]
    query_rows = [x.T for x in query_t]
    weights = [mm(query_rows[i], kp_ref[0, 0, rows[i]].astype(BF)) for i in heads]
    weights = [jnp.where(causal, x, 0.0).astype(BF) for x in weights]
    norms = split(jnp.broadcast_to(pn_ref[0, 0], (length, group * 2 * width)))
    ones = jnp.ones((length, length), BF)
    den = [
        mm_nt(
            cat(weights[i], query_rows[i], query_rows[i]),
            cat(ones, norms[0][:, rows[i]], norms[1][:, rows[i]]),
        )
        for i in heads
    ]
    inverse = [1.0 / x for x in den]
    scaled = [(c_ref[:, cols[i]].astype(F32) * inverse[i]).astype(BF) for i in heads]
    sums = [mm(query_t[i], scaled[i]) for i in heads]
    for i in heads:
        qp_ref[0, 0, rows[i]] = probs[i]
        qr_ref[0, 0, i] = query_rows[i]
        wt_ref[0, 0, i] = weights[i]
        inv_ref[0, 0, i] = inverse[i]
    put_half(own_ref, other_ref, stack(*sums))


def middle_kernel(
    order, q_ref, c_ref, v_ref, kp_ref, qp_ref, qr_ref, wt_ref, inv_ref, pn_ref, so_ref, st_ref,
    att_ref, own_ref, other_ref, gk_ref, sn_ref,
):
    group, length = wt_ref.shape[2], wt_ref.shape[3]
    dim = v_ref.shape[1]
    feats = qp_ref.shape[2] // group
    causal = causal_mask(length)
    half = pl.program_id(1)
    heads = range(group)
    cols = [slice(i * dim, (i + 1) * dim) for i in heads]
    rows = [slice(i * feats, (i + 1) * feats) for i in heads]
    values = v_ref[...]
    ones = jnp.ones((2 * dim, dim), BF)
    lane = lax.broadcasted_iota(jnp.int32, (length, dim), 1)
    values_wide = cat(values, jnp.where(lane < 2, 1.0, 0.0).astype(BF))
    states = [split(jnp.where(half == 0, so_ref[r], st_ref[r])) for r in rows]
    norm_cols = column(pn_ref[0, 0])
    norm_cols = [
        three_lanes(jnp.broadcast_to(norm_cols[r], (feats, dim)), "hhl") for r in rows
    ]
    query_rows = [qr_ref[0, 0, i] for i in heads]
    numerator = [
        mm(
            cat(wt_ref[0, 0, i], query_rows[i], query_rows[i]),
            stack(values, states[i][0], states[i][1]),
        )
        for i in heads
    ]
    inverse = [inv_ref[0, 0, i] for i in heads]
    scaled_wide = [c_ref[:, cols[i]].astype(F32) * inverse[i] for i in heads]
    scaled = [x.astype(BF) for x in scaled_wide]
    products = [cat(*split(-(scaled_wide[i] * inverse[i]) * numerator[i])) for i in heads]
    norm_grad = [mm(x, ones) for x in products]
    norm_lanes = [three_lanes(x, "hlh") for x in norm_grad]
    mixed = [mm_nt(cat(scaled[i], norm_lanes[i]), values_wide) for i in heads]
    block = [jnp.where(causal, x, 0.0).astype(BF) for x in mixed]
    upstream = [
        mm_nt(
            cat(kp_ref[0, 0, rows[i]].astype(BF), states[i][0], norm_cols[i], states[i][1]),
            cat(block[i], scaled[i], norm_lanes[i], scaled[i]),
        )
        for i in heads
    ]
    probs = [qp_ref[0, 0, r] for r in rows]
    back = [soft_back(probs[i], upstream[i]) for i in heads]
    grads = [mm(back[i], q_ref[:, cols[i]]) for i in heads]
    for i in heads:
        att_ref[:, cols[i]] = (numerator[i] * inverse[i]).astype(BF)
        sn_ref[0, 0, :, rows[i]] = jnp.sum(
            query_rows[i].astype(F32) * norm_grad[i], axis=0, keepdims=True
        )
        gk_ref[0, 0, rows[i]] = mm(probs[i].astype(BF), block[i])
    put_half(own_ref, other_ref, stack(*grads))


def last_kernel(
    order, k_ref, v_ref, kp_ref, gk_ref, sn_ref, to_ref, tt_ref, own_ref, other_ref
):
    half = pl.program_id(1)
    rows, length = kp_ref.shape[2:]
    feats = k_ref.shape[1]
    high, low = split(jnp.where(half == 0, to_ref[...], tt_ref[...]))
    values = v_ref[...]
    upstream = gk_ref[0, 0] + mm_nt(cat(high, low), cat(values, values))
    upstream = upstream + jnp.broadcast_to(column(sn_ref[0, 0]), (rows, length))
    probs = kp_ref[0, 0]
    back = [
        soft_back(probs[a : a + feats], upstream[a : a + feats]) for a in range(0, rows, feats)
    ]
    put_half(own_ref, other_ref, mm(stack(*back), k_ref[...]))


def out_kernel(order, x_ref, o_ref):
    o_ref[...] = x_ref[...]


def core_swap(x):
    size = lax.axis_size("ctx")
    return lax.ppermute(x, "ctx", [(i, i ^ 1) for i in range(size)])


def chip_move(x, pairs):
    return lax.ppermute(x, "ctx", [(2 * a + c, 2 * b + c) for a, b in pairs for c in (0, 1)])


def chip_before(x, chip, chips, forward):
    turn = (lambda a: a) if forward else (lambda a: chips - 1 - a)
    place = chip if forward else chips - 1 - chip

    def move(y, pairs):
        return chip_move(y, [(turn(a), turn(b)) for a, b in pairs])

    if chips == 4:
        rows = x.shape[0] // 2
        a, b = x[:rows], x[rows:]
        near = move(jnp.where(place == 1, b, a), [(0, 1), (1, 2), (2, 3)])
        far = move(b, [(0, 2)])
        second = jnp.where(place == 1, a + near, jnp.where(place == 2, b + near + far, b))
        near2 = move(second, [(0, 1), (1, 2), (2, 3)])
        far2 = move(second, [(1, 3)])
        first_half = jnp.where(place == 2, near2, near + far2)
        second_half = jnp.where(place == 2, near + far, near2)
        return jnp.concatenate([first_half, second_half], axis=0)
    total = move(x, [(i, i + 1) for i in range(chips - 1)])
    step = 1
    while step < chips:
        total = total + move(total, [(i, i + step) for i in range(chips - step)])
        step *= 2
    return total


def scan_states(own, other, chip, core, chips, forward):
    got = core_swap(other)
    before = chip_before(own + got, chip, chips, forward)
    second = core == 1 if forward else core == 0
    mine = before + jnp.where(second, got, 0.0)
    sent = before + jnp.where(second, 0.0, own)
    return mine, core_swap(sent)


def scan_norms(norm, chip, core, chips, forward):
    got = core_swap(norm)[:, ::-1]
    second = core == 1 if forward else core == 0
    base = jnp.where(second, got, 0.0)
    total = norm + got
    if chips & (chips - 1):
        before = chip_before(total.reshape(-1, total.shape[-1]), chip, chips, forward)
        return base + before.reshape(total.shape)
    bit = 1
    while bit < chips:
        moved = chip_move(total, [(i, i ^ bit) for i in range(chips)])
        upper = (chip & bit) != 0 if forward else (chip & bit) == 0
        base = base + jnp.where(upper, moved, 0.0)
        total = total + moved
        bit *= 2
    return base


def sum_all(own, other, chips):
    mine = own + core_swap(other)
    dp = lax.axis_size("dp")
    parts = mine.shape[0]
    if dp & (dp - 1) or parts % dp or chips & (chips - 1) or parts & (parts - 1):
        mine = lax.psum(mine, "dp")
        total = sum_chips(mine, chips)
        return jnp.concatenate([total, core_swap(total)], axis=0)
    share = parts // dp
    got = [
        lax.ppermute(mine[k * share : (k + 1) * share], "dp", [(i, i ^ k) for i in range(dp)])
        for k in range(1, dp)
    ]
    total = mine[:share]
    for piece in got:
        total = total + piece
    total = sum_chips(total, chips)
    pieces = [total] + [
        lax.ppermute(total, "dp", [(i, i ^ k) for i in range(dp)]) for k in range(1, dp)
    ]
    full = jnp.concatenate(pieces, axis=0)
    return jnp.concatenate([full, core_swap(full)], axis=0)


def sum_chips(total, chips):
    if chips & (chips - 1):
        size = 2 * chips
        return lax.psum(
            total, "ctx", axis_index_groups=[list(range(c, size, 2)) for c in (0, 1)]
        )
    bit = 1
    while bit < chips:
        total = total + chip_move(total, [(i, i ^ bit) for i in range(chips)])
        bit *= 2
    return total


def shards(queries, key_tokens, value_tokens, cotangent, query_map, key_map):
    length = queries.shape[1]
    head_count, dim, width = query_map.shape
    shared = key_tokens.shape[2] // dim
    group = head_count // shared
    feats = 2 * width
    n = shared // 2
    wide = group * feats
    queries = queries.reshape(length, head_count * dim)
    cotangent = cotangent.reshape(length, head_count * dim)
    keys = key_tokens.reshape(length, shared * dim)
    values = value_tokens.reshape(length, shared * dim)
    query_map = jnp.swapaxes(query_map, 1, 2)
    key_map = jnp.swapaxes(key_map, 1, 2)

    ctx = lax.axis_index("ctx")
    chips = lax.axis_size("ctx") // 2
    chip, core = ctx // 2, ctx % 2
    dp = lax.axis_size("dp")
    turn = lax.axis_index("dp") * (n // dp) if n % dp == 0 and n & (n - 1) == 0 else 0
    part = jnp.arange(n, dtype=jnp.int32) ^ turn
    order = jnp.concatenate([part + n * core, part + n * (1 - core)]).astype(jnp.int32)
    heads = jnp.arange(shared, dtype=jnp.int32)
    back = jnp.where(heads // n == core, 0, n) + ((heads % n) ^ turn)
    back = back.astype(jnp.int32)

    def head_cols(rows, cols):
        return pl.BlockSpec((rows, cols), lambda i, s, order: (0, order[s * n + i]))

    map_spec = pl.BlockSpec((group, width, dim), lambda i, s, order: (order[s * n + i], 0, 0))
    kept_spec = pl.BlockSpec((1, 1, wide, length), lambda i, s, order: (i, s, 0, 0))
    kept = jax.ShapeDtypeStruct((n, 2, wide, length), F32)
    row_spec = pl.BlockSpec((1, 1, 1, wide), lambda i, s, order: (i, s, 0, 0))
    row = jax.ShapeDtypeStruct((n, 2, 1, wide), F32)
    weight_spec = pl.BlockSpec((1, 1, group, length, length), lambda i, s, order: (i, s, 0, 0, 0))
    weight = jax.ShapeDtypeStruct((n, 2, group, length, length), BF)
    inverse = jax.ShapeDtypeStruct((n, 2, group, length, dim), F32)

    def half_spec(rows):
        return pl.BlockSpec((rows, dim), lambda i, s, order: (i, 0))

    def call(name, body, in_specs, out_specs, out_shape):
        return pl.pallas_call(
            body,
            name=name,
            out_shape=out_shape,
            grid_spec=pltpu.PrefetchScalarGridSpec(
                num_scalar_prefetch=1, grid=(n, 2), in_specs=in_specs, out_specs=out_specs
            ),
            compiler_params=pltpu.CompilerParams(vmem_limit_bytes=VMEM_LIMIT),
        )

    state = jax.ShapeDtypeStruct((n * wide, dim), F32)
    grad = jax.ShapeDtypeStruct((n * group * width, dim), F32)
    token = head_cols(length, dim)
    wide_token = head_cols(length, group * dim)

    key_probs, own, other, norm = call(
        "key_features",
        key_kernel,
        [token, token, map_spec],
        [kept_spec, half_spec(wide), half_spec(wide), row_spec],
        [kept, state, state, row],
    )(order, keys, values, key_map)
    prefix_norm = scan_norms(norm, chip, core, chips, True)
    prefix_own, prefix_other = scan_states(own, other, chip, core, chips, True)

    query_probs, query_rows, weights, inverse, own, other = call(
        "query_features",
        query_kernel,
        [wide_token, wide_token, map_spec, kept_spec, row_spec],
        [kept_spec, weight_spec, weight_spec, weight_spec, half_spec(wide), half_spec(wide)],
        [kept, weight, weight, inverse, state, state],
    )(order, queries, cotangent, query_map, key_probs, prefix_norm)
    suffix_own, suffix_other = scan_states(own, other, chip, core, chips, False)

    attended, query_own, query_other, key_up, norm = call(
        "attend",
        middle_kernel,
        [wide_token, wide_token, token, kept_spec, kept_spec]
        + [weight_spec] * 3
        + [row_spec]
        + [half_spec(wide)] * 2,
        [wide_token, half_spec(group * width), half_spec(group * width), kept_spec, row_spec],
        [jax.ShapeDtypeStruct((length, head_count * dim), BF), grad, grad, kept, row],
    )(
        order, queries, cotangent, values, key_probs, query_probs, query_rows, weights, inverse,
        prefix_norm, prefix_own, prefix_other,
    )
    suffix_norm = scan_norms(norm, chip, core, chips, False)

    key_own, key_other = call(
        "key_grads",
        last_kernel,
        [token, token, kept_spec, kept_spec, row_spec] + [half_spec(wide)] * 2,
        [half_spec(group * width)] * 2,
        [grad, grad],
    )(order, keys, values, key_probs, key_up, suffix_norm, suffix_own, suffix_other)

    def finish(name, own, other):
        shape = (n, group * width, dim)
        total = sum_all(own.reshape(shape), other.reshape(shape), chips)
        rows = pl.BlockSpec((1, group * width, dim), lambda i, back: (back[i], 0, 0))
        natural = pl.pallas_call(
            out_kernel,
            name=name,
            out_shape=jax.ShapeDtypeStruct((shared, group * width, dim), F32),
            grid_spec=pltpu.PrefetchScalarGridSpec(
                num_scalar_prefetch=1,
                grid=(shared,),
                in_specs=[rows],
                out_specs=pl.BlockSpec((1, group * width, dim), lambda i, back: (i, 0, 0)),
            ),
            compiler_params=pltpu.CompilerParams(vmem_limit_bytes=VMEM_LIMIT),
        )(back, total)
        return jnp.swapaxes(natural.reshape(head_count, width, dim), 1, 2)

    query_grad = finish("query_out", query_own, query_other)
    key_grad = finish("key_out", key_own, key_other)
    return attended.reshape(1, length, head_count * dim), query_grad, key_grad


def solution(mesh):
    in_specs = (
        P("dp", "ctx", None),
        P("dp", "ctx", None),
        P("dp", "ctx", None),
        P("dp", "ctx", None),
        P(),
        P(),
    )
    out_specs = (P("dp", "ctx", None), P(), P())
    return jax.shard_map(shards, mesh=mesh, in_specs=in_specs, out_specs=out_specs, check_vma=False)
```

```python
import jax
import jax.numpy as jnp
from jax import lax
from jax.experimental import pallas as pl
from jax.experimental.pallas import tpu as pltpu
from jax.sharding import PartitionSpec as P

BF = jnp.bfloat16
F32 = jnp.float32
VMEM_LIMIT = 16 * 1024 * 1024


def mm(a, b):
    return jnp.dot(a, b, preferred_element_type=F32)


def mm_nt(a, b):
    return lax.dot_general(a, b, (((1,), (1,)), ((), ())), preferred_element_type=F32)


def split(x):
    high = x.astype(BF)
    return high, (x - high.astype(F32)).astype(BF)


def soft(scores):
    top = jnp.max(scores, axis=0, keepdims=True)
    raised = jnp.exp(scores - top)
    return raised * (1.0 / jnp.sum(raised, axis=0, keepdims=True))


def both_soft(scores):
    return jnp.concatenate([soft(scores), soft(-scores)], axis=0)


def soft_back(probs, upstream):
    half = probs.shape[0] // 2
    p, n = probs[:half], probs[half:]
    gp, gn = upstream[:half], upstream[half:]
    result = p * (gp - jnp.sum(p * gp, axis=0, keepdims=True))
    result = result - n * (gn - jnp.sum(n * gn, axis=0, keepdims=True))
    return result.astype(BF)


def causal_mask(length):
    rows = lax.broadcasted_iota(jnp.int32, (length, length), 0)
    cols = lax.broadcasted_iota(jnp.int32, (length, length), 1)
    return rows >= cols


def column(row):
    return jnp.broadcast_to(row, (8, row.shape[1])).T[:, :1]


def three_lanes(wide, order):
    lane = lax.broadcasted_iota(jnp.int32, wide.shape, 1)
    high = wide.astype(BF).astype(F32)
    parts = {"h": high, "l": wide - high}
    result = jnp.where(lane == 2, parts[order[2]], 0.0)
    result = jnp.where(lane == 1, parts[order[1]], result)
    return jnp.where(lane == 0, parts[order[0]], result).astype(BF)


def cat(*pieces):
    return jnp.concatenate(pieces, axis=1)


def stack(*pieces):
    return jnp.concatenate(pieces, axis=0)


def put_half(own_ref, other_ref, value):
    half = pl.program_id(1)

    @pl.when(half == 0)
    def _():
        own_ref[...] = value

    @pl.when(half == 1)
    def _():
        other_ref[...] = value


def key_kernel(
    order, ko_ref, vo_ref, wo_ref, kt_ref, vt_ref, wt_ref, kp_ref, own_ref, other_ref, norm_ref
):
    group, width, dim = wo_ref.shape
    length = ko_ref.shape[0]
    halves = ((ko_ref, vo_ref, wo_ref, own_ref), (kt_ref, vt_ref, wt_ref, other_ref))
    scores = [mm_nt(w[...].reshape(group * width, dim), k[...]) for k, _, w, _ in halves]
    probs = [
        stack(*[both_soft(x[i * width : (i + 1) * width]) for i in range(group)]) for x in scores
    ]
    features = [x.astype(BF) for x in probs]
    for s, (_, v_ref, _, out_ref) in enumerate(halves):
        kp_ref[0, s] = probs[s]
        out_ref[...] = mm(features[s], v_ref[...])
        norm_ref[0, s] = mm_nt(jnp.ones((16, length), BF), features[s])[:1]


def query_kernel(
    order, q_ref, c_ref, w_ref, kp_ref, pn_ref, qp_ref, qr_ref, wt_ref, inv_ref, own_ref, other_ref
):
    group, width, dim = w_ref.shape
    length = q_ref.shape[0]
    causal = causal_mask(length)
    heads = range(group)
    cols = [slice(i * dim, (i + 1) * dim) for i in heads]
    rows = [slice(i * 2 * width, (i + 1) * 2 * width) for i in heads]
    scores = [mm_nt(w_ref[i], q_ref[:, cols[i]]) for i in heads]
    probs = [both_soft(x) for x in scores]
    query_t = [x.astype(BF) for x in probs]
    query_rows = [x.T for x in query_t]
    weights = [mm(query_rows[i], kp_ref[0, 0, rows[i]].astype(BF)) for i in heads]
    weights = [jnp.where(causal, x, 0.0).astype(BF) for x in weights]
    norms = split(jnp.broadcast_to(pn_ref[0, 0], (length, group * 2 * width)))
    ones = jnp.ones((length, length), BF)
    den = [
        mm_nt(
            cat(weights[i], query_rows[i], query_rows[i]),
            cat(ones, norms[0][:, rows[i]], norms[1][:, rows[i]]),
        )
        for i in heads
    ]
    inverse = [1.0 / x for x in den]
    scaled = [(c_ref[:, cols[i]].astype(F32) * inverse[i]).astype(BF) for i in heads]
    sums = [mm(query_t[i], scaled[i]) for i in heads]
    for i in heads:
        qp_ref[0, 0, rows[i]] = probs[i]
        qr_ref[0, 0, i] = query_rows[i]
        wt_ref[0, 0, i] = weights[i]
        inv_ref[0, 0, i] = inverse[i]
    put_half(own_ref, other_ref, stack(*sums))


def middle_kernel(
    order, q_ref, c_ref, v_ref, kp_ref, qp_ref, qr_ref, wt_ref, inv_ref, pn_ref, so_ref, st_ref,
    att_ref, own_ref, other_ref, gk_ref, sn_ref,
):
    group, length = wt_ref.shape[2], wt_ref.shape[3]
    dim = v_ref.shape[1]
    feats = qp_ref.shape[2] // group
    causal = causal_mask(length)
    half = pl.program_id(1)
    heads = range(group)
    cols = [slice(i * dim, (i + 1) * dim) for i in heads]
    rows = [slice(i * feats, (i + 1) * feats) for i in heads]
    values = v_ref[...]
    ones = jnp.ones((2 * dim, dim), BF)
    lane = lax.broadcasted_iota(jnp.int32, (length, dim), 1)
    values_wide = cat(values, jnp.where(lane < 2, 1.0, 0.0).astype(BF))
    states = [split(jnp.where(half == 0, so_ref[r], st_ref[r])) for r in rows]
    norm_cols = column(pn_ref[0, 0])
    norm_cols = [
        three_lanes(jnp.broadcast_to(norm_cols[r], (feats, dim)), "hhl") for r in rows
    ]
    query_rows = [qr_ref[0, 0, i] for i in heads]
    numerator = [
        mm(
            cat(wt_ref[0, 0, i], query_rows[i], query_rows[i]),
            stack(values, states[i][0], states[i][1]),
        )
        for i in heads
    ]
    inverse = [inv_ref[0, 0, i] for i in heads]
    scaled_wide = [c_ref[:, cols[i]].astype(F32) * inverse[i] for i in heads]
    scaled = [x.astype(BF) for x in scaled_wide]
    products = [cat(*split(-(scaled_wide[i] * inverse[i]) * numerator[i])) for i in heads]
    norm_grad = [mm(x, ones) for x in products]
    norm_lanes = [three_lanes(x, "hlh") for x in norm_grad]
    mixed = [mm_nt(cat(scaled[i], norm_lanes[i]), values_wide) for i in heads]
    block = [jnp.where(causal, x, 0.0).astype(BF) for x in mixed]
    upstream = [
        mm_nt(
            cat(kp_ref[0, 0, rows[i]].astype(BF), states[i][0], norm_cols[i], states[i][1]),
            cat(block[i], scaled[i], norm_lanes[i], scaled[i]),
        )
        for i in heads
    ]
    probs = [qp_ref[0, 0, r] for r in rows]
    back = [soft_back(probs[i], upstream[i]) for i in heads]
    grads = [mm(back[i], q_ref[:, cols[i]]) for i in heads]
    for i in heads:
        att_ref[:, cols[i]] = (numerator[i] * inverse[i]).astype(BF)
        sn_ref[0, 0, :, rows[i]] = jnp.sum(
            query_rows[i].astype(F32) * norm_grad[i], axis=0, keepdims=True
        )
        gk_ref[0, 0, rows[i]] = mm(probs[i].astype(BF), block[i])
    put_half(own_ref, other_ref, stack(*grads))


def last_kernel(
    order, ko_ref, vo_ref, kt_ref, vt_ref, kp_ref, gk_ref, sn_ref, to_ref, tt_ref, own_ref, other_ref
):
    rows, length = kp_ref.shape[2:]
    feats = ko_ref.shape[1]
    halves = ((ko_ref, vo_ref, to_ref, own_ref), (kt_ref, vt_ref, tt_ref, other_ref))
    states = [cat(*split(t[...])) for _, _, t, _ in halves]
    upstream = [
        gk_ref[0, s] + mm_nt(states[s], cat(v[...], v[...]))
        for s, (_, v, _, _) in enumerate(halves)
    ]
    upstream = [
        upstream[s] + jnp.broadcast_to(column(sn_ref[0, s]), (rows, length)) for s in (0, 1)
    ]
    back = [
        stack(*[soft_back(kp_ref[0, s, a : a + feats], upstream[s][a : a + feats]) for a in range(0, rows, feats)])
        for s in (0, 1)
    ]
    for s, (k_ref, _, _, out_ref) in enumerate(halves):
        out_ref[...] = mm(back[s], k_ref[...])


def out_kernel(order, *refs):
    out_ref = refs[-1]
    for i, ref in enumerate(refs[:-1]):
        out_ref[order[i]] = ref[...]


def core_swap(x):
    size = lax.axis_size("ctx")
    return lax.ppermute(x, "ctx", [(i, i ^ 1) for i in range(size)])


def chip_move(x, pairs):
    return lax.ppermute(x, "ctx", [(2 * a + c, 2 * b + c) for a, b in pairs for c in (0, 1)])


def after(values, *earlier):
    return lax.optimization_barrier((values, earlier))[0]


class Scan:
    def __init__(self, own, other, forward):
        ctx = lax.axis_index("ctx")
        self.chips = lax.axis_size("ctx") // 2
        chip, core = ctx // 2, ctx % 2
        self.forward = forward
        self.place = chip if forward else self.chips - 1 - chip
        self.second = core == 1 if forward else core == 0
        self.own = own
        self.got = core_swap(other)
        rows = own.shape[0] // 2
        self.a = own[:rows] + self.got[:rows]
        self.b = own[rows:] + self.got[rows:]
        if self.chips == 4:
            self.payload = (jnp.where(self.place == 1, self.b, self.a), self.b)
        else:
            self.payload = (jnp.concatenate([self.a, self.b], axis=0),)

    def move(self, x, pairs):
        last = self.chips - 1
        turn = (lambda p: p) if self.forward else (lambda p: last - p)
        return chip_move(x, [(turn(p), turn(q)) for p, q in pairs])

    def first(self):
        if self.chips == 4:
            near, far = self.payload
            self.near = self.move(near, [(0, 1), (1, 2), (2, 3)])
            self.far = self.move(far, [(0, 2)])

    def turn_around(self, *earlier):
        if self.chips == 4:
            a, b = after((self.a, self.b), *earlier) if earlier else (self.a, self.b)
            self.payload = (
                jnp.where(
                    self.place == 1,
                    a + self.near,
                    jnp.where(self.place == 2, b + self.near + self.far, b),
                ),
            )

    def second_move(self):
        if self.chips == 4:
            (second,) = self.payload
            self.near2 = self.move(second, [(0, 1), (1, 2), (2, 3)])
            self.far2 = self.move(second, [(1, 3)])

    def finish(self, *earlier):
        own, got = after((self.own, self.got), *earlier) if earlier else (self.own, self.got)
        if self.chips == 4:
            near = after(self.near, *earlier) if earlier else self.near
            first_half = jnp.where(self.place == 2, self.near2, near + self.far2)
            second_half = jnp.where(self.place == 2, near + self.far, self.near2)
            before = jnp.concatenate([first_half, second_half], axis=0)
        else:
            (total,) = self.payload
            before = self.move(total, [(i, i + 1) for i in range(self.chips - 1)])
            step = 1
            while step < self.chips:
                pairs = [(i, i + step) for i in range(self.chips - step)]
                before = before + self.move(before, pairs)
                step *= 2
        mine = before + jnp.where(self.second, got, 0.0)
        sent = before + jnp.where(self.second, 0.0, own)
        return mine, core_swap(sent)


def scan_norms(norm, chip, core, chips, forward, *earlier):
    got = core_swap(norm)[:, ::-1]
    second = core == 1 if forward else core == 0
    base = jnp.where(second, got, 0.0)
    total = norm + got
    if earlier:
        total = after(total, *earlier)
    bit = 1
    while bit < chips:
        moved = chip_move(total, [(i, i ^ bit) for i in range(chips)])
        upper = (chip & bit) != 0 if forward else (chip & bit) == 0
        base = base + jnp.where(upper, moved, 0.0)
        total = total + moved
        bit *= 2
    return base


def sum_all(own, other, chips):
    mine = own + core_swap(other)
    dp = lax.axis_size("dp")
    parts = own.shape[0]
    share = parts // dp
    got = [
        lax.ppermute(mine[k * share : (k + 1) * share], "dp", [(i, i ^ k) for i in range(dp)])
        for k in range(1, dp)
    ]
    total = mine[:share]
    for piece in got:
        total = total + piece
    bit = 1
    while bit < chips:
        total = total + chip_move(total, [(i, i ^ bit) for i in range(chips)])
        bit *= 2
    pieces = [total] + [
        lax.ppermute(total, "dp", [(i, i ^ k) for i in range(dp)]) for k in range(1, dp)
    ]
    pieces = pieces + [core_swap(x) for x in pieces]
    return [x[i] for x in pieces for i in range(share)]


def shards(queries, key_tokens, value_tokens, cotangent, query_map, key_map):
    length = queries.shape[1]
    head_count, dim, width = query_map.shape
    shared = key_tokens.shape[2] // dim
    group = head_count // shared
    feats = 2 * width
    n = shared // 2
    wide = group * feats
    queries = queries.reshape(length, head_count * dim)
    cotangent = cotangent.reshape(length, head_count * dim)
    keys = key_tokens.reshape(length, shared * dim)
    values = value_tokens.reshape(length, shared * dim)
    query_map = jnp.swapaxes(query_map, 1, 2)
    key_map = jnp.swapaxes(key_map, 1, 2)

    ctx = lax.axis_index("ctx")
    chips = lax.axis_size("ctx") // 2
    chip, core = ctx // 2, ctx % 2
    dp = lax.axis_size("dp")
    part = jnp.arange(n, dtype=jnp.int32) ^ (lax.axis_index("dp") * (n // dp))
    order = jnp.concatenate([part + n * core, part + n * (1 - core)]).astype(jnp.int32)

    def head_cols(rows, cols):
        return pl.BlockSpec((rows, cols), lambda i, s, order: (0, order[s * n + i]))

    map_spec = pl.BlockSpec((group, width, dim), lambda i, s, order: (order[s * n + i], 0, 0))
    kept_spec = pl.BlockSpec((1, 1, wide, length), lambda i, s, order: (i, s, 0, 0))
    kept = jax.ShapeDtypeStruct((n, 2, wide, length), F32)
    row_spec = pl.BlockSpec((1, 1, 1, wide), lambda i, s, order: (i, s, 0, 0))
    row = jax.ShapeDtypeStruct((n, 2, 1, wide), F32)
    weight_spec = pl.BlockSpec((1, 1, group, length, length), lambda i, s, order: (i, s, 0, 0, 0))
    weight = jax.ShapeDtypeStruct((n, 2, group, length, length), BF)
    inverse = jax.ShapeDtypeStruct((n, 2, group, length, dim), F32)

    def half_spec(rows):
        return pl.BlockSpec((rows, dim), lambda i, s, order: (i, 0))

    def side(spec, s):
        return pl.BlockSpec(spec.block_shape, lambda i, order: spec.index_map(i, s, order))

    def call(name, body, grid, in_specs, out_specs, out_shape):
        run = pl.pallas_call(
            body,
            name=name,
            out_shape=[pltpu.HBM(x.shape, x.dtype) for x in out_shape],
            grid_spec=pltpu.PrefetchScalarGridSpec(
                num_scalar_prefetch=1, grid=grid, in_specs=in_specs, out_specs=out_specs
            ),
            compiler_params=pltpu.CompilerParams(vmem_limit_bytes=VMEM_LIMIT),
        )
        return lambda order, *arrays: run(
            order, *[pltpu.with_memory_space_constraint(x, pltpu.HBM) for x in arrays]
        )

    state = jax.ShapeDtypeStruct((n * wide, dim), F32)
    grad = jax.ShapeDtypeStruct((n * group * width, dim), F32)
    token = head_cols(length, dim)
    wide_token = head_cols(length, group * dim)
    half_state = pl.BlockSpec((wide, dim), lambda i, order: (i, 0))
    half_grad = pl.BlockSpec((group * width, dim), lambda i, order: (i, 0))
    both_kept = pl.BlockSpec((1, 2, wide, length), lambda i, order: (i, 0, 0, 0))
    both_rows = pl.BlockSpec((1, 2, 1, wide), lambda i, order: (i, 0, 0, 0))
    pair = (n, 2)

    key_probs, own, other, norm = call(
        "key_features",
        key_kernel,
        (n,),
        [side(x, s) for s in (0, 1) for x in (token, token, map_spec)],
        [both_kept, half_state, half_state, both_rows],
        [kept, state, state, row],
    )(order, keys, values, key_map, keys, values, key_map)
    prefix = Scan(own, other, True)
    prefix.first()
    prefix_norm = scan_norms(norm, chip, core, chips, True, *prefix.payload)

    query_probs, query_rows, weights, inverse, own, other = call(
        "query_features",
        query_kernel,
        pair,
        [wide_token, wide_token, map_spec, kept_spec, row_spec],
        [kept_spec, weight_spec, weight_spec, weight_spec, half_spec(wide), half_spec(wide)],
        [kept, weight, weight, inverse, state, state],
    )(order, queries, cotangent, query_map, key_probs, prefix_norm)
    suffix = Scan(own, other, False)
    suffix.first()
    prefix.turn_around(*suffix.payload)
    prefix.second_move()
    suffix.turn_around()
    suffix.second_move()
    prefix_own, prefix_other = after(prefix.finish(), *suffix.payload)

    attended, query_own, query_other, key_up, norm = call(
        "attend",
        middle_kernel,
        pair,
        [wide_token, wide_token, token, kept_spec, kept_spec]
        + [weight_spec] * 3
        + [row_spec]
        + [half_spec(wide)] * 2,
        [wide_token, half_spec(group * width), half_spec(group * width), kept_spec, row_spec],
        [jax.ShapeDtypeStruct((length, head_count * dim), BF), grad, grad, kept, row],
    )(
        order, queries, cotangent, values, key_probs, query_probs, query_rows, weights, inverse,
        prefix_norm, prefix_own, prefix_other,
    )
    suffix_norm = scan_norms(norm, chip, core, chips, False)
    suffix_own, suffix_other = suffix.finish(suffix_norm)

    key_own, key_other = call(
        "key_grads",
        last_kernel,
        (n,),
        [side(token, 0)] * 2 + [side(token, 1)] * 2 + [both_kept] * 2 + [both_rows] + [half_state] * 2,
        [half_grad] * 2,
        [grad, grad],
    )(order, keys, values, keys, values, key_probs, key_up, suffix_norm, suffix_own, suffix_other)

    def finish(name, own, other):
        shape = (n, group * width, dim)
        pieces = sum_all(own.reshape(shape), other.reshape(shape), chips)
        whole = pl.BlockSpec(memory_space=pltpu.VMEM)
        natural = pl.pallas_call(
            out_kernel,
            name=name,
            out_shape=jax.ShapeDtypeStruct((shared, group * width, dim), F32),
            in_specs=[pl.BlockSpec(memory_space=pltpu.SMEM)] + [whole] * shared,
            out_specs=whole,
            compiler_params=pltpu.CompilerParams(vmem_limit_bytes=VMEM_LIMIT),
        )(order, *pieces)
        return jnp.swapaxes(natural.reshape(head_count, width, dim), 1, 2)

    query_grad = finish("query_out", query_own, query_other)
    key_grad = finish("key_out", key_own, key_other)
    return attended.reshape(1, length, head_count * dim), query_grad, key_grad


def solution(mesh):
    in_specs = (
        P("dp", "ctx", None),
        P("dp", "ctx", None),
        P("dp", "ctx", None),
        P("dp", "ctx", None),
        P(),
        P(),
    )
    out_specs = (P("dp", "ctx", None), P(), P())
    return jax.shard_map(shards, mesh=mesh, in_specs=in_specs, out_specs=out_specs, check_vma=False)
```

```python
import jax
import jax.numpy as jnp
from jax import lax
from jax.experimental import pallas as pl
from jax.experimental.pallas import tpu as pltpu
from jax.sharding import PartitionSpec as P

BF = jnp.bfloat16
F32 = jnp.float32
VMEM_LIMIT = 16 * 1024 * 1024


def mm(a, b):
    return jnp.dot(a, b, preferred_element_type=F32)


def mm_nt(a, b):
    return lax.dot_general(a, b, (((1,), (1,)), ((), ())), preferred_element_type=F32)


def split(x):
    high = x.astype(BF)
    return high, (x - high.astype(F32)).astype(BF)


def soft(scores):
    top = jnp.max(scores, axis=0, keepdims=True)
    raised = jnp.exp(scores - top)
    return raised * (1.0 / jnp.sum(raised, axis=0, keepdims=True))


def both_soft(scores):
    return jnp.concatenate([soft(scores), soft(-scores)], axis=0)


def soft_back(probs, upstream):
    half = probs.shape[0] // 2
    p, n = probs[:half], probs[half:]
    gp, gn = upstream[:half], upstream[half:]
    result = p * (gp - jnp.sum(p * gp, axis=0, keepdims=True))
    result = result - n * (gn - jnp.sum(n * gn, axis=0, keepdims=True))
    return result.astype(BF)


def causal_mask(length):
    rows = lax.broadcasted_iota(jnp.int32, (length, length), 0)
    cols = lax.broadcasted_iota(jnp.int32, (length, length), 1)
    return rows >= cols


def column(row):
    return jnp.broadcast_to(row, (8, row.shape[1])).T[:, :1]


def three_lanes(wide, order):
    lane = lax.broadcasted_iota(jnp.int32, wide.shape, 1)
    high = wide.astype(BF).astype(F32)
    parts = {"h": high, "l": wide - high}
    result = jnp.where(lane == 2, parts[order[2]], 0.0)
    result = jnp.where(lane == 1, parts[order[1]], result)
    return jnp.where(lane == 0, parts[order[0]], result).astype(BF)


def cat(*pieces):
    return jnp.concatenate(pieces, axis=1)


def stack(*pieces):
    return jnp.concatenate(pieces, axis=0)


def put_half(own_ref, other_ref, value):
    half = pl.program_id(1)

    @pl.when(half == 0)
    def _():
        own_ref[...] = value

    @pl.when(half == 1)
    def _():
        other_ref[...] = value


def key_kernel(
    order, ko_ref, vo_ref, wo_ref, kt_ref, vt_ref, wt_ref, kp_ref, own_ref, other_ref, norm_ref
):
    group, width, dim = wo_ref.shape
    length = ko_ref.shape[0]
    halves = ((ko_ref, vo_ref, wo_ref, own_ref), (kt_ref, vt_ref, wt_ref, other_ref))
    scores = [mm_nt(w[...].reshape(group * width, dim), k[...]) for k, _, w, _ in halves]
    probs = [
        stack(*[both_soft(x[i * width : (i + 1) * width]) for i in range(group)]) for x in scores
    ]
    features = [x.astype(BF) for x in probs]
    for s, (_, v_ref, _, out_ref) in enumerate(halves):
        kp_ref[0, s] = probs[s]
        out_ref[...] = mm(features[s], v_ref[...])
        norm_ref[0, s] = mm_nt(jnp.ones((16, length), BF), features[s])[:1]


def query_kernel(
    order, q_ref, c_ref, w_ref, kp_ref, pn_ref, qp_ref, qr_ref, wt_ref, inv_ref, own_ref, other_ref
):
    group, width, dim = w_ref.shape
    length = q_ref.shape[0]
    causal = causal_mask(length)
    heads = range(group)
    cols = [slice(i * dim, (i + 1) * dim) for i in heads]
    rows = [slice(i * 2 * width, (i + 1) * 2 * width) for i in heads]
    scores = [mm_nt(w_ref[i], q_ref[:, cols[i]]) for i in heads]
    probs = [both_soft(x) for x in scores]
    query_t = [x.astype(BF) for x in probs]
    query_rows = [x.T for x in query_t]
    weights = [mm(query_rows[i], kp_ref[0, 0, rows[i]].astype(BF)) for i in heads]
    weights = [jnp.where(causal, x, 0.0).astype(BF) for x in weights]
    norms = split(jnp.broadcast_to(pn_ref[0, 0], (length, group * 2 * width)))
    ones = jnp.ones((length, length), BF)
    den = [
        mm_nt(
            cat(weights[i], query_rows[i], query_rows[i]),
            cat(ones, norms[0][:, rows[i]], norms[1][:, rows[i]]),
        )
        for i in heads
    ]
    inverse = [1.0 / x for x in den]
    scaled = [(c_ref[:, cols[i]].astype(F32) * inverse[i]).astype(BF) for i in heads]
    sums = [mm(query_t[i], scaled[i]) for i in heads]
    for i in heads:
        qp_ref[0, 0, rows[i]] = probs[i]
        qr_ref[0, 0, i] = query_rows[i]
        wt_ref[0, 0, i] = weights[i]
        inv_ref[0, 0, i] = inverse[i]
    put_half(own_ref, other_ref, stack(*sums))


def middle_kernel(
    order, q_ref, c_ref, v_ref, kp_ref, qp_ref, qr_ref, wt_ref, inv_ref, pn_ref, so_ref, st_ref,
    att_ref, own_ref, other_ref, gk_ref, sn_ref,
):
    group, length = wt_ref.shape[2], wt_ref.shape[3]
    dim = v_ref.shape[1]
    feats = qp_ref.shape[2] // group
    causal = causal_mask(length)
    half = pl.program_id(1)
    heads = range(group)
    cols = [slice(i * dim, (i + 1) * dim) for i in heads]
    rows = [slice(i * feats, (i + 1) * feats) for i in heads]
    values = v_ref[...]
    ones = jnp.ones((2 * dim, dim), BF)
    lane = lax.broadcasted_iota(jnp.int32, (length, dim), 1)
    values_wide = cat(values, jnp.where(lane < 2, 1.0, 0.0).astype(BF))
    states = [split(jnp.where(half == 0, so_ref[r], st_ref[r])) for r in rows]
    norm_cols = column(pn_ref[0, 0])
    norm_cols = [
        three_lanes(jnp.broadcast_to(norm_cols[r], (feats, dim)), "hhl") for r in rows
    ]
    query_rows = [qr_ref[0, 0, i] for i in heads]
    numerator = [
        mm(
            cat(wt_ref[0, 0, i], query_rows[i], query_rows[i]),
            stack(values, states[i][0], states[i][1]),
        )
        for i in heads
    ]
    inverse = [inv_ref[0, 0, i] for i in heads]
    scaled_wide = [c_ref[:, cols[i]].astype(F32) * inverse[i] for i in heads]
    scaled = [x.astype(BF) for x in scaled_wide]
    products = [cat(*split(-(scaled_wide[i] * inverse[i]) * numerator[i])) for i in heads]
    norm_grad = [mm(x, ones) for x in products]
    norm_lanes = [three_lanes(x, "hlh") for x in norm_grad]
    mixed = [mm_nt(cat(scaled[i], norm_lanes[i]), values_wide) for i in heads]
    block = [jnp.where(causal, x, 0.0).astype(BF) for x in mixed]
    upstream = [
        mm_nt(
            cat(kp_ref[0, 0, rows[i]].astype(BF), states[i][0], norm_cols[i], states[i][1]),
            cat(block[i], scaled[i], norm_lanes[i], scaled[i]),
        )
        for i in heads
    ]
    probs = [qp_ref[0, 0, r] for r in rows]
    back = [soft_back(probs[i], upstream[i]) for i in heads]
    grads = [mm(back[i], q_ref[:, cols[i]]) for i in heads]
    for i in heads:
        att_ref[:, cols[i]] = (numerator[i] * inverse[i]).astype(BF)
        sn_ref[0, 0, :, rows[i]] = jnp.sum(
            query_rows[i].astype(F32) * norm_grad[i], axis=0, keepdims=True
        )
        gk_ref[0, 0, rows[i]] = mm(probs[i].astype(BF), block[i])
    put_half(own_ref, other_ref, stack(*grads))


def last_kernel(
    order, ko_ref, vo_ref, kt_ref, vt_ref, kp_ref, gk_ref, sn_ref, to_ref, tt_ref, own_ref, other_ref
):
    rows, length = kp_ref.shape[2:]
    feats = ko_ref.shape[1]
    halves = ((ko_ref, vo_ref, to_ref, own_ref), (kt_ref, vt_ref, tt_ref, other_ref))
    states = [cat(*split(t[...])) for _, _, t, _ in halves]
    upstream = [
        gk_ref[0, s] + mm_nt(states[s], cat(v[...], v[...]))
        for s, (_, v, _, _) in enumerate(halves)
    ]
    upstream = [
        upstream[s] + jnp.broadcast_to(column(sn_ref[0, s]), (rows, length)) for s in (0, 1)
    ]
    back = [
        stack(*[soft_back(kp_ref[0, s, a : a + feats], upstream[s][a : a + feats]) for a in range(0, rows, feats)])
        for s in (0, 1)
    ]
    for s, (k_ref, _, _, out_ref) in enumerate(halves):
        out_ref[...] = mm(back[s], k_ref[...])


def out_kernel(order, *refs):
    out_ref = refs[-1]
    for i, ref in enumerate(refs[:-1]):
        out_ref[order[i]] = ref[...]


def core_swap(x):
    size = lax.axis_size("ctx")
    return lax.ppermute(x, "ctx", [(i, i ^ 1) for i in range(size)])


def chip_move(x, pairs):
    return lax.ppermute(x, "ctx", [(2 * a + c, 2 * b + c) for a, b in pairs for c in (0, 1)])


def after(values, *earlier):
    return lax.optimization_barrier((values, earlier))[0]


class Scan:
    def __init__(self, own, other, forward):
        ctx = lax.axis_index("ctx")
        self.chips = lax.axis_size("ctx") // 2
        chip, core = ctx // 2, ctx % 2
        self.forward = forward
        self.place = chip if forward else self.chips - 1 - chip
        self.second = core == 1 if forward else core == 0
        self.own = own
        self.got = core_swap(other)
        rows = own.shape[0] // 2
        self.a = own[:rows] + self.got[:rows]
        self.b = own[rows:] + self.got[rows:]
        if self.chips == 4:
            self.payload = (jnp.where(self.place == 1, self.b, self.a), self.b)
        else:
            self.payload = (jnp.concatenate([self.a, self.b], axis=0),)

    def move(self, x, pairs):
        last = self.chips - 1
        turn = (lambda p: p) if self.forward else (lambda p: last - p)
        return chip_move(x, [(turn(p), turn(q)) for p, q in pairs])

    def first(self):
        if self.chips == 4:
            near, far = self.payload
            self.near = self.move(near, [(0, 1), (1, 2), (2, 3)])
            self.far = self.move(far, [(0, 2)])

    def turn_around(self, *earlier):
        if self.chips == 4:
            a, b = after((self.a, self.b), *earlier) if earlier else (self.a, self.b)
            self.payload = (
                jnp.where(
                    self.place == 1,
                    a + self.near,
                    jnp.where(self.place == 2, b + self.near + self.far, b),
                ),
            )

    def second_move(self):
        if self.chips == 4:
            (second,) = self.payload
            self.near2 = self.move(second, [(0, 1), (1, 2), (2, 3)])
            self.far2 = self.move(second, [(1, 3)])

    def finish(self, *earlier):
        own, got = after((self.own, self.got), *earlier) if earlier else (self.own, self.got)
        if self.chips == 4:
            near = after(self.near, *earlier) if earlier else self.near
            first_half = jnp.where(self.place == 2, self.near2, near + self.far2)
            second_half = jnp.where(self.place == 2, near + self.far, self.near2)
            before = jnp.concatenate([first_half, second_half], axis=0)
        else:
            (total,) = self.payload
            before = self.move(total, [(i, i + 1) for i in range(self.chips - 1)])
            step = 1
            while step < self.chips:
                pairs = [(i, i + step) for i in range(self.chips - step)]
                before = before + self.move(before, pairs)
                step *= 2
        mine = before + jnp.where(self.second, got, 0.0)
        sent = before + jnp.where(self.second, 0.0, own)
        return mine, core_swap(sent)


def scan_norms(norm, chip, core, chips, forward, *earlier):
    got = core_swap(norm)[:, ::-1]
    second = core == 1 if forward else core == 0
    base = jnp.where(second, got, 0.0)
    total = norm + got
    if earlier:
        total = after(total, *earlier)
    bit = 1
    while bit < chips:
        moved = chip_move(total, [(i, i ^ bit) for i in range(chips)])
        upper = (chip & bit) != 0 if forward else (chip & bit) == 0
        base = base + jnp.where(upper, moved, 0.0)
        total = total + moved
        bit *= 2
    return base


def sum_all(mine, chips):
    dp = lax.axis_size("dp")
    parts = mine.shape[0]
    share = parts // dp
    got = [
        lax.ppermute(mine[k * share : (k + 1) * share], "dp", [(i, i ^ k) for i in range(dp)])
        for k in range(1, dp)
    ]
    total = mine[:share]
    for piece in got:
        total = total + piece
    bit = 1
    while bit < chips:
        total = total + chip_move(total, [(i, i ^ bit) for i in range(chips)])
        bit *= 2
    pieces = [total] + [
        lax.ppermute(total, "dp", [(i, i ^ k) for i in range(dp)]) for k in range(1, dp)
    ]
    pieces = pieces + [core_swap(x) for x in pieces]
    return [x[i] for x in pieces for i in range(share)]


def shards(queries, key_tokens, value_tokens, cotangent, query_map, key_map):
    length = queries.shape[1]
    head_count, dim, width = query_map.shape
    shared = key_tokens.shape[2] // dim
    group = head_count // shared
    feats = 2 * width
    n = shared // 2
    wide = group * feats
    queries = queries.reshape(length, head_count * dim)
    cotangent = cotangent.reshape(length, head_count * dim)
    keys = key_tokens.reshape(length, shared * dim)
    values = value_tokens.reshape(length, shared * dim)
    query_map = jnp.swapaxes(query_map, 1, 2)
    key_map = jnp.swapaxes(key_map, 1, 2)

    ctx = lax.axis_index("ctx")
    chips = lax.axis_size("ctx") // 2
    chip, core = ctx // 2, ctx % 2
    dp = lax.axis_size("dp")
    part = jnp.arange(n, dtype=jnp.int32) ^ (lax.axis_index("dp") * (n // dp))
    order = jnp.concatenate([part + n * core, part + n * (1 - core)]).astype(jnp.int32)

    def head_cols(rows, cols):
        return pl.BlockSpec((rows, cols), lambda i, s, order: (0, order[s * n + i]))

    map_spec = pl.BlockSpec((group, width, dim), lambda i, s, order: (order[s * n + i], 0, 0))
    kept_spec = pl.BlockSpec((1, 1, wide, length), lambda i, s, order: (i, s, 0, 0))
    kept = jax.ShapeDtypeStruct((n, 2, wide, length), F32)
    row_spec = pl.BlockSpec((1, 1, 1, wide), lambda i, s, order: (i, s, 0, 0))
    row = jax.ShapeDtypeStruct((n, 2, 1, wide), F32)
    weight_spec = pl.BlockSpec((1, 1, group, length, length), lambda i, s, order: (i, s, 0, 0, 0))
    weight = jax.ShapeDtypeStruct((n, 2, group, length, length), BF)
    inverse = jax.ShapeDtypeStruct((n, 2, group, length, dim), F32)

    def half_spec(rows):
        return pl.BlockSpec((rows, dim), lambda i, s, order: (i, 0))

    def side(spec, s):
        return pl.BlockSpec(spec.block_shape, lambda i, order: spec.index_map(i, s, order))

    def call(name, body, grid, in_specs, out_specs, out_shape):
        run = pl.pallas_call(
            body,
            name=name,
            out_shape=[pltpu.HBM(x.shape, x.dtype) for x in out_shape],
            grid_spec=pltpu.PrefetchScalarGridSpec(
                num_scalar_prefetch=1, grid=grid, in_specs=in_specs, out_specs=out_specs
            ),
            compiler_params=pltpu.CompilerParams(vmem_limit_bytes=VMEM_LIMIT),
        )
        return lambda order, *arrays: run(
            order, *[pltpu.with_memory_space_constraint(x, pltpu.HBM) for x in arrays]
        )

    state = jax.ShapeDtypeStruct((n * wide, dim), F32)
    grad = jax.ShapeDtypeStruct((n * group * width, dim), F32)
    token = head_cols(length, dim)
    wide_token = head_cols(length, group * dim)
    half_state = pl.BlockSpec((wide, dim), lambda i, order: (i, 0))
    half_grad = pl.BlockSpec((group * width, dim), lambda i, order: (i, 0))
    both_kept = pl.BlockSpec((1, 2, wide, length), lambda i, order: (i, 0, 0, 0))
    both_rows = pl.BlockSpec((1, 2, 1, wide), lambda i, order: (i, 0, 0, 0))
    pair = (n, 2)

    key_probs, own, other, norm = call(
        "key_features",
        key_kernel,
        (n,),
        [side(x, s) for s in (0, 1) for x in (token, token, map_spec)],
        [both_kept, half_state, half_state, both_rows],
        [kept, state, state, row],
    )(order, keys, values, key_map, keys, values, key_map)
    prefix = Scan(own, other, True)
    prefix.first()
    prefix_norm = scan_norms(norm, chip, core, chips, True, *prefix.payload)
    query_probs, query_rows, weights, inverse, own, other = call(
        "query_features",
        query_kernel,
        pair,
        [wide_token, wide_token, map_spec, kept_spec, row_spec],
        [kept_spec, weight_spec, weight_spec, weight_spec, half_spec(wide), half_spec(wide)],
        [kept, weight, weight, inverse, state, state],
    )(order, queries, cotangent, query_map, key_probs, prefix_norm)
    prefix.turn_around(own)
    prefix.second_move()
    suffix = Scan(*after((own, other), prefix.payload), False)
    suffix.first()
    suffix.turn_around()
    suffix.second_move()
    prefix_own, prefix_other = prefix.finish(*suffix.payload)

    attended, query_own, query_other, key_up, norm = call(
        "attend",
        middle_kernel,
        pair,
        [wide_token, wide_token, token, kept_spec, kept_spec]
        + [weight_spec] * 3
        + [row_spec]
        + [half_spec(wide)] * 2,
        [wide_token, half_spec(group * width), half_spec(group * width), kept_spec, row_spec],
        [jax.ShapeDtypeStruct((length, head_count * dim), BF), grad, grad, kept, row],
    )(
        order, queries, cotangent, values, key_probs, query_probs, query_rows, weights, inverse,
        prefix_norm, prefix_own, prefix_other,
    )
    suffix_norm = scan_norms(norm, chip, core, chips, False)
    query_mine = query_own + core_swap(query_other)
    suffix_own, suffix_other = suffix.finish(suffix_norm)

    key_own, key_other = call(
        "key_grads",
        last_kernel,
        (n,),
        [side(token, 0)] * 2 + [side(token, 1)] * 2 + [both_kept] * 2 + [both_rows] + [half_state] * 2,
        [half_grad] * 2,
        [grad, grad],
    )(order, keys, values, keys, values, key_probs, key_up, suffix_norm, suffix_own, suffix_other)

    def finish(name, mine):
        pieces = sum_all(mine.reshape(n, group * width, dim), chips)
        whole = pl.BlockSpec(memory_space=pltpu.VMEM)
        natural = pl.pallas_call(
            out_kernel,
            name=name,
            out_shape=jax.ShapeDtypeStruct((shared, group * width, dim), F32),
            in_specs=[pl.BlockSpec(memory_space=pltpu.SMEM)] + [whole] * shared,
            out_specs=whole,
            compiler_params=pltpu.CompilerParams(vmem_limit_bytes=VMEM_LIMIT),
        )(order, *pieces)
        return jnp.swapaxes(natural.reshape(head_count, width, dim), 1, 2)

    query_grad = finish("query_out", query_mine)
    key_grad = finish("key_out", key_own + core_swap(key_other))
    return attended.reshape(1, length, head_count * dim), query_grad, key_grad


def solution(mesh):
    in_specs = (
        P("dp", "ctx", None),
        P("dp", "ctx", None),
        P("dp", "ctx", None),
        P("dp", "ctx", None),
        P(),
        P(),
    )
    out_specs = (P("dp", "ctx", None), P(), P())
    return jax.shard_map(shards, mesh=mesh, in_specs=in_specs, out_specs=out_specs, check_vma=False)
```

```python
import jax
import jax.numpy as jnp
from jax import lax
from jax.experimental import pallas as pl
from jax.experimental.pallas import tpu as pltpu
from jax.sharding import PartitionSpec as P

BF = jnp.bfloat16
F32 = jnp.float32
VMEM_LIMIT = 32 * 1024 * 1024


def mm(a, b):
    return jnp.dot(a, b, preferred_element_type=F32)


def mm_nt(a, b):
    return lax.dot_general(a, b, (((1,), (1,)), ((), ())), preferred_element_type=F32)


def split(x):
    high = x.astype(BF)
    return high, (x - high.astype(F32)).astype(BF)


def cat(*pieces):
    return jnp.concatenate(pieces, axis=1)


def stack(*pieces):
    return jnp.concatenate(pieces, axis=0)


def soft(scores):
    top = jnp.max(scores, axis=0, keepdims=True)
    raised = jnp.exp(scores - top)
    return raised * (1.0 / jnp.sum(raised, axis=0, keepdims=True))


def both_soft(scores):
    return stack(soft(scores), soft(-scores))


def soft_back(probs, upstream):
    half = probs.shape[0] // 2
    p, n = probs[:half], probs[half:]
    gp, gn = upstream[:half], upstream[half:]
    result = p * (gp - jnp.sum(p * gp, axis=0, keepdims=True))
    result = result - n * (gn - jnp.sum(n * gn, axis=0, keepdims=True))
    return result.astype(BF)


def causal_mask(core, tokens):
    own = tokens // 2
    shift = core * own
    rows = lax.broadcasted_iota(jnp.int32, (tokens, tokens), 0)
    cols = lax.broadcasted_iota(jnp.int32, (tokens, tokens), 1)
    rows = rows + jnp.where(rows < own, shift, -shift)
    cols = cols + jnp.where(cols < own, shift, -shift)
    return rows >= cols


def column(row):
    return jnp.broadcast_to(row, (8, row.shape[1])).T[:, :1]


def three_lanes(wide, order):
    lane = lax.broadcasted_iota(jnp.int32, wide.shape, 1)
    high = wide.astype(BF).astype(F32)
    parts = {"h": high, "l": wide - high}
    result = jnp.where(lane == 2, parts[order[2]], 0.0)
    result = jnp.where(lane == 1, parts[order[1]], result)
    return jnp.where(lane == 0, parts[order[0]], result).astype(BF)


def tokens_of(own_ref, got_ref):
    return stack(own_ref[...], got_ref[...].astype(BF))


def put_parts(place, half, n, value, a_ref, b_ref, near_ref):
    i = pl.program_id(0)

    @pl.when(i < half)
    def _():
        a_ref[...] = value

    @pl.when(i >= half)
    def _():
        b_ref[...] = value

    @pl.when((i >= half) == (place == 1))
    def _():
        near_ref[...] = value


def before_of(place, half, near, far, near2, far2):
    first = jnp.where(place == 2, near2[...], near[...] + far2[...])
    second = jnp.where(place == 2, near[...] + far[...], near2[...])
    return jnp.where(pl.program_id(0) < half, first, second)


def pack_kernel(info, *refs):
    half = len(refs) // 2
    for x_ref, o_ref in zip(refs[:half], refs[half:]):
        o_ref[...] = x_ref[...].astype(F32)


def key_kernel(
    n, info, k_ref, kg_ref, v_ref, vg_ref, w_ref, kp_ref, kb_ref, norm_ref, a_ref, b_ref, near_ref
):
    group, width, dim = w_ref.shape
    keys = tokens_of(k_ref, kg_ref)
    values = tokens_of(v_ref, vg_ref)
    scores = mm_nt(w_ref[...].reshape(group * width, dim), keys)
    probs = stack(*[both_soft(scores[i * width : (i + 1) * width]) for i in range(group)])
    features = probs.astype(BF)
    kp_ref[0] = probs
    kb_ref[0] = features
    norm_ref[0] = mm_nt(jnp.ones((16, keys.shape[0]), BF), features)[:1]
    put_parts(info[2 * n + 1], n // 2, n, mm(features, values), a_ref, b_ref, near_ref)


def query_kernel(
    n, info, q_ref, qg_ref, c_ref, cg_ref, w_ref, kb_ref, pn_ref,
    qp_ref, qr_ref, wt_ref, a_ref, b_ref, near_ref,
):
    group, width, dim = w_ref.shape
    feats = 2 * width
    queries = tokens_of(q_ref, qg_ref)
    upstream = stack(c_ref[...].astype(F32), cg_ref[...])
    length = queries.shape[0]
    causal = causal_mask(info[2 * n], length)
    heads = range(group)
    cols = [slice(i * dim, (i + 1) * dim) for i in heads]
    rows = [slice(i * feats, (i + 1) * feats) for i in heads]
    scores = [mm_nt(w_ref[i], queries[:, cols[i]]) for i in heads]
    probs = [both_soft(x) for x in scores]
    query_t = [x.astype(BF) for x in probs]
    query_rows = [x.T for x in query_t]
    weights = [mm(query_rows[i], kb_ref[0, rows[i]]) for i in heads]
    weights = [jnp.where(causal, x, 0.0).astype(BF) for x in weights]
    norms = split(jnp.broadcast_to(pn_ref[0], (dim, group * feats)))
    ones = jnp.ones((dim, length), BF)
    den = [
        mm_nt(
            cat(weights[i], query_rows[i], query_rows[i]),
            cat(ones, norms[0][:, rows[i]], norms[1][:, rows[i]]),
        )
        for i in heads
    ]
    scaled = [(upstream[:, cols[i]] * (1.0 / den[i])).astype(BF) for i in heads]
    sums = [mm(query_t[i], scaled[i]) for i in heads]
    for i in heads:
        qp_ref[0, rows[i]] = probs[i]
        qr_ref[0, i] = query_rows[i]
        wt_ref[0, i] = weights[i]
    put_parts(info[2 * n + 2], n // 2, n, stack(*sums), a_ref, b_ref, near_ref)


def attend_kernel(
    n, info, c_ref, cg_ref, v_ref, vg_ref, qr_ref, wt_ref, pn_ref, near, far, near2, far2,
    att_ref, atg_ref, sc_ref, nl_ref, sn_ref,
):
    group, length, dim = qr_ref.shape[1:]
    feats = dim
    own = length // 2
    heads = range(group)
    cols = [slice(i * dim, (i + 1) * dim) for i in heads]
    rows = [slice(i * feats, (i + 1) * feats) for i in heads]
    upstream = stack(c_ref[...].astype(F32), cg_ref[...])
    values = tokens_of(v_ref, vg_ref)
    high, low = split(before_of(info[2 * n + 1], n // 2, near, far, near2, far2))
    norm_high, norm_low = split(jnp.broadcast_to(column(pn_ref[0]), (group * feats, dim)))
    high, low = cat(high, norm_high), cat(low, norm_low)
    values = cat(values, jnp.ones((length, dim), BF))
    query_rows = [qr_ref[0, i] for i in heads]
    both = [
        mm(cat(wt_ref[0, i], query_rows[i], query_rows[i]), stack(values, high[rows[i]], low[rows[i]]))
        for i in heads
    ]
    numerator = [x[:, :dim] for x in both]
    inverse = [1.0 / x[:, dim:] for x in both]
    scaled = [upstream[:, cols[i]] * inverse[i] for i in heads]
    products = [cat(*split(-(scaled[i] * inverse[i]) * numerator[i])) for i in heads]
    ones = jnp.ones((2 * dim, dim), BF)
    norm_grad = [mm(x, ones) for x in products]
    for i in heads:
        result = numerator[i] * inverse[i]
        att_ref[:, cols[i]] = result[:own].astype(BF)
        atg_ref[:, cols[i]] = result[own:]
        sc_ref[0, i] = scaled[i].astype(BF)
        nl_ref[0, i] = three_lanes(norm_grad[i], "hlh")
        sn_ref[0, :, rows[i]] = jnp.sum(
            query_rows[i].astype(F32) * norm_grad[i], axis=0, keepdims=True
        )


def query_grad_kernel(
    n, info, q_ref, qg_ref, v_ref, vg_ref, kb_ref, qp_ref, sc_ref, nl_ref, pn_ref,
    near, far, near2, far2, gq_ref, gk_ref,
):
    group, length, dim = sc_ref.shape[1:]
    feats = dim
    width = feats // 2
    heads = range(group)
    cols = [slice(i * dim, (i + 1) * dim) for i in heads]
    rows = [slice(i * feats, (i + 1) * feats) for i in heads]
    causal = causal_mask(info[2 * n], length)
    queries = tokens_of(q_ref, qg_ref)
    lane = lax.broadcasted_iota(jnp.int32, (length, dim), 1)
    values = cat(tokens_of(v_ref, vg_ref), jnp.where(lane < 2, 1.0, 0.0).astype(BF))
    high, low = split(before_of(info[2 * n + 1], n // 2, near, far, near2, far2))
    norm_cols = three_lanes(jnp.broadcast_to(column(pn_ref[0]), (group * feats, dim)), "hhl")
    scaled = [sc_ref[0, i] for i in heads]
    lanes = [nl_ref[0, i] for i in heads]
    mixed = [mm_nt(cat(scaled[i], lanes[i]), values) for i in heads]
    block = [jnp.where(causal, x, 0.0).astype(BF) for x in mixed]
    upstream = [
        mm_nt(
            cat(kb_ref[0, rows[i]], high[rows[i]], norm_cols[rows[i]], low[rows[i]]),
            cat(block[i], scaled[i], lanes[i], scaled[i]),
        )
        for i in heads
    ]
    probs = [qp_ref[0, r] for r in rows]
    back = [soft_back(probs[i], upstream[i]) for i in heads]
    for i in heads:
        gq_ref[0, i * width : (i + 1) * width] = mm(back[i], queries[:, cols[i]])
        gk_ref[0, rows[i]] = mm(probs[i].astype(BF), block[i])


def key_grad_kernel(
    n, info, k_ref, kg_ref, v_ref, vg_ref, kp_ref, gk_ref, sn_ref, near, far, near2, far2, out_ref
):
    rows, length = kp_ref.shape[1:]
    feats = k_ref.shape[1]
    values = tokens_of(v_ref, vg_ref)
    state = cat(*split(before_of(info[2 * n + 2], n // 2, near, far, near2, far2)))
    upstream = gk_ref[0] + mm_nt(state, cat(values, values))
    upstream = upstream + jnp.broadcast_to(column(sn_ref[0]), (rows, length))
    back = [
        soft_back(kp_ref[0, a : a + feats], upstream[a : a + feats])
        for a in range(0, rows, feats)
    ]
    out_ref[0] = mm(stack(*back), tokens_of(k_ref, kg_ref))


def attended_kernel(info, x_ref, kept_ref, o_ref):
    o_ref[...] = x_ref[...].astype(BF)


def out_kernel(info, *refs):
    out_ref = refs[-1]
    for i, ref in enumerate(refs[:-1]):
        out_ref[info[i]] = ref[...]


def core_swap(x):
    size = lax.axis_size("ctx")
    return lax.ppermute(x, "ctx", [(i, i ^ 1) for i in range(size)])


def chip_move(x, pairs):
    return lax.ppermute(x, "ctx", [(2 * a + c, 2 * b + c) for a, b in pairs for c in (0, 1)])


def after(values, *earlier):
    return lax.optimization_barrier((values, earlier))[0]


class Scan:
    def __init__(self, a, b, near, forward):
        self.chips = lax.axis_size("ctx") // 2
        chip = lax.axis_index("ctx") // 2
        self.forward = forward
        self.place = chip if forward else self.chips - 1 - chip
        self.a, self.b, self.payload = a, b, near

    def move(self, x, pairs):
        last = self.chips - 1
        turn = (lambda p: p) if self.forward else (lambda p: last - p)
        return chip_move(x, [(turn(p), turn(q)) for p, q in pairs])

    def first(self):
        if self.chips == 4:
            self.near = self.move(self.payload, [(0, 1), (1, 2), (2, 3)])
            self.far = self.move(self.b, [(0, 2)])

    def turn_around(self, *earlier):
        if self.chips == 4:
            a, b = after((self.a, self.b), *earlier) if earlier else (self.a, self.b)
            self.payload = jnp.where(
                self.place == 1,
                a + self.near,
                jnp.where(self.place == 2, b + self.near + self.far, b),
            )

    def second(self):
        if self.chips == 4:
            self.near2 = self.move(self.payload, [(0, 1), (1, 2), (2, 3)])
            self.far2 = self.move(self.payload, [(1, 3)])
            return self.near, self.far, self.near2, self.far2
        total = jnp.concatenate([self.a, self.b], axis=0)
        before = self.move(total, [(i, i + 1) for i in range(self.chips - 1)])
        step = 1
        while step < self.chips:
            pairs = [(i, i + step) for i in range(self.chips - step)]
            before = before + self.move(before, pairs)
            step *= 2
        rows = self.a.shape[0]
        zero = jnp.zeros_like(self.a)
        return before[:rows], zero, before[rows:], zero


def scan_norms(norm, chip, chips, forward, *earlier):
    base = jnp.zeros_like(norm)
    if earlier and chips <= 4:
        bits = range(1, chips)
        moved = [chip_move(norm, [(i, i ^ bit) for i in range(chips)]) for bit in bits]
        moved = after(moved, *earlier)
        for bit in bits:
            other = chip ^ bit
            base = base + jnp.where(other < chip if forward else other > chip, moved[bit - 1], 0.0)
        return base
    total = norm
    bit = 1
    while bit < chips:
        moved = chip_move(total, [(i, i ^ bit) for i in range(chips)])
        upper = (chip & bit) != 0 if forward else (chip & bit) == 0
        base = base + jnp.where(upper, moved, 0.0)
        total = total + moved
        bit *= 2
    return base


def sum_all(mine, chips):
    dp = lax.axis_size("dp")
    share = mine.shape[0] // dp
    got = [
        lax.ppermute(mine[k * share : (k + 1) * share], "dp", [(i, i ^ k) for i in range(dp)])
        for k in range(1, dp)
    ]
    total = mine[:share]
    for piece in got:
        total = total + piece
    bit = 1
    while bit < chips:
        total = total + chip_move(total, [(i, i ^ bit) for i in range(chips)])
        bit *= 2
    pieces = [total] + [
        lax.ppermute(total, "dp", [(i, i ^ k) for i in range(dp)]) for k in range(1, dp)
    ]
    pieces = pieces + [core_swap(x) for x in pieces]
    return [x[i] for x in pieces for i in range(share)]


def shards(queries, key_tokens, value_tokens, cotangent, query_map, key_map):
    own = queries.shape[1]
    length = 2 * own
    head_count, dim, width = query_map.shape
    shared = key_tokens.shape[2] // dim
    group = head_count // shared
    feats = 2 * width
    n = shared // 2
    wide = group * feats
    queries = queries.reshape(own, head_count * dim)
    cotangent = cotangent.reshape(own, head_count * dim)
    keys = key_tokens.reshape(own, shared * dim)
    values = value_tokens.reshape(own, shared * dim)
    query_map = jnp.swapaxes(query_map, 1, 2)
    key_map = jnp.swapaxes(key_map, 1, 2)

    ctx = lax.axis_index("ctx")
    chips = lax.axis_size("ctx") // 2
    chip, core = ctx // 2, ctx % 2
    dp = lax.axis_size("dp")
    part = jnp.arange(n, dtype=jnp.int32) ^ (lax.axis_index("dp") * (n // dp))
    places = jnp.stack([core, chip, chips - 1 - chip]) if chips == 4 else jnp.stack([core, core * 0 + 3, core * 0 + 3])
    info = jnp.concatenate([part + n * core, part + n * (1 - core), places]).astype(jnp.int32)

    def spec(shape, index):
        return pl.BlockSpec(shape, index)

    def own_cols(cols):
        return spec((own, cols), lambda i, info: (0, info[i]))

    def other_cols(cols):
        return spec((own, cols), lambda i, info: (0, info[n + i]))

    def got_cols(cols):
        return spec((own, cols), lambda i, info: (0, i))

    def per_head(*shape):
        return spec((1,) + shape, lambda i, info: (i,) + (0,) * len(shape))

    def shape_of(*shape, dtype=F32):
        return jax.ShapeDtypeStruct((n,) + shape, dtype)

    def call(name, body, in_specs, out_specs, out_shape, **options):
        run = pl.pallas_call(
            body,
            name=name,
            out_shape=[pltpu.HBM(x.shape, x.dtype) for x in out_shape],
            grid_spec=pltpu.PrefetchScalarGridSpec(
                num_scalar_prefetch=1, grid=(n,), in_specs=in_specs, out_specs=out_specs
            ),
            compiler_params=pltpu.CompilerParams(vmem_limit_bytes=VMEM_LIMIT),
            **options,
        )
        return lambda *arrays: run(
            info, *[pltpu.with_memory_space_constraint(x, pltpu.HBM) for x in arrays]
        )

    def part_body(body):
        return lambda *refs: body(n, *refs)

    one, four = dim, group * dim
    map_spec = spec((group, width, dim), lambda i, info: (info[i], 0, 0))
    row_spec, row = per_head(1, wide), shape_of(1, wide)
    flat_spec, flat = per_head(wide, length), shape_of(wide, length)
    half = n // 2
    half_state = jax.ShapeDtypeStruct((half * wide, dim), F32)
    a_spec = spec((wide, dim), lambda i, info: (jnp.minimum(i, half - 1), 0))
    b_spec = spec((wide, dim), lambda i, info: (jnp.maximum(i - half, 0), 0))
    moved_spec = spec((wide, dim), lambda i, info: (i % half, 0))

    def near_spec(which):
        def index(i, info):
            off = jnp.where(info[2 * n + which] == 1, half, 0)
            return (jnp.clip(i - off, 0, half - 1), 0)

        return spec((wide, dim), index)

    def pack(name, arrays, cols):
        packed = call(
            name,
            pack_kernel,
            [other_cols(cols)] * len(arrays),
            [got_cols(cols)] * len(arrays),
            [jax.ShapeDtypeStruct((own, n * cols), F32)] * len(arrays),
        )(*arrays)
        return packed

    packed_keys = pack("pack_keys", (keys, values), one)
    packed_queries = pack("pack_queries", after((queries, cotangent), *packed_keys), four)
    keys_got, values_got = [core_swap(x) for x in packed_keys]
    queries_got, cotangent_got = [core_swap(x) for x in packed_queries]

    key_probs, key_features, norm, a, b, near = call(
        "key_features",
        part_body(key_kernel),
        [own_cols(one), got_cols(one)] * 2 + [map_spec],
        [flat_spec, flat_spec, row_spec, a_spec, b_spec, near_spec(1)],
        [flat, shape_of(wide, length, dtype=BF), row] + [half_state] * 3,
    )(keys, keys_got, values, values_got, key_map)
    prefix_norm = scan_norms(norm, chip, chips, True)
    prefix = Scan(*after((a, b, near), prefix_norm), True)
    prefix.first()

    rows_spec = per_head(group, length, dim)
    rows_bf = shape_of(group, length, dim, dtype=BF)
    query_probs, query_rows, weights, a, b, near = call(
        "query_features",
        part_body(query_kernel),
        [own_cols(four), got_cols(four)] * 2 + [map_spec, flat_spec, row_spec],
        [flat_spec, rows_spec, per_head(group, length, length), a_spec, b_spec, near_spec(2)],
        [flat, rows_bf, shape_of(group, length, length, dtype=BF)] + [half_state] * 3,
    )(queries, queries_got, cotangent, cotangent_got, query_map, key_features, prefix_norm)
    suffix = Scan(a, b, near, False)
    suffix.first()
    prefix.turn_around(near)
    before = prefix.second()
    suffix.turn_around()
    before = after(before, suffix.payload)
    later = suffix.second()

    attended, attended_got, scaled, norm_lanes, norm = call(
        "attend",
        part_body(attend_kernel),
        [own_cols(four), got_cols(four), own_cols(one), got_cols(one)]
        + [rows_spec, per_head(group, length, length), row_spec]
        + [moved_spec] * 4,
        [own_cols(four), got_cols(four), rows_spec, rows_spec, row_spec],
        [
            jax.ShapeDtypeStruct((own, head_count * dim), BF),
            jax.ShapeDtypeStruct((own, n * four), F32),
            rows_bf,
            rows_bf,
            row,
        ],
    )(cotangent, cotangent_got, values, values_got, query_rows, weights, prefix_norm, *before)
    suffix_norm = scan_norms(norm, chip, chips, False, *later)
    grad_spec, grad = per_head(group * width, dim), shape_of(group * width, dim)
    query_part, key_up = call(
        "query_grads",
        part_body(query_grad_kernel),
        [own_cols(four), got_cols(four), own_cols(one), got_cols(one)]
        + [flat_spec, flat_spec, rows_spec, rows_spec, row_spec]
        + [moved_spec] * 4,
        [grad_spec, flat_spec],
        [grad, flat],
    )(
        queries, queries_got, values, values_got, key_features, query_probs, scaled, norm_lanes,
        prefix_norm, *before,
    )
    (key_part,) = call(
        "key_grads",
        part_body(key_grad_kernel),
        [own_cols(one), got_cols(one)] * 2 + [flat_spec, flat_spec, row_spec] + [moved_spec] * 4,
        [grad_spec],
        [grad],
    )(keys, keys_got, values, values_got, key_probs, key_up, suffix_norm, *later)
    (attended,) = call(
        "attended",
        attended_kernel,
        [got_cols(four), pl.BlockSpec(memory_space=pl.ANY)],
        [other_cols(four)],
        [jax.ShapeDtypeStruct((own, head_count * dim), BF)],
        input_output_aliases={2: 0},
    )(core_swap(attended_got), attended)

    def finish(name, mine):
        pieces = sum_all(mine, chips)
        whole = pl.BlockSpec(memory_space=pltpu.VMEM)
        natural = pl.pallas_call(
            out_kernel,
            name=name,
            out_shape=jax.ShapeDtypeStruct((shared, group * width, dim), F32),
            in_specs=[pl.BlockSpec(memory_space=pltpu.SMEM)] + [whole] * shared,
            out_specs=whole,
            compiler_params=pltpu.CompilerParams(vmem_limit_bytes=VMEM_LIMIT),
        )(info, *pieces)
        return jnp.swapaxes(natural.reshape(head_count, width, dim), 1, 2)

    query_grad = finish("query_out", query_part)
    key_grad = finish("key_out", key_part)
    return attended.reshape(1, own, head_count * dim), query_grad, key_grad


def solution(mesh):
    in_specs = (
        P("dp", "ctx", None),
        P("dp", "ctx", None),
        P("dp", "ctx", None),
        P("dp", "ctx", None),
        P(),
        P(),
    )
    out_specs = (P("dp", "ctx", None), P(), P())
    return jax.shard_map(shards, mesh=mesh, in_specs=in_specs, out_specs=out_specs, check_vma=False)
```

```python
import jax
import jax.numpy as jnp
from jax import lax
from jax.experimental import pallas as pl
from jax.experimental.pallas import tpu as pltpu
from jax.sharding import PartitionSpec as P

BF = jnp.bfloat16
F32 = jnp.float32
VMEM_LIMIT = 32 * 1024 * 1024


def mm(a, b):
    return jnp.dot(a, b, preferred_element_type=F32)


def mm_nt(a, b):
    return lax.dot_general(a, b, (((1,), (1,)), ((), ())), preferred_element_type=F32)


def split(x):
    high = x.astype(BF)
    return high, (x - high.astype(F32)).astype(BF)


def cat(*pieces):
    return jnp.concatenate(pieces, axis=1)


def stack(*pieces):
    return jnp.concatenate(pieces, axis=0)


def soft(scores):
    top = jnp.max(scores, axis=0, keepdims=True)
    raised = jnp.exp(scores - top)
    return raised * (1.0 / jnp.sum(raised, axis=0, keepdims=True))


def both_soft(scores):
    return stack(soft(scores), soft(-scores))


def soft_back(probs, upstream):
    half = probs.shape[0] // 2
    p, n = probs[:half], probs[half:]
    gp, gn = upstream[:half], upstream[half:]
    result = p * (gp - jnp.sum(p * gp, axis=0, keepdims=True))
    result = result - n * (gn - jnp.sum(n * gn, axis=0, keepdims=True))
    return result.astype(BF)


def causal_mask(core, tokens):
    own = tokens // 2
    shift = core * own
    rows = lax.broadcasted_iota(jnp.int32, (tokens, tokens), 0)
    cols = lax.broadcasted_iota(jnp.int32, (tokens, tokens), 1)
    rows = rows + jnp.where(rows < own, shift, -shift)
    cols = cols + jnp.where(cols < own, shift, -shift)
    return rows >= cols


def column(row):
    return jnp.broadcast_to(row, (8, row.shape[1])).T[:, :1]


def three_lanes(wide, order):
    lane = lax.broadcasted_iota(jnp.int32, wide.shape, 1)
    high = wide.astype(BF).astype(F32)
    parts = {"h": high, "l": wide - high}
    result = jnp.where(lane == 2, parts[order[2]], 0.0)
    result = jnp.where(lane == 1, parts[order[1]], result)
    return jnp.where(lane == 0, parts[order[0]], result).astype(BF)


def tokens_of(own_ref, got_ref):
    return stack(own_ref[...], got_ref[...].astype(BF))


def put_parts(place, half, n, value, a_ref, b_ref, near_ref):
    i = pl.program_id(0)

    @pl.when(i < half)
    def _():
        a_ref[...] = value

    @pl.when(i >= half)
    def _():
        b_ref[...] = value

    @pl.when((i >= half) == (place == 1))
    def _():
        near_ref[...] = value


def before_of(place, half, near, far, near2, far2):
    first = jnp.where(place == 2, near2[...], near[...] + far2[...])
    second = jnp.where(place == 2, near[...] + far[...], near2[...])
    return jnp.where(pl.program_id(0) < half, first, second)


def pack_kernel(n, info, *refs):
    half = len(refs) // 2
    for x_ref, o_ref in zip(refs[:half], refs[half:]):
        cols = x_ref.shape[1] // n
        for i in range(n):
            start = pl.multiple_of((info[n + i] % n) * cols, cols)
            o_ref[:, i * cols : (i + 1) * cols] = x_ref[:, pl.ds(start, cols)].astype(F32)


def key_kernel(
    n, info, k_ref, kg_ref, v_ref, vg_ref, w_ref, kp_ref, kb_ref, norm_ref, a_ref, b_ref, near_ref
):
    group, width, dim = w_ref.shape
    keys = tokens_of(k_ref, kg_ref)
    values = tokens_of(v_ref, vg_ref)
    scores = mm_nt(w_ref[...].reshape(group * width, dim), keys)
    probs = stack(*[both_soft(scores[i * width : (i + 1) * width]) for i in range(group)])
    features = probs.astype(BF)
    kp_ref[0] = probs
    kb_ref[0] = features
    norm_ref[0] = mm_nt(jnp.ones((16, keys.shape[0]), BF), features)[:1]
    put_parts(info[2 * n + 1], n // 2, n, mm(features, values), a_ref, b_ref, near_ref)


def query_kernel(
    n, info, q_ref, qg_ref, c_ref, cg_ref, w_ref, kb_ref, pn_ref,
    qp_ref, qr_ref, wt_ref, a_ref, b_ref, near_ref,
):
    group, width, dim = w_ref.shape
    feats = 2 * width
    queries = tokens_of(q_ref, qg_ref)
    upstream = stack(c_ref[...].astype(F32), cg_ref[...])
    length = queries.shape[0]
    causal = causal_mask(info[2 * n], length)
    heads = range(group)
    cols = [slice(i * dim, (i + 1) * dim) for i in heads]
    rows = [slice(i * feats, (i + 1) * feats) for i in heads]
    scores = [mm_nt(w_ref[i], queries[:, cols[i]]) for i in heads]
    probs = [both_soft(x) for x in scores]
    query_t = [x.astype(BF) for x in probs]
    query_rows = [x.T for x in query_t]
    weights = [mm(query_rows[i], kb_ref[0, rows[i]]) for i in heads]
    weights = [jnp.where(causal, x, 0.0).astype(BF) for x in weights]
    norms = split(jnp.broadcast_to(pn_ref[0], (dim, group * feats)))
    ones = jnp.ones((dim, length), BF)
    den = [
        mm_nt(
            cat(weights[i], query_rows[i], query_rows[i]),
            cat(ones, norms[0][:, rows[i]], norms[1][:, rows[i]]),
        )
        for i in heads
    ]
    scaled = [(upstream[:, cols[i]] * (1.0 / den[i])).astype(BF) for i in heads]
    sums = [mm(query_t[i], scaled[i]) for i in heads]
    for i in heads:
        qp_ref[0, rows[i]] = probs[i]
        qr_ref[0, i] = query_rows[i]
        wt_ref[0, i] = weights[i]
    put_parts(info[2 * n + 2], n // 2, n, stack(*sums), a_ref, b_ref, near_ref)


def attend_kernel(
    n, info, c_ref, cg_ref, v_ref, vg_ref, qr_ref, wt_ref, pn_ref, near, far, near2, far2,
    att_ref, atg_ref, sc_ref, nl_ref, sn_ref,
):
    group, length, dim = qr_ref.shape[1:]
    feats = dim
    own = length // 2
    heads = range(group)
    cols = [slice(i * dim, (i + 1) * dim) for i in heads]
    rows = [slice(i * feats, (i + 1) * feats) for i in heads]
    upstream = stack(c_ref[...].astype(F32), cg_ref[...])
    values = tokens_of(v_ref, vg_ref)
    high, low = split(before_of(info[2 * n + 1], n // 2, near, far, near2, far2))
    norm_high, norm_low = split(jnp.broadcast_to(column(pn_ref[0]), (group * feats, dim)))
    high, low = cat(high, norm_high), cat(low, norm_low)
    values = cat(values, jnp.ones((length, dim), BF))
    query_rows = [qr_ref[0, i] for i in heads]
    both = [
        mm(cat(wt_ref[0, i], query_rows[i], query_rows[i]), stack(values, high[rows[i]], low[rows[i]]))
        for i in heads
    ]
    numerator = [x[:, :dim] for x in both]
    inverse = [1.0 / x[:, dim:] for x in both]
    scaled = [upstream[:, cols[i]] * inverse[i] for i in heads]
    products = [cat(*split(-(scaled[i] * inverse[i]) * numerator[i])) for i in heads]
    ones = jnp.ones((2 * dim, dim), BF)
    norm_grad = [mm(x, ones) for x in products]
    for i in heads:
        result = numerator[i] * inverse[i]
        att_ref[:, cols[i]] = result[:own].astype(BF)
        atg_ref[:, cols[i]] = result[own:]
        sc_ref[0, i] = scaled[i].astype(BF)
        nl_ref[0, i] = three_lanes(norm_grad[i], "hlh")
        sn_ref[0, :, rows[i]] = jnp.sum(
            query_rows[i].astype(F32) * norm_grad[i], axis=0, keepdims=True
        )


def query_grad_kernel(
    n, info, q_ref, qg_ref, v_ref, vg_ref, kb_ref, qp_ref, sc_ref, nl_ref, pn_ref,
    near, far, near2, far2, gq_ref, gk_ref,
):
    group, length, dim = sc_ref.shape[1:]
    feats = dim
    width = feats // 2
    heads = range(group)
    cols = [slice(i * dim, (i + 1) * dim) for i in heads]
    rows = [slice(i * feats, (i + 1) * feats) for i in heads]
    causal = causal_mask(info[2 * n], length)
    queries = tokens_of(q_ref, qg_ref)
    lane = lax.broadcasted_iota(jnp.int32, (length, dim), 1)
    values = cat(tokens_of(v_ref, vg_ref), jnp.where(lane < 2, 1.0, 0.0).astype(BF))
    high, low = split(before_of(info[2 * n + 1], n // 2, near, far, near2, far2))
    norm_cols = three_lanes(jnp.broadcast_to(column(pn_ref[0]), (group * feats, dim)), "hhl")
    scaled = [sc_ref[0, i] for i in heads]
    lanes = [nl_ref[0, i] for i in heads]
    mixed = [mm_nt(cat(scaled[i], lanes[i]), values) for i in heads]
    block = [jnp.where(causal, x, 0.0).astype(BF) for x in mixed]
    upstream = [
        mm_nt(
            cat(kb_ref[0, rows[i]], high[rows[i]], norm_cols[rows[i]], low[rows[i]]),
            cat(block[i], scaled[i], lanes[i], scaled[i]),
        )
        for i in heads
    ]
    probs = [qp_ref[0, r] for r in rows]
    back = [soft_back(probs[i], upstream[i]) for i in heads]
    for i in heads:
        gq_ref[0, i * width : (i + 1) * width] = mm(back[i], queries[:, cols[i]])
        gk_ref[0, rows[i]] = mm(probs[i].astype(BF), block[i])


def key_grad_kernel(
    n, info, k_ref, kg_ref, v_ref, vg_ref, kp_ref, gk_ref, sn_ref, near, far, near2, far2, out_ref
):
    rows, length = kp_ref.shape[1:]
    feats = k_ref.shape[1]
    values = tokens_of(v_ref, vg_ref)
    state = cat(*split(before_of(info[2 * n + 2], n // 2, near, far, near2, far2)))
    upstream = gk_ref[0] + mm_nt(state, cat(values, values))
    upstream = upstream + jnp.broadcast_to(column(sn_ref[0]), (rows, length))
    back = [
        soft_back(kp_ref[0, a : a + feats], upstream[a : a + feats])
        for a in range(0, rows, feats)
    ]
    out_ref[0] = mm(stack(*back), tokens_of(k_ref, kg_ref))


def attended_kernel(n, info, x_ref, kept_ref, o_ref):
    cols = o_ref.shape[1] // n
    for i in range(n):
        start = pl.multiple_of((info[n + i] % n) * cols, cols)
        o_ref[:, pl.ds(start, cols)] = x_ref[:, i * cols : (i + 1) * cols].astype(BF)


def out_kernel(info, *refs):
    out_ref = refs[-1]
    for i, ref in enumerate(refs[:-1]):
        out_ref[info[i]] = ref[...]


def core_swap(x):
    size = lax.axis_size("ctx")
    return lax.ppermute(x, "ctx", [(i, i ^ 1) for i in range(size)])


def chip_move(x, pairs):
    return lax.ppermute(x, "ctx", [(2 * a + c, 2 * b + c) for a, b in pairs for c in (0, 1)])


def after(values, *earlier):
    return lax.optimization_barrier((values, earlier))[0]


class Scan:
    def __init__(self, a, b, near, forward):
        self.chips = lax.axis_size("ctx") // 2
        chip = lax.axis_index("ctx") // 2
        self.forward = forward
        self.place = chip if forward else self.chips - 1 - chip
        self.a, self.b, self.payload = a, b, near

    def move(self, x, pairs):
        last = self.chips - 1
        turn = (lambda p: p) if self.forward else (lambda p: last - p)
        return chip_move(x, [(turn(p), turn(q)) for p, q in pairs])

    def first(self):
        if self.chips == 4:
            self.near = self.move(self.payload, [(0, 1), (1, 2), (2, 3)])
            self.far = self.move(self.b, [(0, 2)])

    def turn_around(self, *earlier):
        if self.chips == 4:
            a, b = after((self.a, self.b), *earlier) if earlier else (self.a, self.b)
            self.payload = jnp.where(
                self.place == 1,
                a + self.near,
                jnp.where(self.place == 2, b + self.near + self.far, b),
            )

    def second(self):
        if self.chips == 4:
            self.near2 = self.move(self.payload, [(0, 1), (1, 2), (2, 3)])
            self.far2 = self.move(self.payload, [(1, 3)])
            return self.near, self.far, self.near2, self.far2
        total = jnp.concatenate([self.a, self.b], axis=0)
        before = self.move(total, [(i, i + 1) for i in range(self.chips - 1)])
        step = 1
        while step < self.chips:
            pairs = [(i, i + step) for i in range(self.chips - step)]
            before = before + self.move(before, pairs)
            step *= 2
        rows = self.a.shape[0]
        zero = jnp.zeros_like(self.a)
        return before[:rows], zero, before[rows:], zero


def scan_norms(norm, chip, chips, forward, *earlier):
    base = jnp.zeros_like(norm)
    if earlier and chips <= 4:
        bits = range(1, chips)
        moved = [chip_move(norm, [(i, i ^ bit) for i in range(chips)]) for bit in bits]
        moved = after(moved, *earlier)
        for bit in bits:
            other = chip ^ bit
            base = base + jnp.where(other < chip if forward else other > chip, moved[bit - 1], 0.0)
        return base
    total = norm
    bit = 1
    while bit < chips:
        moved = chip_move(total, [(i, i ^ bit) for i in range(chips)])
        upper = (chip & bit) != 0 if forward else (chip & bit) == 0
        base = base + jnp.where(upper, moved, 0.0)
        total = total + moved
        bit *= 2
    return base


def sum_all(mine, chips, *earlier):
    dp = lax.axis_size("dp")
    share = mine.shape[0] // dp
    got = [
        lax.ppermute(mine[k * share : (k + 1) * share], "dp", [(i, i ^ k) for i in range(dp)])
        for k in range(1, dp)
    ]
    if earlier:
        got = after(got, *earlier)
    total = mine[:share]
    for piece in got:
        total = total + piece
    bit = 1
    while bit < chips:
        total = total + chip_move(total, [(i, i ^ bit) for i in range(chips)])
        bit *= 2
    pieces = [total] + [
        lax.ppermute(total, "dp", [(i, i ^ k) for i in range(dp)]) for k in range(1, dp)
    ]
    pieces = pieces + [core_swap(x) for x in pieces]
    return [x[i] for x in pieces for i in range(share)]


def shards(queries, key_tokens, value_tokens, cotangent, query_map, key_map):
    own = queries.shape[1]
    length = 2 * own
    head_count, dim, width = query_map.shape
    shared = key_tokens.shape[2] // dim
    group = head_count // shared
    feats = 2 * width
    n = shared // 2
    wide = group * feats
    queries = queries.reshape(own, head_count * dim)
    cotangent = cotangent.reshape(own, head_count * dim)
    keys = key_tokens.reshape(own, shared * dim)
    values = value_tokens.reshape(own, shared * dim)
    query_map = jnp.swapaxes(query_map, 1, 2)
    key_map = jnp.swapaxes(key_map, 1, 2)

    ctx = lax.axis_index("ctx")
    chips = lax.axis_size("ctx") // 2
    chip, core = ctx // 2, ctx % 2
    dp = lax.axis_size("dp")
    part = jnp.arange(n, dtype=jnp.int32) ^ (lax.axis_index("dp") * (n // dp))
    places = jnp.stack([core, chip, chips - 1 - chip]) if chips == 4 else jnp.stack([core, core * 0 + 3, core * 0 + 3])
    info = jnp.concatenate([part + n * core, part + n * (1 - core), places]).astype(jnp.int32)

    def spec(shape, index):
        return pl.BlockSpec(shape, index)

    def own_cols(cols):
        return spec((own, cols), lambda i, info: (0, info[i]))

    def other_cols(cols):
        return spec((own, cols), lambda i, info: (0, info[n + i]))

    def got_cols(cols):
        return spec((own, cols), lambda i, info: (0, i))

    def per_head(*shape):
        return spec((1,) + shape, lambda i, info: (i,) + (0,) * len(shape))

    def shape_of(*shape, dtype=F32):
        return jax.ShapeDtypeStruct((n,) + shape, dtype)

    def call(name, body, in_specs, out_specs, out_shape, steps=n, **options):
        run = pl.pallas_call(
            body,
            name=name,
            out_shape=[pltpu.HBM(x.shape, x.dtype) for x in out_shape],
            grid_spec=pltpu.PrefetchScalarGridSpec(
                num_scalar_prefetch=1, grid=(steps,), in_specs=in_specs, out_specs=out_specs
            ),
            compiler_params=pltpu.CompilerParams(vmem_limit_bytes=VMEM_LIMIT),
            **options,
        )
        return lambda *arrays: run(
            info, *[pltpu.with_memory_space_constraint(x, pltpu.HBM) for x in arrays]
        )

    def part_body(body):
        return lambda *refs: body(n, *refs)

    one, four = dim, group * dim
    map_spec = spec((group, width, dim), lambda i, info: (info[i], 0, 0))
    row_spec, row = per_head(1, wide), shape_of(1, wide)
    flat_spec, flat = per_head(wide, length), shape_of(wide, length)
    half = n // 2
    half_state = jax.ShapeDtypeStruct((half * wide, dim), F32)
    a_spec = spec((wide, dim), lambda i, info: (jnp.minimum(i, half - 1), 0))
    b_spec = spec((wide, dim), lambda i, info: (jnp.maximum(i - half, 0), 0))
    moved_spec = spec((wide, dim), lambda i, info: (i % half, 0))

    def near_spec(which):
        def index(i, info):
            off = jnp.where(info[2 * n + which] == 1, half, 0)
            return (jnp.clip(i - off, 0, half - 1), 0)

        return spec((wide, dim), index)

    def other_half(cols):
        return spec((own, n * cols), lambda i, info: (0, info[n] // n))

    def pack(name, arrays, cols):
        return call(
            name,
            part_body(pack_kernel),
            [other_half(cols)] * len(arrays),
            [spec((own, n * cols), lambda i, info: (0, 0))] * len(arrays),
            [jax.ShapeDtypeStruct((own, n * cols), F32)] * len(arrays),
            steps=1,
        )(*arrays)

    keys_got, values_got = [core_swap(x) for x in pack("pack_keys", (keys, values), one)]
    key_probs, key_features, norm, a, b, near = call(
        "key_features",
        part_body(key_kernel),
        [own_cols(one), got_cols(one)] * 2 + [map_spec],
        [flat_spec, flat_spec, row_spec, a_spec, b_spec, near_spec(1)],
        [flat, shape_of(wide, length, dtype=BF), row] + [half_state] * 3,
    )(keys, keys_got, values, values_got, key_map)
    packed = pack("pack_queries", after((queries, cotangent), norm), four)
    queries_got, cotangent_got = [core_swap(x) for x in packed]
    prefix_norm = scan_norms(norm, chip, chips, True)
    prefix = Scan(*after((a, b, near), prefix_norm), True)
    prefix.first()

    rows_spec = per_head(group, length, dim)
    rows_bf = shape_of(group, length, dim, dtype=BF)
    query_probs, query_rows, weights, a, b, near = call(
        "query_features",
        part_body(query_kernel),
        [own_cols(four), got_cols(four)] * 2 + [map_spec, flat_spec, row_spec],
        [flat_spec, rows_spec, per_head(group, length, length), a_spec, b_spec, near_spec(2)],
        [flat, rows_bf, shape_of(group, length, length, dtype=BF)] + [half_state] * 3,
    )(queries, queries_got, cotangent, cotangent_got, query_map, key_features, prefix_norm)
    suffix = Scan(a, b, near, False)
    suffix.first()
    prefix.turn_around(near)
    before = prefix.second()
    suffix.turn_around()
    before = after(before, suffix.payload)
    later = suffix.second()

    attended, attended_got, scaled, norm_lanes, norm = call(
        "attend",
        part_body(attend_kernel),
        [own_cols(four), got_cols(four), own_cols(one), got_cols(one)]
        + [rows_spec, per_head(group, length, length), row_spec]
        + [moved_spec] * 4,
        [own_cols(four), got_cols(four), rows_spec, rows_spec, row_spec],
        [
            jax.ShapeDtypeStruct((own, head_count * dim), BF),
            jax.ShapeDtypeStruct((own, n * four), F32),
            rows_bf,
            rows_bf,
            row,
        ],
    )(cotangent, cotangent_got, values, values_got, query_rows, weights, prefix_norm, *before)
    grad_spec, grad = per_head(group * width, dim), shape_of(group * width, dim)
    query_part, key_up = call(
        "query_grads",
        part_body(query_grad_kernel),
        [own_cols(four), got_cols(four), own_cols(one), got_cols(one)]
        + [flat_spec, flat_spec, rows_spec, rows_spec, row_spec]
        + [moved_spec] * 4,
        [grad_spec, flat_spec],
        [grad, flat],
    )(
        queries, queries_got, values, values_got, key_features, query_probs, scaled, norm_lanes,
        prefix_norm, *before,
    )
    suffix_norm = scan_norms(norm, chip, chips, False, query_part)
    query_part = after(query_part, suffix_norm)
    (key_part,) = call(
        "key_grads",
        part_body(key_grad_kernel),
        [own_cols(one), got_cols(one)] * 2 + [flat_spec, flat_spec, row_spec] + [moved_spec] * 4,
        [grad_spec],
        [grad],
    )(keys, keys_got, values, values_got, key_probs, key_up, suffix_norm, *later)
    (attended,) = call(
        "attended",
        part_body(attended_kernel),
        [spec((own, n * four), lambda i, info: (0, 0)), pl.BlockSpec(memory_space=pl.ANY)],
        [other_half(four)],
        [jax.ShapeDtypeStruct((own, head_count * dim), BF)],
        steps=1,
        input_output_aliases={2: 0},
    )(core_swap(after(attended_got, *later)), attended)

    def finish(name, mine, *earlier):
        pieces = sum_all(mine, chips, *earlier)
        whole = pl.BlockSpec(memory_space=pltpu.VMEM)
        natural = pl.pallas_call(
            out_kernel,
            name=name,
            out_shape=jax.ShapeDtypeStruct((shared, group * width, dim), F32),
            in_specs=[pl.BlockSpec(memory_space=pltpu.SMEM)] + [whole] * shared,
            out_specs=whole,
            compiler_params=pltpu.CompilerParams(vmem_limit_bytes=VMEM_LIMIT),
        )(info, *pieces)
        return jnp.swapaxes(natural.reshape(head_count, width, dim), 1, 2)

    query_grad = finish("query_out", query_part, key_part)
    key_grad = finish("key_out", key_part, attended)
    return attended.reshape(1, own, head_count * dim), query_grad, key_grad


def solution(mesh):
    in_specs = (
        P("dp", "ctx", None),
        P("dp", "ctx", None),
        P("dp", "ctx", None),
        P("dp", "ctx", None),
        P(),
        P(),
    )
    out_specs = (P("dp", "ctx", None), P(), P())
    return jax.shard_map(shards, mesh=mesh, in_specs=in_specs, out_specs=out_specs, check_vma=False)
```

```python
import jax
import jax.numpy as jnp
from jax import lax
from jax.experimental import pallas as pl
from jax.experimental.pallas import tpu as pltpu
from jax.sharding import PartitionSpec as P

BF = jnp.bfloat16
F32 = jnp.float32
VMEM_LIMIT = 40 * 1024 * 1024


def mm(a, b):
    return jnp.dot(a, b, preferred_element_type=F32)


def mm_nt(a, b):
    return lax.dot_general(a, b, (((1,), (1,)), ((), ())), preferred_element_type=F32)


def split(x):
    high = x.astype(BF)
    return high, (x - high.astype(F32)).astype(BF)


def cat(*pieces):
    return jnp.concatenate(pieces, axis=1)


def stack(*pieces):
    return jnp.concatenate(pieces, axis=0)


def soft(scores):
    top = jnp.max(scores, axis=0, keepdims=True)
    raised = jnp.exp(scores - top)
    return raised * (1.0 / jnp.sum(raised, axis=0, keepdims=True))


def both_soft(scores):
    return stack(soft(scores), soft(-scores))


def soft_back(probs, upstream):
    half = probs.shape[0] // 2
    p, n = probs[:half], probs[half:]
    gp, gn = upstream[:half], upstream[half:]
    result = p * (gp - jnp.sum(p * gp, axis=0, keepdims=True))
    result = result - n * (gn - jnp.sum(n * gn, axis=0, keepdims=True))
    return result.astype(BF)


def causal_mask(core, tokens):
    own = tokens // 2
    shift = core * own
    rows = lax.broadcasted_iota(jnp.int32, (tokens, tokens), 0)
    cols = lax.broadcasted_iota(jnp.int32, (tokens, tokens), 1)
    rows = rows + jnp.where(rows < own, shift, -shift)
    cols = cols + jnp.where(cols < own, shift, -shift)
    return rows >= cols


def column(row):
    return jnp.broadcast_to(row, (8, row.shape[1])).T[:, :1]


def three_lanes(wide, order):
    lane = lax.broadcasted_iota(jnp.int32, wide.shape, 1)
    high = wide.astype(BF).astype(F32)
    parts = {"h": high, "l": wide - high}
    result = jnp.where(lane == 2, parts[order[2]], 0.0)
    result = jnp.where(lane == 1, parts[order[1]], result)
    return jnp.where(lane == 0, parts[order[0]], result).astype(BF)


def tokens_of(own_ref, got_ref):
    return stack(own_ref[...], got_ref[...].astype(BF))


def before_of(place, first, near, far, near2, far2):
    if first:
        return jnp.where(place == 2, near2[...], near[...] + far2[...])
    return jnp.where(place == 2, near[...] + far[...], near2[...])


def pack_kernel(n, i, info, *refs):
    half = len(refs) // 2
    for x_ref, o_ref in zip(refs[:half], refs[half:]):
        o_ref[...] = x_ref[...].astype(F32)


def key_kernel(
    n, i, info, k_ref, kg_ref, v_ref, vg_ref, w_ref, kp_ref, kb_ref, norm_ref, state_ref
):
    group, width, dim = w_ref.shape
    keys = tokens_of(k_ref, kg_ref)
    values = tokens_of(v_ref, vg_ref)
    scores = mm_nt(w_ref[...].reshape(group * width, dim), keys)
    probs = stack(*[both_soft(scores[a : a + width]) for a in range(0, group * width, width)])
    features = probs.astype(BF)
    kp_ref[0] = probs
    kb_ref[0] = features
    norm_ref[0] = mm_nt(jnp.ones((16, keys.shape[0]), BF), features)[:1]
    state_ref[...] = mm(features, values)


def query_kernel(
    n, step, info, q_ref, qg_ref, c_ref, cg_ref, w_ref, kb_ref, pn_ref,
    qp_ref, qr_ref, wt_ref, state_ref,
):
    group, width, dim = w_ref.shape
    feats = 2 * width
    queries = tokens_of(q_ref, qg_ref)
    upstream = stack(c_ref[...].astype(F32), cg_ref[...])
    length = queries.shape[0]
    causal = causal_mask(info[2 * n], length)
    heads = range(group)
    cols = [slice(i * dim, (i + 1) * dim) for i in heads]
    rows = [slice(i * feats, (i + 1) * feats) for i in heads]
    scores = [mm_nt(w_ref[i], queries[:, cols[i]]) for i in heads]
    probs = [both_soft(x) for x in scores]
    query_t = [x.astype(BF) for x in probs]
    query_rows = [x.T for x in query_t]
    weights = [mm(query_rows[i], kb_ref[0, rows[i]]) for i in heads]
    weights = [jnp.where(causal, x, 0.0).astype(BF) for x in weights]
    norms = split(jnp.broadcast_to(pn_ref[0], (dim, group * feats)))
    ones = jnp.ones((dim, length), BF)
    den = [
        mm_nt(
            cat(weights[i], query_rows[i], query_rows[i]),
            cat(ones, norms[0][:, rows[i]], norms[1][:, rows[i]]),
        )
        for i in heads
    ]
    scaled = [(upstream[:, cols[i]] * (1.0 / den[i])).astype(BF) for i in heads]
    sums = [mm(query_t[i], scaled[i]) for i in heads]
    for i in heads:
        qp_ref[0, rows[i]] = probs[i]
        qr_ref[0, i] = query_rows[i]
        wt_ref[0, i] = weights[i]
    state_ref[...] = stack(*sums)


def attend_kernel(
    n, step, info, c_ref, cg_ref, v_ref, vg_ref, qr_ref, wt_ref, pn_ref, near, far, near2, far2,
    att_ref, atg_ref, sc_ref, nl_ref, sn_ref,
):
    group, length, dim = qr_ref.shape[1:]
    feats = dim
    own = length // 2
    heads = range(group)
    cols = [slice(i * dim, (i + 1) * dim) for i in heads]
    rows = [slice(i * feats, (i + 1) * feats) for i in heads]
    upstream = stack(c_ref[...].astype(F32), cg_ref[...])
    values = tokens_of(v_ref, vg_ref)
    high, low = split(before_of(info[2 * n + 1], step < n // 2, near, far, near2, far2))
    norm_high, norm_low = split(jnp.broadcast_to(column(pn_ref[0]), (group * feats, dim)))
    high, low = cat(high, norm_high), cat(low, norm_low)
    values = cat(values, jnp.ones((length, dim), BF))
    query_rows = [qr_ref[0, i] for i in heads]
    both = [
        mm(cat(wt_ref[0, i], query_rows[i], query_rows[i]), stack(values, high[rows[i]], low[rows[i]]))
        for i in heads
    ]
    numerator = [x[:, :dim] for x in both]
    inverse = [1.0 / x[:, dim:] for x in both]
    scaled = [upstream[:, cols[i]] * inverse[i] for i in heads]
    products = [cat(*split(-(scaled[i] * inverse[i]) * numerator[i])) for i in heads]
    ones = jnp.ones((2 * dim, dim), BF)
    norm_grad = [mm(x, ones) for x in products]
    for i in heads:
        result = numerator[i] * inverse[i]
        att_ref[:, cols[i]] = result[:own].astype(BF)
        atg_ref[:, cols[i]] = result[own:]
        sc_ref[0, i] = scaled[i].astype(BF)
        nl_ref[0, i] = three_lanes(norm_grad[i], "hlh")
        sn_ref[0, :, rows[i]] = jnp.sum(
            query_rows[i].astype(F32) * norm_grad[i], axis=0, keepdims=True
        )


def query_grad_kernel(
    n, step, info, q_ref, qg_ref, v_ref, vg_ref, kb_ref, qp_ref, sc_ref, nl_ref, pn_ref,
    near, far, near2, far2, gq_ref, gk_ref,
):
    group, length, dim = sc_ref.shape[1:]
    feats = dim
    width = feats // 2
    heads = range(group)
    cols = [slice(i * dim, (i + 1) * dim) for i in heads]
    rows = [slice(i * feats, (i + 1) * feats) for i in heads]
    causal = causal_mask(info[2 * n], length)
    queries = tokens_of(q_ref, qg_ref)
    lane = lax.broadcasted_iota(jnp.int32, (length, dim), 1)
    values = cat(tokens_of(v_ref, vg_ref), jnp.where(lane < 2, 1.0, 0.0).astype(BF))
    high, low = split(before_of(info[2 * n + 1], step < n // 2, near, far, near2, far2))
    norm_cols = three_lanes(jnp.broadcast_to(column(pn_ref[0]), (group * feats, dim)), "hhl")
    scaled = [sc_ref[0, i] for i in heads]
    lanes = [nl_ref[0, i] for i in heads]
    mixed = [mm_nt(cat(scaled[i], lanes[i]), values) for i in heads]
    block = [jnp.where(causal, x, 0.0).astype(BF) for x in mixed]
    upstream = [
        mm_nt(
            cat(kb_ref[0, rows[i]], high[rows[i]], norm_cols[rows[i]], low[rows[i]]),
            cat(block[i], scaled[i], lanes[i], scaled[i]),
        )
        for i in heads
    ]
    probs = [qp_ref[0, r] for r in rows]
    back = [soft_back(probs[i], upstream[i]) for i in heads]
    for i in heads:
        gq_ref[0, i * width : (i + 1) * width] = mm(back[i], queries[:, cols[i]])
        gk_ref[0, rows[i]] = mm(probs[i].astype(BF), block[i])


def key_grad_kernel(
    n, step, info, k_ref, kg_ref, v_ref, vg_ref, kp_ref, gk_ref, sn_ref, near, far, near2, far2, out_ref
):
    rows, length = kp_ref.shape[1:]
    feats = k_ref.shape[1]
    values = tokens_of(v_ref, vg_ref)
    state = cat(*split(before_of(info[2 * n + 2], step < n // 2, near, far, near2, far2)))
    upstream = gk_ref[0] + mm_nt(state, cat(values, values))
    upstream = upstream + jnp.broadcast_to(column(sn_ref[0]), (rows, length))
    back = [
        soft_back(kp_ref[0, a : a + feats], upstream[a : a + feats])
        for a in range(0, rows, feats)
    ]
    out_ref[0] = mm(stack(*back), tokens_of(k_ref, kg_ref))


def attended_kernel(n, i, info, x_ref, o_ref):
    o_ref[...] = x_ref[...].astype(BF)


def out_kernel(info, *refs):
    out_ref = refs[-1]
    for i, ref in enumerate(refs[:-1]):
        out_ref[info[i]] = ref[...]


def core_swap(x):
    size = lax.axis_size("ctx")
    return lax.ppermute(x, "ctx", [(i, i ^ 1) for i in range(size)])


def chip_move(x, pairs):
    return lax.ppermute(x, "ctx", [(2 * a + c, 2 * b + c) for a, b in pairs for c in (0, 1)])


def after(values, *earlier):
    return lax.optimization_barrier((values, earlier))[0]


class Scan:
    def __init__(self, a, b, near, forward):
        self.chips = lax.axis_size("ctx") // 2
        chip = lax.axis_index("ctx") // 2
        self.forward = forward
        self.place = chip if forward else self.chips - 1 - chip
        self.a, self.b, self.payload = a, b, near

    def move(self, x, pairs):
        last = self.chips - 1
        turn = (lambda p: p) if self.forward else (lambda p: last - p)
        return chip_move(x, [(turn(p), turn(q)) for p, q in pairs])

    def first(self):
        if self.chips == 4:
            self.near = self.move(self.payload, [(0, 1), (1, 2), (2, 3)])
            self.far = self.move(self.b, [(0, 2)])

    def turn_around(self, *earlier):
        if self.chips == 4:
            a, b = after((self.a, self.b), *earlier) if earlier else (self.a, self.b)
            self.payload = jnp.where(
                self.place == 1,
                a + self.near,
                jnp.where(self.place == 2, b + self.near + self.far, b),
            )

    def second(self):
        if self.chips == 4:
            self.near2 = self.move(self.payload, [(0, 1), (1, 2), (2, 3)])
            self.far2 = self.move(self.payload, [(1, 3)])
            return self.near, self.far, self.near2, self.far2
        total = jnp.concatenate([self.a, self.b], axis=0)
        before = self.move(total, [(i, i + 1) for i in range(self.chips - 1)])
        step = 1
        while step < self.chips:
            pairs = [(i, i + step) for i in range(self.chips - step)]
            before = before + self.move(before, pairs)
            step *= 2
        rows = self.a.shape[0]
        zero = jnp.zeros_like(self.a)
        return before[:rows], zero, before[rows:], zero


def scan_norms(norm, chip, chips, forward, *earlier):
    base = jnp.zeros_like(norm)
    if earlier and chips <= 4:
        bits = range(1, chips)
        moved = [chip_move(norm, [(i, i ^ bit) for i in range(chips)]) for bit in bits]
        moved = after(moved, *earlier)
        for bit in bits:
            other = chip ^ bit
            base = base + jnp.where(other < chip if forward else other > chip, moved[bit - 1], 0.0)
        return base
    total = norm
    bit = 1
    while bit < chips:
        moved = chip_move(total, [(i, i ^ bit) for i in range(chips)])
        upper = (chip & bit) != 0 if forward else (chip & bit) == 0
        base = base + jnp.where(upper, moved, 0.0)
        total = total + moved
        bit *= 2
    return base


def sum_all(mine, chips, *earlier):
    dp = lax.axis_size("dp")
    share = mine.shape[0] // dp
    got = [
        lax.ppermute(mine[k * share : (k + 1) * share], "dp", [(i, i ^ k) for i in range(dp)])
        for k in range(1, dp)
    ]
    if earlier:
        got = after(got, *earlier)
    total = mine[:share]
    for piece in got:
        total = total + piece
    bit = 1
    while bit < chips:
        total = total + chip_move(total, [(i, i ^ bit) for i in range(chips)])
        bit *= 2
    pieces = [total] + [
        lax.ppermute(total, "dp", [(i, i ^ k) for i in range(dp)]) for k in range(1, dp)
    ]
    pieces = pieces + [core_swap(x) for x in pieces]
    return [x[i] for x in pieces for i in range(share)]


def shards(queries, key_tokens, value_tokens, cotangent, query_map, key_map):
    own = queries.shape[1]
    length = 2 * own
    head_count, dim, width = query_map.shape
    shared = key_tokens.shape[2] // dim
    group = head_count // shared
    feats = 2 * width
    n = shared // 2
    wide = group * feats
    queries = queries.reshape(own, head_count * dim)
    cotangent = cotangent.reshape(own, head_count * dim)
    keys = key_tokens.reshape(own, shared * dim)
    values = value_tokens.reshape(own, shared * dim)
    query_map = jnp.swapaxes(query_map, 1, 2)
    key_map = jnp.swapaxes(key_map, 1, 2)

    ctx = lax.axis_index("ctx")
    chips = lax.axis_size("ctx") // 2
    chip, core = ctx // 2, ctx % 2
    dp = lax.axis_size("dp")
    part = jnp.arange(n, dtype=jnp.int32) ^ (lax.axis_index("dp") * (n // dp))
    places = jnp.stack([core, chip, chips - 1 - chip]) if chips == 4 else jnp.stack([core, core * 0 + 3, core * 0 + 3])
    info = jnp.concatenate([part + n * core, part + n * (1 - core), places]).astype(jnp.int32)

    def spec(shape, index):
        return pl.BlockSpec(shape, index)

    def own_cols(cols):
        return spec((own, cols), lambda i, info: (0, info[i]))

    def other_cols(cols):
        return spec((own, cols), lambda i, info: (0, info[n + i]))

    def got_cols(cols):
        return spec((own, cols), lambda i, info: (0, i))

    def per_head(*shape):
        return spec((1,) + shape, lambda i, info: (i,) + (0,) * len(shape))

    def shape_of(*shape, dtype=F32):
        return jax.ShapeDtypeStruct((n,) + shape, dtype)

    def block(ref, spec, i, info):
        places = spec.index_map(i, info)
        return ref.at[
            tuple(
                pl.ds(p * size if isinstance(p, int) else pl.multiple_of(p * size, size), size)
                for p, size in zip(places, spec.block_shape)
            )
        ]

    def call(name, body, in_specs, out_specs, out_shape, aliases=None):
        in_specs = [x if isinstance(x, tuple) else (x, n) for x in in_specs]
        kinds = [x.dtype for x in out_shape]
        results = {}
        for (spec_, which, _), kind in zip(out_specs, kinds):
            results[which] = (spec_.block_shape, kind)
        results = [results[k] for k in range(len(results))]
        extra = len(aliases or {})

        def kernel(info, *refs):
            count = len(in_specs) + extra
            ins, outs = refs[: len(in_specs)], refs[count : count + len(out_specs)]
            rest = refs[count + len(out_specs) :]
            in_bufs, out_bufs = rest[: len(in_specs)], rest[len(in_specs) : -2]
            in_sem, out_sem = rest[-2:]

            def incoming(i):
                return [
                    pltpu.make_async_copy(block(ref, spec_, i, info), buf.at[i], in_sem.at[k, i])
                    for k, ((spec_, period), ref, buf) in enumerate(zip(in_specs, ins, in_bufs))
                    if i < period
                ]

            def outgoing(i, act):
                for k, ((spec_, which, when), ref) in enumerate(zip(out_specs, outs)):
                    here = when(i, info)
                    if here is False:
                        continue
                    copy = pltpu.make_async_copy(
                        out_bufs[which].at[i], block(ref, spec_, i, info), out_sem.at[k, i]
                    )
                    if here is True:
                        act(copy)
                    else:
                        pl.when(here)(lambda copy=copy: act(copy))

            for i in range(n):
                for copy in incoming(i):
                    copy.start()
            for i in range(n):
                for copy in incoming(i):
                    copy.wait()
                blocks = [buf.at[i % period] for (_, period), buf in zip(in_specs, in_bufs)]
                body(n, i, info, *blocks, *[buf.at[i] for buf in out_bufs])
                outgoing(i, lambda copy: copy.start())
            for i in range(n):
                outgoing(i, lambda copy: copy.wait())

        def run(*arrays):
            anywhere = pl.BlockSpec(memory_space=pl.ANY)
            buffers = [
                pltpu.VMEM((period,) + tuple(x.block_shape), y.dtype)
                for (x, period), y in zip(in_specs, arrays)
            ] + [pltpu.VMEM((n,) + tuple(shape), kind) for shape, kind in results]
            return pl.pallas_call(
                kernel,
                name=name,
                out_shape=[pltpu.HBM(x.shape, x.dtype) for x in out_shape],
                in_specs=[pl.BlockSpec(memory_space=pltpu.SMEM)] + [anywhere] * len(arrays),
                out_specs=[anywhere] * len(out_shape),
                scratch_shapes=buffers
                + [
                    pltpu.SemaphoreType.DMA((len(in_specs), n)),
                    pltpu.SemaphoreType.DMA((len(out_specs), n)),
                ],
                input_output_aliases=aliases or {},
                compiler_params=pltpu.CompilerParams(vmem_limit_bytes=VMEM_LIMIT),
            )(info, *[pltpu.with_memory_space_constraint(x, pltpu.HBM) for x in arrays])

        return run

    def always(i, info):
        return True

    def each(*specs):
        return [(x, k, always) for k, x in enumerate(specs)]

    one, four = dim, group * dim
    map_spec = spec((group, width, dim), lambda i, info: (info[i], 0, 0))
    row_spec, row = per_head(1, wide), shape_of(1, wide)
    flat_spec, flat = per_head(wide, length), shape_of(wide, length)
    half = n // 2
    half_state = jax.ShapeDtypeStruct((half * wide, dim), F32)
    moved_spec = (spec((wide, dim), lambda i, info: (i, 0)), half)
    half_spec = spec((wide, dim), lambda i, info: (i % half, 0))

    def states(which, place):
        return [
            (half_spec, which, lambda i, info: i < half),
            (half_spec, which, lambda i, info: i >= half),
            (half_spec, which, lambda i, info: (info[2 * n + place] == 1) == (i >= half)),
        ]

    def pack(name, arrays, cols):
        return call(
            name,
            pack_kernel,
            [other_cols(cols)] * len(arrays),
            each(*[got_cols(cols)] * len(arrays)),
            [jax.ShapeDtypeStruct((own, n * cols), F32)] * len(arrays),
        )(*arrays)

    keys_got, values_got = [core_swap(x) for x in pack("pack_keys", (keys, values), one)]
    key_probs, key_features, norm, a, b, near = call(
        "key_features",
        key_kernel,
        [own_cols(one), got_cols(one)] * 2 + [map_spec],
        each(flat_spec, flat_spec, row_spec) + states(3, 1),
        [flat, shape_of(wide, length, dtype=BF), row] + [half_state] * 3,
    )(keys, keys_got, values, values_got, key_map)
    packed = pack("pack_queries", after((queries, cotangent), norm), four)
    queries_got, cotangent_got = [core_swap(x) for x in packed]
    prefix_norm = scan_norms(norm, chip, chips, True)
    prefix = Scan(*after((a, b, near), prefix_norm), True)
    prefix.first()

    rows_spec = per_head(group, length, dim)
    rows_bf = shape_of(group, length, dim, dtype=BF)
    query_probs, query_rows, weights, a, b, near = call(
        "query_features",
        query_kernel,
        [own_cols(four), got_cols(four)] * 2 + [map_spec, flat_spec, row_spec],
        each(flat_spec, rows_spec, per_head(group, length, length)) + states(3, 2),
        [flat, rows_bf, shape_of(group, length, length, dtype=BF)] + [half_state] * 3,
    )(queries, queries_got, cotangent, cotangent_got, query_map, key_features, prefix_norm)
    suffix = Scan(a, b, near, False)
    suffix.first()
    prefix.turn_around(near)
    before = prefix.second()
    suffix.turn_around()
    before = after(before, suffix.payload)
    later = suffix.second()

    attended, attended_got, scaled, norm_lanes, norm = call(
        "attend",
        attend_kernel,
        [own_cols(four), got_cols(four), own_cols(one), got_cols(one)]
        + [rows_spec, per_head(group, length, length), row_spec]
        + [moved_spec] * 4,
        each(own_cols(four), got_cols(four), rows_spec, rows_spec, row_spec),
        [
            jax.ShapeDtypeStruct((own, head_count * dim), BF),
            jax.ShapeDtypeStruct((own, n * four), F32),
            rows_bf,
            rows_bf,
            row,
        ],
    )(cotangent, cotangent_got, values, values_got, query_rows, weights, prefix_norm, *before)
    grad_spec, grad = per_head(group * width, dim), shape_of(group * width, dim)
    query_part, key_up = call(
        "query_grads",
        query_grad_kernel,
        [own_cols(four), got_cols(four), own_cols(one), got_cols(one)]
        + [flat_spec, flat_spec, rows_spec, rows_spec, row_spec]
        + [moved_spec] * 4,
        each(grad_spec, flat_spec),
        [grad, flat],
    )(
        queries, queries_got, values, values_got, key_features, query_probs, scaled, norm_lanes,
        prefix_norm, *before,
    )
    suffix_norm = scan_norms(norm, chip, chips, False, query_part)
    query_part = after(query_part, suffix_norm)
    (key_part,) = call(
        "key_grads",
        key_grad_kernel,
        [own_cols(one), got_cols(one)] * 2 + [flat_spec, flat_spec, row_spec] + [moved_spec] * 4,
        each(grad_spec),
        [grad],
    )(keys, keys_got, values, values_got, key_probs, key_up, suffix_norm, *later)
    (attended,) = call(
        "attended",
        attended_kernel,
        [got_cols(four)],
        each(other_cols(four)),
        [jax.ShapeDtypeStruct((own, head_count * dim), BF)],
        aliases={2: 0},
    )(core_swap(after(attended_got, *later)), attended)

    def finish(name, mine, *earlier):
        pieces = sum_all(mine, chips, *earlier)
        whole = pl.BlockSpec(memory_space=pltpu.VMEM)
        natural = pl.pallas_call(
            out_kernel,
            name=name,
            out_shape=jax.ShapeDtypeStruct((shared, group * width, dim), F32),
            in_specs=[pl.BlockSpec(memory_space=pltpu.SMEM)] + [whole] * shared,
            out_specs=whole,
            compiler_params=pltpu.CompilerParams(vmem_limit_bytes=VMEM_LIMIT),
        )(info, *pieces)
        return jnp.swapaxes(natural.reshape(head_count, width, dim), 1, 2)

    query_grad = finish("query_out", query_part, key_part)
    key_grad = finish("key_out", key_part, attended)
    return attended.reshape(1, own, head_count * dim), query_grad, key_grad


def solution(mesh):
    in_specs = (
        P("dp", "ctx", None),
        P("dp", "ctx", None),
        P("dp", "ctx", None),
        P("dp", "ctx", None),
        P(),
        P(),
    )
    out_specs = (P("dp", "ctx", None), P(), P())
    return jax.shard_map(shards, mesh=mesh, in_specs=in_specs, out_specs=out_specs, check_vma=False)
```

```python
import jax
import jax.numpy as jnp
from jax import lax
from jax.experimental import pallas as pl
from jax.experimental.pallas import tpu as pltpu
from jax.sharding import PartitionSpec as P

BF = jnp.bfloat16
F32 = jnp.float32
VMEM_LIMIT = 40 * 1024 * 1024


def mm(a, b):
    return jnp.dot(a, b, preferred_element_type=F32)


def mm_nt(a, b):
    return lax.dot_general(a, b, (((1,), (1,)), ((), ())), preferred_element_type=F32)


def split(x):
    high = x.astype(BF)
    return high, (x - high.astype(F32)).astype(BF)


def cat(*pieces):
    return jnp.concatenate(pieces, axis=1)


def stack(*pieces):
    return jnp.concatenate(pieces, axis=0)


def soft(scores):
    top = jnp.max(scores, axis=0, keepdims=True)
    raised = jnp.exp(scores - top)
    return raised * (1.0 / jnp.sum(raised, axis=0, keepdims=True))


def both_soft(scores):
    return stack(soft(scores), soft(-scores))


def soft_back(probs, upstream):
    half = probs.shape[0] // 2
    p, n = probs[:half], probs[half:]
    gp, gn = upstream[:half], upstream[half:]
    result = p * (gp - jnp.sum(p * gp, axis=0, keepdims=True))
    result = result - n * (gn - jnp.sum(n * gn, axis=0, keepdims=True))
    return result.astype(BF)


def causal_mask(core, tokens):
    own = tokens // 2
    shift = core * own
    rows = lax.broadcasted_iota(jnp.int32, (tokens, tokens), 0)
    cols = lax.broadcasted_iota(jnp.int32, (tokens, tokens), 1)
    rows = rows + jnp.where(rows < own, shift, -shift)
    cols = cols + jnp.where(cols < own, shift, -shift)
    return rows >= cols


def column(row):
    return jnp.broadcast_to(row, (8, row.shape[1])).T[:, :1]


def three_lanes(wide, order):
    lane = lax.broadcasted_iota(jnp.int32, wide.shape, 1)
    high = wide.astype(BF).astype(F32)
    parts = {"h": high, "l": wide - high}
    result = jnp.where(lane == 2, parts[order[2]], 0.0)
    result = jnp.where(lane == 1, parts[order[1]], result)
    return jnp.where(lane == 0, parts[order[0]], result).astype(BF)


def tokens_of(own_ref, got_ref):
    return stack(own_ref[...], got_ref[...].astype(BF))


def before_of(place, first, near, far, near2, far2):
    if first:
        return jnp.where(place == 2, near2[...], near[...] + far2[...])
    return jnp.where(place == 2, near[...] + far[...], near2[...])


def key_kernel(
    n, i, info, k_ref, kg_ref, v_ref, vg_ref, w_ref, q_ref, c_ref,
    kp_ref, kb_ref, norm_ref, state_ref, qw_ref, cw_ref,
):
    group, width, dim = w_ref.shape
    keys = tokens_of(k_ref, kg_ref)
    values = tokens_of(v_ref, vg_ref)
    scores = mm_nt(w_ref[...].reshape(group * width, dim), keys)
    probs = stack(*[both_soft(scores[a : a + width]) for a in range(0, group * width, width)])
    features = probs.astype(BF)
    kp_ref[0] = probs
    kb_ref[0] = features
    norm_ref[0] = mm_nt(jnp.ones((16, keys.shape[0]), BF), features)[:1]
    state_ref[...] = mm(features, values)
    qw_ref[...] = q_ref[...].astype(F32)
    cw_ref[...] = c_ref[...].astype(F32)


def query_kernel(
    n, step, info, q_ref, qg_ref, c_ref, cg_ref, w_ref, kb_ref, pn_ref,
    qp_ref, qr_ref, wt_ref, state_ref,
):
    group, width, dim = w_ref.shape
    feats = 2 * width
    queries = tokens_of(q_ref, qg_ref)
    upstream = stack(c_ref[...].astype(F32), cg_ref[...])
    length = queries.shape[0]
    causal = causal_mask(info[2 * n], length)
    heads = range(group)
    cols = [slice(i * dim, (i + 1) * dim) for i in heads]
    rows = [slice(i * feats, (i + 1) * feats) for i in heads]
    scores = [mm_nt(w_ref[i], queries[:, cols[i]]) for i in heads]
    probs = [both_soft(x) for x in scores]
    query_t = [x.astype(BF) for x in probs]
    query_rows = [x.T for x in query_t]
    weights = [mm(query_rows[i], kb_ref[0, rows[i]]) for i in heads]
    weights = [jnp.where(causal, x, 0.0).astype(BF) for x in weights]
    norms = split(jnp.broadcast_to(pn_ref[0], (dim, group * feats)))
    ones = jnp.ones((dim, length), BF)
    den = [
        mm_nt(
            cat(weights[i], query_rows[i], query_rows[i]),
            cat(ones, norms[0][:, rows[i]], norms[1][:, rows[i]]),
        )
        for i in heads
    ]
    scaled = [(upstream[:, cols[i]] * (1.0 / den[i])).astype(BF) for i in heads]
    sums = [mm(query_t[i], scaled[i]) for i in heads]
    for i in heads:
        qp_ref[0, rows[i]] = probs[i]
        qr_ref[0, i] = query_rows[i]
        wt_ref[0, i] = weights[i]
    state_ref[...] = stack(*sums)


def attend_kernel(
    n, step, info, q_ref, qg_ref, c_ref, cg_ref, v_ref, vg_ref, kb_ref, qp_ref, qr_ref, wt_ref, pn_ref,
    near, far, near2, far2, att_ref, atg_ref, sn_ref, gq_ref, gk_ref,
):
    group, length, dim = qr_ref.shape[1:]
    feats = dim
    width = feats // 2
    own = length // 2
    heads = range(group)
    cols = [slice(i * dim, (i + 1) * dim) for i in heads]
    rows = [slice(i * feats, (i + 1) * feats) for i in heads]
    causal = causal_mask(info[2 * n], length)
    queries = tokens_of(q_ref, qg_ref)
    upstream = stack(c_ref[...].astype(F32), cg_ref[...])
    values = tokens_of(v_ref, vg_ref)
    high, low = split(before_of(info[2 * n + 1], step < n // 2, near, far, near2, far2))
    norm_wide = jnp.broadcast_to(column(pn_ref[0]), (group * feats, dim))
    norm_high, norm_low = split(norm_wide)
    norm_cols = three_lanes(norm_wide, "hhl")
    values_ones = cat(values, jnp.ones((length, dim), BF))
    query_rows = [qr_ref[0, i] for i in heads]
    both = [
        mm(
            cat(wt_ref[0, i], query_rows[i], query_rows[i]),
            stack(
                values_ones,
                cat(high[rows[i]], norm_high[rows[i]]),
                cat(low[rows[i]], norm_low[rows[i]]),
            ),
        )
        for i in heads
    ]
    numerator = [x[:, :dim] for x in both]
    inverse = [1.0 / x[:, dim:] for x in both]
    scaled_wide = [upstream[:, cols[i]] * inverse[i] for i in heads]
    scaled = [x.astype(BF) for x in scaled_wide]
    products = [cat(*split(-(scaled_wide[i] * inverse[i]) * numerator[i])) for i in heads]
    ones = jnp.ones((2 * dim, dim), BF)
    norm_grad = [mm(x, ones) for x in products]
    for i in heads:
        result = numerator[i] * inverse[i]
        att_ref[:, cols[i]] = result[:own].astype(BF)
        atg_ref[:, cols[i]] = result[own:]
        sn_ref[0, :, rows[i]] = jnp.sum(
            query_rows[i].astype(F32) * norm_grad[i], axis=0, keepdims=True
        )
    lanes = [three_lanes(x, "hlh") for x in norm_grad]
    lane = lax.broadcasted_iota(jnp.int32, (length, dim), 1)
    values_lanes = cat(values, jnp.where(lane < 2, 1.0, 0.0).astype(BF))
    mixed = [mm_nt(cat(scaled[i], lanes[i]), values_lanes) for i in heads]
    block = [jnp.where(causal, x, 0.0).astype(BF) for x in mixed]
    upstream_q = [
        mm_nt(
            cat(kb_ref[0, rows[i]], high[rows[i]], norm_cols[rows[i]], low[rows[i]]),
            cat(block[i], scaled[i], lanes[i], scaled[i]),
        )
        for i in heads
    ]
    probs = [qp_ref[0, r] for r in rows]
    back = [soft_back(probs[i], upstream_q[i]) for i in heads]
    for i in heads:
        gq_ref[0, i * width : (i + 1) * width] = mm(back[i], queries[:, cols[i]])
        gk_ref[0, rows[i]] = mm(probs[i].astype(BF), block[i])


def key_grad_kernel(
    n, step, info, k_ref, kg_ref, v_ref, vg_ref, kp_ref, gk_ref, sn_ref, near, far, near2, far2, out_ref
):
    rows, length = kp_ref.shape[1:]
    feats = k_ref.shape[1]
    values = tokens_of(v_ref, vg_ref)
    state = cat(*split(before_of(info[2 * n + 2], step < n // 2, near, far, near2, far2)))
    upstream = gk_ref[0] + mm_nt(state, cat(values, values))
    upstream = upstream + jnp.broadcast_to(column(sn_ref[0]), (rows, length))
    back = [
        soft_back(kp_ref[0, a : a + feats], upstream[a : a + feats])
        for a in range(0, rows, feats)
    ]
    out_ref[0] = mm(stack(*back), tokens_of(k_ref, kg_ref))


def attended_kernel(n, i, info, x_ref, o_ref):
    o_ref[...] = x_ref[...].astype(BF)


def out_kernel(info, *refs):
    out_ref = refs[-1]
    for i, ref in enumerate(refs[:-1]):
        out_ref[info[i]] = ref[...]


def core_swap(x):
    size = lax.axis_size("ctx")
    return lax.ppermute(x, "ctx", [(i, i ^ 1) for i in range(size)])


def chip_move(x, pairs):
    return lax.ppermute(x, "ctx", [(2 * a + c, 2 * b + c) for a, b in pairs for c in (0, 1)])


def after(values, *earlier):
    return lax.optimization_barrier((values, earlier))[0]


class Scan:
    def __init__(self, a, b, near, forward):
        self.chips = lax.axis_size("ctx") // 2
        chip = lax.axis_index("ctx") // 2
        self.forward = forward
        self.place = chip if forward else self.chips - 1 - chip
        self.a, self.b, self.payload = a, b, near

    def move(self, x, pairs):
        last = self.chips - 1
        turn = (lambda p: p) if self.forward else (lambda p: last - p)
        return chip_move(x, [(turn(p), turn(q)) for p, q in pairs])

    def first(self):
        if self.chips == 4:
            self.near = self.move(self.payload, [(0, 1), (1, 2), (2, 3)])
            self.far = self.move(self.b, [(0, 2)])

    def turn_around(self, *earlier):
        if self.chips == 4:
            a, b = after((self.a, self.b), *earlier) if earlier else (self.a, self.b)
            self.payload = jnp.where(
                self.place == 1,
                a + self.near,
                jnp.where(self.place == 2, b + self.near + self.far, b),
            )

    def second(self):
        if self.chips == 4:
            self.near2 = self.move(self.payload, [(0, 1), (1, 2), (2, 3)])
            self.far2 = self.move(self.payload, [(1, 3)])
            return self.near, self.far, self.near2, self.far2
        total = jnp.concatenate([self.a, self.b], axis=0)
        before = self.move(total, [(i, i + 1) for i in range(self.chips - 1)])
        step = 1
        while step < self.chips:
            pairs = [(i, i + step) for i in range(self.chips - step)]
            before = before + self.move(before, pairs)
            step *= 2
        rows = self.a.shape[0]
        zero = jnp.zeros_like(self.a)
        return before[:rows], zero, before[rows:], zero


def scan_norms(norm, chip, chips, forward, *earlier):
    base = jnp.zeros_like(norm)
    if earlier and chips <= 4:
        bits = range(1, chips)
        moved = [chip_move(norm, [(i, i ^ bit) for i in range(chips)]) for bit in bits]
        moved = after(moved, *earlier)
        for bit in bits:
            other = chip ^ bit
            base = base + jnp.where(other < chip if forward else other > chip, moved[bit - 1], 0.0)
        return base
    total = norm
    bit = 1
    while bit < chips:
        moved = chip_move(total, [(i, i ^ bit) for i in range(chips)])
        upper = (chip & bit) != 0 if forward else (chip & bit) == 0
        base = base + jnp.where(upper, moved, 0.0)
        total = total + moved
        bit *= 2
    return base


def sum_all(mine, chips, *earlier):
    dp = lax.axis_size("dp")
    share = mine.shape[0] // dp
    got = [
        lax.ppermute(mine[k * share : (k + 1) * share], "dp", [(i, i ^ k) for i in range(dp)])
        for k in range(1, dp)
    ]
    if earlier:
        got = after(got, *earlier)
    total = mine[:share]
    for piece in got:
        total = total + piece
    bit = 1
    while bit < chips:
        total = total + chip_move(total, [(i, i ^ bit) for i in range(chips)])
        bit *= 2
    pieces = [total] + [
        lax.ppermute(total, "dp", [(i, i ^ k) for i in range(dp)]) for k in range(1, dp)
    ]
    pieces = pieces + [core_swap(x) for x in pieces]
    return [x[i] for x in pieces for i in range(share)]


def shards(queries, key_tokens, value_tokens, cotangent, query_map, key_map):
    own = queries.shape[1]
    length = 2 * own
    head_count, dim, width = query_map.shape
    shared = key_tokens.shape[2] // dim
    group = head_count // shared
    feats = 2 * width
    n = shared // 2
    wide = group * feats
    queries = queries.reshape(own, head_count * dim)
    cotangent = cotangent.reshape(own, head_count * dim)
    keys = key_tokens.reshape(own, shared * dim)
    values = value_tokens.reshape(own, shared * dim)
    query_map = jnp.swapaxes(query_map, 1, 2)
    key_map = jnp.swapaxes(key_map, 1, 2)

    ctx = lax.axis_index("ctx")
    chips = lax.axis_size("ctx") // 2
    chip, core = ctx // 2, ctx % 2
    dp = lax.axis_size("dp")
    part = jnp.arange(n, dtype=jnp.int32) ^ (lax.axis_index("dp") * (n // dp))
    places = jnp.stack([core, chip, chips - 1 - chip]) if chips == 4 else jnp.stack([core, core * 0 + 3, core * 0 + 3])
    info = jnp.concatenate([part + n * core, part + n * (1 - core), places]).astype(jnp.int32)

    def spec(shape, index):
        return pl.BlockSpec(shape, index)

    def own_cols(cols):
        return spec((own, cols), lambda i, info: (0, info[i]))

    def other_cols(cols):
        return spec((own, cols), lambda i, info: (0, info[n + i]))

    def got_cols(cols):
        return spec((own, cols), lambda i, info: (0, i))

    def per_head(*shape):
        return spec((1,) + shape, lambda i, info: (i,) + (0,) * len(shape))

    def shape_of(*shape, dtype=F32):
        return jax.ShapeDtypeStruct((n,) + shape, dtype)

    def block(ref, spec, i, info):
        places = spec.index_map(i, info)
        return ref.at[
            tuple(
                pl.ds(p * size if isinstance(p, int) else pl.multiple_of(p * size, size), size)
                for p, size in zip(places, spec.block_shape)
            )
        ]

    def call(name, body, in_specs, out_specs, out_shape, aliases=None):
        in_specs = [x if isinstance(x, tuple) else (x, n) for x in in_specs]
        kinds = [x.dtype for x in out_shape]
        results = {}
        for (spec_, which, _), kind in zip(out_specs, kinds):
            results[which] = (spec_.block_shape, kind)
        results = [results[k] for k in range(len(results))]
        extra = len(aliases or {})

        def kernel(info, *refs):
            count = len(in_specs) + extra
            ins, outs = refs[: len(in_specs)], refs[count : count + len(out_specs)]
            rest = refs[count + len(out_specs) :]
            in_bufs, out_bufs = rest[: len(in_specs)], rest[len(in_specs) : -2]
            in_sem, out_sem = rest[-2:]

            def incoming(i):
                return [
                    pltpu.make_async_copy(block(ref, spec_, i, info), buf.at[i], in_sem.at[k, i])
                    for k, ((spec_, period), ref, buf) in enumerate(zip(in_specs, ins, in_bufs))
                    if i < period
                ]

            def outgoing(i, act):
                for k, ((spec_, which, when), ref) in enumerate(zip(out_specs, outs)):
                    here = when(i, info)
                    if here is False:
                        continue
                    copy = pltpu.make_async_copy(
                        out_bufs[which].at[i], block(ref, spec_, i, info), out_sem.at[k, i]
                    )
                    if here is True:
                        act(copy)
                    else:
                        pl.when(here)(lambda copy=copy: act(copy))

            for i in range(n):
                for copy in incoming(i):
                    copy.start()
            for i in range(n):
                for copy in incoming(i):
                    copy.wait()
                blocks = [buf.at[i % period] for (_, period), buf in zip(in_specs, in_bufs)]
                body(n, i, info, *blocks, *[buf.at[i] for buf in out_bufs])
                outgoing(i, lambda copy: copy.start())
            for i in range(n):
                outgoing(i, lambda copy: copy.wait())

        def run(*arrays):
            anywhere = pl.BlockSpec(memory_space=pl.ANY)
            buffers = [
                pltpu.VMEM((period,) + tuple(x.block_shape), y.dtype)
                for (x, period), y in zip(in_specs, arrays)
            ] + [pltpu.VMEM((n,) + tuple(shape), kind) for shape, kind in results]
            return pl.pallas_call(
                kernel,
                name=name,
                out_shape=[pltpu.HBM(x.shape, x.dtype) for x in out_shape],
                in_specs=[pl.BlockSpec(memory_space=pltpu.SMEM)] + [anywhere] * len(arrays),
                out_specs=[anywhere] * len(out_shape),
                scratch_shapes=buffers
                + [
                    pltpu.SemaphoreType.DMA((len(in_specs), n)),
                    pltpu.SemaphoreType.DMA((len(out_specs), n)),
                ],
                input_output_aliases=aliases or {},
                compiler_params=pltpu.CompilerParams(vmem_limit_bytes=VMEM_LIMIT),
            )(info, *[pltpu.with_memory_space_constraint(x, pltpu.HBM) for x in arrays])

        return run

    def always(i, info):
        return True

    def each(*specs):
        return [(x, k, always) for k, x in enumerate(specs)]

    one, four = dim, group * dim
    map_spec = spec((group, width, dim), lambda i, info: (info[i], 0, 0))
    row_spec, row = per_head(1, wide), shape_of(1, wide)
    flat_spec, flat = per_head(wide, length), shape_of(wide, length)
    half = n // 2
    half_state = jax.ShapeDtypeStruct((half * wide, dim), F32)
    moved_spec = (spec((wide, dim), lambda i, info: (i, 0)), half)
    half_spec = spec((wide, dim), lambda i, info: (i % half, 0))

    def states(which, place):
        return [
            (half_spec, which, lambda i, info: i < half),
            (half_spec, which, lambda i, info: i >= half),
            (half_spec, which, lambda i, info: (info[2 * n + place] == 1) == (i >= half)),
        ]

    got_keys = spec((own, one), lambda i, info: (0, info[i] % n))
    got_values = spec((own, one), lambda i, info: (1, info[i] % n))
    half_cols = n * one
    packed = jnp.concatenate(
        [lax.dynamic_slice_in_dim(x, (1 - core) * half_cols, half_cols, axis=1) for x in (keys, values)]
    )
    swapped = core_swap(packed.astype(F32))
    keys_got = values_got = swapped

    wide_flat = jax.ShapeDtypeStruct((own, n * four), F32)
    key_probs, key_features, norm, a, b, near, *packed = call(
        "key_features",
        key_kernel,
        [own_cols(one), got_keys, own_cols(one), got_values, map_spec] + [other_cols(four)] * 2,
        each(flat_spec, flat_spec, row_spec)
        + states(3, 1)
        + [(got_cols(four), 4, always), (got_cols(four), 5, always)],
        [flat, shape_of(wide, length, dtype=BF), row] + [half_state] * 3 + [wide_flat] * 2,
    )(keys, keys_got, values, values_got, key_map, queries, cotangent)
    queries_got, cotangent_got = [core_swap(x) for x in packed]
    prefix_norm = scan_norms(norm, chip, chips, True)
    prefix = Scan(*after((a, b, near), prefix_norm), True)
    prefix.first()

    rows_spec = per_head(group, length, dim)
    rows_bf = shape_of(group, length, dim, dtype=BF)
    query_probs, query_rows, weights, a, b, near = call(
        "query_features",
        query_kernel,
        [own_cols(four), got_cols(four)] * 2 + [map_spec, flat_spec, row_spec],
        each(flat_spec, rows_spec, per_head(group, length, length)) + states(3, 2),
        [flat, rows_bf, shape_of(group, length, length, dtype=BF)] + [half_state] * 3,
    )(queries, queries_got, cotangent, cotangent_got, query_map, key_features, prefix_norm)
    suffix = Scan(a, b, near, False)
    suffix.first()
    prefix.turn_around(near)
    before = prefix.second()
    suffix.turn_around()
    before = after(before, suffix.payload)
    later = suffix.second()

    grad_spec, grad = per_head(group * width, dim), shape_of(group * width, dim)
    attended, attended_got, norm, query_part, key_up = call(
        "attend",
        attend_kernel,
        [own_cols(four), got_cols(four)] * 2
        + [own_cols(one), got_values, flat_spec, flat_spec, rows_spec]
        + [per_head(group, length, length), row_spec]
        + [moved_spec] * 4,
        each(own_cols(four), got_cols(four), row_spec, grad_spec, flat_spec),
        [
            jax.ShapeDtypeStruct((own, head_count * dim), BF),
            jax.ShapeDtypeStruct((own, n * four), F32),
            row,
            grad,
            flat,
        ],
    )(
        queries, queries_got, cotangent, cotangent_got, values, values_got, key_features,
        query_probs, query_rows, weights, prefix_norm, *before,
    )
    suffix_norm = scan_norms(norm, chip, chips, False, query_part)
    query_part = after(query_part, suffix_norm)
    (key_part,) = call(
        "key_grads",
        key_grad_kernel,
        [own_cols(one), got_keys, own_cols(one), got_values]
        + [flat_spec, flat_spec, row_spec]
        + [moved_spec] * 4,
        each(grad_spec),
        [grad],
    )(keys, keys_got, values, values_got, key_probs, key_up, suffix_norm, *later)
    (attended,) = call(
        "attended",
        attended_kernel,
        [got_cols(four)],
        each(other_cols(four)),
        [jax.ShapeDtypeStruct((own, head_count * dim), BF)],
        aliases={2: 0},
    )(core_swap(after(attended_got, *later)), attended)

    def finish(name, mine, *earlier):
        pieces = sum_all(mine, chips, *earlier)
        whole = pl.BlockSpec(memory_space=pltpu.VMEM)
        natural = pl.pallas_call(
            out_kernel,
            name=name,
            out_shape=jax.ShapeDtypeStruct((shared, group * width, dim), F32),
            in_specs=[pl.BlockSpec(memory_space=pltpu.SMEM)] + [whole] * shared,
            out_specs=whole,
            compiler_params=pltpu.CompilerParams(vmem_limit_bytes=VMEM_LIMIT),
        )(info, *pieces)
        return jnp.swapaxes(natural.reshape(head_count, width, dim), 1, 2)

    query_grad = finish("query_out", query_part, key_part)
    key_grad = finish("key_out", key_part, attended)
    return attended.reshape(1, own, head_count * dim), query_grad, key_grad


def solution(mesh):
    in_specs = (
        P("dp", "ctx", None),
        P("dp", "ctx", None),
        P("dp", "ctx", None),
        P("dp", "ctx", None),
        P(),
        P(),
    )
    out_specs = (P("dp", "ctx", None), P(), P())
    return jax.shard_map(shards, mesh=mesh, in_specs=in_specs, out_specs=out_specs, check_vma=False)
```

```python
import jax
import jax.numpy as jnp
from jax import lax
from jax.experimental import pallas as pl
from jax.experimental.pallas import tpu as pltpu
from jax.sharding import PartitionSpec as P

BF = jnp.bfloat16
F32 = jnp.float32
VMEM_LIMIT = 40 * 1024 * 1024


def mm(a, b):
    return jnp.dot(a, b, preferred_element_type=F32)


def mm_nt(a, b):
    return lax.dot_general(a, b, (((1,), (1,)), ((), ())), preferred_element_type=F32)


def split(x):
    high = x.astype(BF)
    return high, (x - high.astype(F32)).astype(BF)


def cat(*pieces):
    return jnp.concatenate(pieces, axis=1)


def stack(*pieces):
    return jnp.concatenate(pieces, axis=0)


def soft(scores):
    top = jnp.max(scores, axis=0, keepdims=True)
    raised = jnp.exp(scores - top)
    return raised * (1.0 / jnp.sum(raised, axis=0, keepdims=True))


def both_soft(scores):
    return stack(soft(scores), soft(-scores))


def soft_back(probs, upstream):
    half = probs.shape[0] // 2
    p, n = probs[:half], probs[half:]
    gp, gn = upstream[:half], upstream[half:]
    result = p * (gp - jnp.sum(p * gp, axis=0, keepdims=True))
    result = result - n * (gn - jnp.sum(n * gn, axis=0, keepdims=True))
    return result.astype(BF)


def causal_mask(core, tokens):
    own = tokens // 2
    shift = core * own
    rows = lax.broadcasted_iota(jnp.int32, (tokens, tokens), 0)
    cols = lax.broadcasted_iota(jnp.int32, (tokens, tokens), 1)
    rows = rows + jnp.where(rows < own, shift, -shift)
    cols = cols + jnp.where(cols < own, shift, -shift)
    return rows >= cols


def column(row):
    return jnp.broadcast_to(row, (8, row.shape[1])).T[:, :1]


def three_lanes(wide, order):
    lane = lax.broadcasted_iota(jnp.int32, wide.shape, 1)
    high = wide.astype(BF).astype(F32)
    parts = {"h": high, "l": wide - high}
    result = jnp.where(lane == 2, parts[order[2]], 0.0)
    result = jnp.where(lane == 1, parts[order[1]], result)
    return jnp.where(lane == 0, parts[order[0]], result).astype(BF)


def tokens_of(own_ref, got_ref):
    return stack(own_ref[...], got_ref[...].astype(BF))


def before_of(place, first, near, far, near2, far2):
    if first:
        return jnp.where(place == 2, near2[...], near[...] + far2[...])
    return jnp.where(place == 2, near[...] + far[...], near2[...])


def key_kernel(
    n, i, info, k_ref, kg_ref, v_ref, vg_ref, w_ref, q_ref, c_ref,
    kp_ref, kb_ref, norm_ref, state_ref, qw_ref, cw_ref,
):
    group, width, dim = w_ref.shape
    keys = tokens_of(k_ref, kg_ref)
    values = tokens_of(v_ref, vg_ref)
    scores = mm_nt(w_ref[...].reshape(group * width, dim), keys)
    probs = stack(*[both_soft(scores[a : a + width]) for a in range(0, group * width, width)])
    features = probs.astype(BF)
    kp_ref[0] = probs
    kb_ref[0] = features
    norm_ref[0] = mm_nt(jnp.ones((16, keys.shape[0]), BF), features)[:1]
    state_ref[...] = mm(features, values)
    qw_ref[...] = q_ref[...].astype(F32)
    cw_ref[...] = c_ref[...].astype(F32)


def query_kernel(
    n, step, info, q_ref, qg_ref, c_ref, cg_ref, w_ref, kb_ref, pn_ref,
    qp_ref, qr_ref, wt_ref, state_ref,
):
    group, width, dim = w_ref.shape
    feats = 2 * width
    queries = tokens_of(q_ref, qg_ref)
    upstream = stack(c_ref[...].astype(F32), cg_ref[...])
    length = queries.shape[0]
    causal = causal_mask(info[2 * n], length)
    heads = range(group)
    cols = [slice(i * dim, (i + 1) * dim) for i in heads]
    rows = [slice(i * feats, (i + 1) * feats) for i in heads]
    scores = [mm_nt(w_ref[i], queries[:, cols[i]]) for i in heads]
    probs = [both_soft(x) for x in scores]
    query_t = [x.astype(BF) for x in probs]
    query_rows = [x.T for x in query_t]
    weights = [mm(query_rows[i], kb_ref[0, rows[i]]) for i in heads]
    weights = [jnp.where(causal, x, 0.0).astype(BF) for x in weights]
    norms = split(jnp.broadcast_to(pn_ref[0], (dim, group * feats)))
    ones = jnp.ones((dim, length), BF)
    den = [
        mm_nt(
            cat(weights[i], query_rows[i], query_rows[i]),
            cat(ones, norms[0][:, rows[i]], norms[1][:, rows[i]]),
        )
        for i in heads
    ]
    scaled = [(upstream[:, cols[i]] * (1.0 / den[i])).astype(BF) for i in heads]
    sums = [mm(query_t[i], scaled[i]) for i in heads]
    for i in heads:
        qp_ref[0, rows[i]] = probs[i]
        qr_ref[0, i] = query_rows[i]
        wt_ref[0, i] = weights[i]
    state_ref[...] = stack(*sums)


def attend_kernel(
    n, step, info, q_ref, qg_ref, c_ref, cg_ref, v_ref, vg_ref, kb_ref, qp_ref, qr_ref, wt_ref, pn_ref,
    near, far, near2, far2, att_ref, atg_ref, sn_ref, gk_ref, gq_ref,
):
    group, length, dim = qr_ref.shape[1:]
    feats = dim
    width = feats // 2
    own = length // 2
    heads = range(group)
    cols = [slice(i * dim, (i + 1) * dim) for i in heads]
    rows = [slice(i * feats, (i + 1) * feats) for i in heads]
    causal = causal_mask(info[2 * n], length)
    queries = tokens_of(q_ref, qg_ref)
    upstream = stack(c_ref[...].astype(F32), cg_ref[...])
    values = tokens_of(v_ref, vg_ref)
    high, low = split(before_of(info[2 * n + 1], step < n // 2, near, far, near2, far2))
    norm_wide = jnp.broadcast_to(column(pn_ref[0]), (group * feats, dim))
    norm_high, norm_low = split(norm_wide)
    norm_cols = three_lanes(norm_wide, "hhl")
    values_ones = cat(values, jnp.ones((length, dim), BF))
    query_rows = [qr_ref[0, i] for i in heads]
    both = [
        mm(
            cat(wt_ref[0, i], query_rows[i], query_rows[i]),
            stack(
                values_ones,
                cat(high[rows[i]], norm_high[rows[i]]),
                cat(low[rows[i]], norm_low[rows[i]]),
            ),
        )
        for i in heads
    ]
    numerator = [x[:, :dim] for x in both]
    inverse = [1.0 / x[:, dim:] for x in both]
    scaled_wide = [upstream[:, cols[i]] * inverse[i] for i in heads]
    scaled = [x.astype(BF) for x in scaled_wide]
    products = [cat(*split(-(scaled_wide[i] * inverse[i]) * numerator[i])) for i in heads]
    ones = jnp.ones((2 * dim, dim), BF)
    norm_grad = [mm(x, ones) for x in products]
    for i in heads:
        result = numerator[i] * inverse[i]
        att_ref[:, cols[i]] = result[:own].astype(BF)
        atg_ref[:, cols[i]] = result[own:]
        sn_ref[0, :, rows[i]] = jnp.sum(
            query_rows[i].astype(F32) * norm_grad[i], axis=0, keepdims=True
        )
    lanes = [three_lanes(x, "hlh") for x in norm_grad]
    lane = lax.broadcasted_iota(jnp.int32, (length, dim), 1)
    values_lanes = cat(values, jnp.where(lane < 2, 1.0, 0.0).astype(BF))
    mixed = [mm_nt(cat(scaled[i], lanes[i]), values_lanes) for i in heads]
    block = [jnp.where(causal, x, 0.0).astype(BF) for x in mixed]
    upstream_q = [
        mm_nt(
            cat(kb_ref[0, rows[i]], high[rows[i]], norm_cols[rows[i]], low[rows[i]]),
            cat(block[i], scaled[i], lanes[i], scaled[i]),
        )
        for i in heads
    ]
    probs = [qp_ref[0, r] for r in rows]
    back = [soft_back(probs[i], upstream_q[i]) for i in heads]
    for i in heads:
        gq_ref[i * width : (i + 1) * width] = mm(back[i], queries[:, cols[i]])
        gk_ref[0, rows[i]] = mm(probs[i].astype(BF), block[i])


def key_grad_kernel(
    n, step, info, k_ref, kg_ref, v_ref, vg_ref, kp_ref, gk_ref, sn_ref, near, far, near2, far2, out_ref
):
    rows, length = kp_ref.shape[1:]
    feats = k_ref.shape[1]
    values = tokens_of(v_ref, vg_ref)
    state = cat(*split(before_of(info[2 * n + 2], step < n // 2, near, far, near2, far2)))
    upstream = gk_ref[0] + mm_nt(state, cat(values, values))
    upstream = upstream + jnp.broadcast_to(column(sn_ref[0]), (rows, length))
    back = [
        soft_back(kp_ref[0, a : a + feats], upstream[a : a + feats])
        for a in range(0, rows, feats)
    ]
    out_ref[...] = mm(stack(*back), tokens_of(k_ref, kg_ref))


def attended_kernel(n, i, info, x_ref, o_ref):
    o_ref[...] = x_ref[...].astype(BF)


def out_kernel(info, *refs):
    count = len(refs) // 2 - 1
    for out_ref, pieces in zip(refs[-2:], (refs[:count], refs[count:-2])):
        for i, ref in enumerate(pieces):
            out_ref[info[i]] = ref[...]


def core_swap(x):
    size = lax.axis_size("ctx")
    return lax.ppermute(x, "ctx", [(i, i ^ 1) for i in range(size)])


def chip_move(x, pairs):
    return lax.ppermute(x, "ctx", [(2 * a + c, 2 * b + c) for a, b in pairs for c in (0, 1)])


def after(values, *earlier):
    return lax.optimization_barrier((values, earlier))[0]


class Scan:
    def __init__(self, a, b, near, forward):
        self.chips = lax.axis_size("ctx") // 2
        chip = lax.axis_index("ctx") // 2
        self.forward = forward
        self.place = chip if forward else self.chips - 1 - chip
        self.a, self.b, self.payload = a, b, near

    def move(self, x, pairs):
        last = self.chips - 1
        turn = (lambda p: p) if self.forward else (lambda p: last - p)
        return chip_move(x, [(turn(p), turn(q)) for p, q in pairs])

    def first(self):
        if self.chips == 4:
            self.near = self.move(self.payload, [(0, 1), (1, 2), (2, 3)])
            self.far = self.move(self.b, [(0, 2)])

    def turn_around(self, *earlier):
        if self.chips == 4:
            a, b = after((self.a, self.b), *earlier) if earlier else (self.a, self.b)
            self.payload = jnp.where(
                self.place == 1,
                a + self.near,
                jnp.where(self.place == 2, b + self.near + self.far, b),
            )

    def second(self):
        if self.chips == 4:
            self.near2 = self.move(self.payload, [(0, 1), (1, 2), (2, 3)])
            self.far2 = self.move(self.payload, [(1, 3)])
            return self.near, self.far, self.near2, self.far2
        total = jnp.concatenate([self.a, self.b], axis=0)
        before = self.move(total, [(i, i + 1) for i in range(self.chips - 1)])
        step = 1
        while step < self.chips:
            pairs = [(i, i + step) for i in range(self.chips - step)]
            before = before + self.move(before, pairs)
            step *= 2
        rows = self.a.shape[0]
        zero = jnp.zeros_like(self.a)
        return before[:rows], zero, before[rows:], zero


def scan_norms(norm, chip, chips, forward, *earlier):
    base = jnp.zeros_like(norm)
    if earlier and chips <= 4:
        bits = range(1, chips)
        moved = [chip_move(norm, [(i, i ^ bit) for i in range(chips)]) for bit in bits]
        moved = after(moved, *earlier)
        for bit in bits:
            other = chip ^ bit
            base = base + jnp.where(other < chip if forward else other > chip, moved[bit - 1], 0.0)
        return base
    total = norm
    bit = 1
    while bit < chips:
        moved = chip_move(total, [(i, i ^ bit) for i in range(chips)])
        upper = (chip & bit) != 0 if forward else (chip & bit) == 0
        base = base + jnp.where(upper, moved, 0.0)
        total = total + moved
        bit *= 2
    return base


def sum_all(mine, chips, *earlier):
    dp = lax.axis_size("dp")
    share = len(mine) // dp
    rows = mine[0].shape[0]
    blocks = [
        jnp.concatenate(mine[k * share : (k + 1) * share]) if share > 1 else mine[k]
        for k in range(dp)
    ]
    got = [lax.ppermute(blocks[k], "dp", [(i, i ^ k) for i in range(dp)]) for k in range(1, dp)]
    if earlier:
        got = after(got, *earlier)
    total = blocks[0]
    for piece in got:
        total = total + piece
    bit = 1
    while bit < chips:
        total = total + chip_move(total, [(i, i ^ bit) for i in range(chips)])
        bit *= 2
    pieces = [total] + [
        lax.ppermute(total, "dp", [(i, i ^ k) for i in range(dp)]) for k in range(1, dp)
    ]
    pieces = pieces + [core_swap(x) for x in pieces]
    return [x[a : a + rows] if share > 1 else x for x in pieces for a in range(0, share * rows, rows)]


def shards(queries, key_tokens, value_tokens, cotangent, query_map, key_map):
    own = queries.shape[1]
    length = 2 * own
    head_count, dim, width = query_map.shape
    shared = key_tokens.shape[2] // dim
    group = head_count // shared
    feats = 2 * width
    n = shared // 2
    wide = group * feats
    queries = queries.reshape(own, head_count * dim)
    cotangent = cotangent.reshape(own, head_count * dim)
    keys = key_tokens.reshape(own, shared * dim)
    values = value_tokens.reshape(own, shared * dim)
    query_map = jnp.swapaxes(query_map, 1, 2)
    key_map = jnp.swapaxes(key_map, 1, 2)

    ctx = lax.axis_index("ctx")
    chips = lax.axis_size("ctx") // 2
    chip, core = ctx // 2, ctx % 2
    dp = lax.axis_size("dp")
    part = jnp.arange(n, dtype=jnp.int32) ^ (lax.axis_index("dp") * (n // dp))
    places = jnp.stack([core, chip, chips - 1 - chip]) if chips == 4 else jnp.stack([core, core * 0 + 3, core * 0 + 3])
    info = jnp.concatenate([part + n * core, part + n * (1 - core), places]).astype(jnp.int32)

    def spec(shape, index):
        return pl.BlockSpec(shape, index)

    def own_cols(cols):
        return spec((own, cols), lambda i, info: (0, info[i]))

    def other_cols(cols):
        return spec((own, cols), lambda i, info: (0, info[n + i]))

    def got_cols(cols):
        return spec((own, cols), lambda i, info: (0, i))

    def per_head(*shape):
        return spec((1,) + shape, lambda i, info: (i,) + (0,) * len(shape))

    def shape_of(*shape, dtype=F32):
        return jax.ShapeDtypeStruct((n,) + shape, dtype)

    def block(ref, spec, i, info):
        places = spec.index_map(i, info)
        return ref.at[
            tuple(
                pl.ds(p * size if isinstance(p, int) else pl.multiple_of(p * size, size), size)
                for p, size in zip(places, spec.block_shape)
            )
        ]

    in_hbm = [queries, cotangent, keys, values, query_map, key_map]

    def pinned(x):
        if any(x is y for y in in_hbm):
            return pltpu.with_memory_space_constraint(x, pltpu.HBM)
        return x

    def call(name, body, in_specs, out_specs, out_shape, aliases=None):
        in_specs = [x if isinstance(x, tuple) else (x, n) for x in in_specs]
        kinds = [x.dtype for x in out_shape]
        results = {}
        for (spec_, which, _), kind in zip(out_specs, kinds):
            results[which] = (spec_.block_shape, kind)
        results = [results[k] for k in range(len(results))]
        extra = len(aliases or {})

        def kernel(info, *refs):
            count = len(in_specs) + extra
            ins, outs = refs[: len(in_specs)], refs[count : count + len(out_specs)]
            rest = refs[count + len(out_specs) :]
            in_bufs, out_bufs = rest[: len(in_specs)], rest[len(in_specs) : -2]
            in_sem, out_sem = rest[-2:]

            def incoming(i):
                return [
                    pltpu.make_async_copy(block(ref, spec_, i, info), buf.at[i], in_sem.at[k, i])
                    for k, ((spec_, period), ref, buf) in enumerate(zip(in_specs, ins, in_bufs))
                    if i < period
                ]

            def outgoing(i, act):
                for k, ((spec_, which, when), ref) in enumerate(zip(out_specs, outs)):
                    here = when(i, info)
                    if here is False:
                        continue
                    copy = pltpu.make_async_copy(
                        out_bufs[which].at[i], block(ref, spec_, i, info), out_sem.at[k, i]
                    )
                    if here is True:
                        act(copy)
                    else:
                        pl.when(here)(lambda copy=copy: act(copy))

            for i in range(n):
                for copy in incoming(i):
                    copy.start()
            for i in range(n):
                for copy in incoming(i):
                    copy.wait()
                blocks = [buf.at[i % period] for (_, period), buf in zip(in_specs, in_bufs)]
                body(n, i, info, *blocks, *[buf.at[i] for buf in out_bufs])
                outgoing(i, lambda copy: copy.start())
            for i in range(n):
                outgoing(i, lambda copy: copy.wait())

        def run(*arrays):
            anywhere = pl.BlockSpec(memory_space=pl.ANY)
            buffers = [
                pltpu.VMEM((period,) + tuple(x.block_shape), y.dtype)
                for (x, period), y in zip(in_specs, arrays)
            ] + [pltpu.VMEM((n,) + tuple(shape), kind) for shape, kind in results]
            return pl.pallas_call(
                kernel,
                name=name,
                out_shape=[pltpu.HBM(x.shape, x.dtype) for x in out_shape],
                in_specs=[pl.BlockSpec(memory_space=pltpu.SMEM)] + [anywhere] * len(arrays),
                out_specs=[anywhere] * len(out_shape),
                scratch_shapes=buffers
                + [
                    pltpu.SemaphoreType.DMA((len(in_specs), n)),
                    pltpu.SemaphoreType.DMA((len(out_specs), n)),
                ],
                input_output_aliases=aliases or {},
                compiler_params=pltpu.CompilerParams(vmem_limit_bytes=VMEM_LIMIT),
            )(info, *[pinned(x) for x in arrays])

        def remember(*arrays):
            made = run(*arrays)
            in_hbm.extend(made)
            return made

        return remember

    def spread(which):
        whole = spec((group * width, dim), lambda i, info: (0, 0))
        return [(whole, which, lambda i, info, k=k: i == k) for k in range(n)]

    def always(i, info):
        return True

    def each(*specs):
        return [(x, k, always) for k, x in enumerate(specs)]

    one, four = dim, group * dim
    map_spec = spec((group, width, dim), lambda i, info: (info[i], 0, 0))
    row_spec, row = per_head(1, wide), shape_of(1, wide)
    flat_spec, flat = per_head(wide, length), shape_of(wide, length)
    half = n // 2
    half_state = jax.ShapeDtypeStruct((half * wide, dim), F32)
    moved_spec = (spec((wide, dim), lambda i, info: (i, 0)), half)
    half_spec = spec((wide, dim), lambda i, info: (i % half, 0))

    def states(which, place):
        return [
            (half_spec, which, lambda i, info: i < half),
            (half_spec, which, lambda i, info: i >= half),
            (half_spec, which, lambda i, info: (info[2 * n + place] == 1) == (i >= half)),
        ]

    got_keys = spec((own, one), lambda i, info: (0, info[i] % n))
    got_values = spec((own, one), lambda i, info: (1, info[i] % n))
    half_cols = n * one
    packed = jnp.concatenate(
        [lax.dynamic_slice_in_dim(x, (1 - core) * half_cols, half_cols, axis=1) for x in (keys, values)]
    )
    swapped = core_swap(packed.astype(F32))
    keys_got = values_got = swapped

    wide_flat = jax.ShapeDtypeStruct((own, n * four), F32)
    key_probs, key_features, norm, a, b, near, *packed = call(
        "key_features",
        key_kernel,
        [own_cols(one), got_keys, own_cols(one), got_values, map_spec] + [other_cols(four)] * 2,
        each(flat_spec, flat_spec, row_spec)
        + states(3, 1)
        + [(got_cols(four), 4, always), (got_cols(four), 5, always)],
        [flat, shape_of(wide, length, dtype=BF), row] + [half_state] * 3 + [wide_flat] * 2,
    )(keys, keys_got, values, values_got, key_map, queries, cotangent)
    queries_got, cotangent_got = [core_swap(x) for x in packed]
    prefix_norm = scan_norms(norm, chip, chips, True)
    prefix = Scan(*after((a, b, near), prefix_norm), True)
    prefix.first()

    rows_spec = per_head(group, length, dim)
    rows_bf = shape_of(group, length, dim, dtype=BF)
    query_probs, query_rows, weights, a, b, near = call(
        "query_features",
        query_kernel,
        [own_cols(four), got_cols(four)] * 2 + [map_spec, flat_spec, row_spec],
        each(flat_spec, rows_spec, per_head(group, length, length)) + states(3, 2),
        [flat, rows_bf, shape_of(group, length, length, dtype=BF)] + [half_state] * 3,
    )(queries, queries_got, cotangent, cotangent_got, query_map, key_features, prefix_norm)
    suffix = Scan(a, b, near, False)
    suffix.first()
    prefix.turn_around(near)
    before = prefix.second()
    suffix.turn_around()
    before = after(before, suffix.payload)
    later = suffix.second()

    grad = jax.ShapeDtypeStruct((group * width, dim), F32)
    attended, attended_got, norm, key_up, *query_part = call(
        "attend",
        attend_kernel,
        [own_cols(four), got_cols(four)] * 2
        + [own_cols(one), got_values, flat_spec, flat_spec, rows_spec]
        + [per_head(group, length, length), row_spec]
        + [moved_spec] * 4,
        each(own_cols(four), got_cols(four), row_spec, flat_spec) + spread(4),
        [
            jax.ShapeDtypeStruct((own, head_count * dim), BF),
            jax.ShapeDtypeStruct((own, n * four), F32),
            row,
            flat,
        ]
        + [grad] * n,
    )(
        queries, queries_got, cotangent, cotangent_got, values, values_got, key_features,
        query_probs, query_rows, weights, prefix_norm, *before,
    )
    suffix_norm = scan_norms(norm, chip, chips, False, *query_part)
    key_part = call(
        "key_grads",
        key_grad_kernel,
        [own_cols(one), got_keys, own_cols(one), got_values]
        + [flat_spec, flat_spec, row_spec]
        + [moved_spec] * 4,
        spread(0),
        [grad] * n,
    )(keys, keys_got, values, values_got, key_probs, key_up, suffix_norm, *later)
    (attended,) = call(
        "attended",
        attended_kernel,
        [got_cols(four)],
        each(other_cols(four)),
        [jax.ShapeDtypeStruct((own, head_count * dim), BF)],
        aliases={2: 0},
    )(core_swap(after(attended_got, suffix_norm, *later)), attended)

    key_pieces = sum_all(key_part, chips, attended)
    query_pieces = sum_all(after(query_part, suffix_norm), chips, *key_part)
    whole = pl.BlockSpec(memory_space=pltpu.VMEM)
    sums = pl.pallas_call(
        out_kernel,
        name="sums_out",
        out_shape=[jax.ShapeDtypeStruct((shared, group * width, dim), F32)] * 2,
        in_specs=[pl.BlockSpec(memory_space=pltpu.SMEM)] + [whole] * (2 * shared),
        out_specs=[whole] * 2,
        compiler_params=pltpu.CompilerParams(vmem_limit_bytes=VMEM_LIMIT),
    )(info, *query_pieces, *key_pieces)
    query_grad, key_grad = [
        jnp.swapaxes(x.reshape(head_count, width, dim), 1, 2) for x in sums
    ]
    return attended.reshape(1, own, head_count * dim), query_grad, key_grad


def solution(mesh):
    in_specs = (
        P("dp", "ctx", None),
        P("dp", "ctx", None),
        P("dp", "ctx", None),
        P("dp", "ctx", None),
        P(),
        P(),
    )
    out_specs = (P("dp", "ctx", None), P(), P())
    return jax.shard_map(shards, mesh=mesh, in_specs=in_specs, out_specs=out_specs, check_vma=False)
```

```python
import jax
import jax.numpy as jnp
from jax import lax
from jax.experimental import pallas as pl
from jax.experimental.pallas import tpu as pltpu
from jax.sharding import PartitionSpec as P

BF = jnp.bfloat16
F32 = jnp.float32
VMEM_LIMIT = 40 * 1024 * 1024


def mm(a, b):
    return jnp.dot(a, b, preferred_element_type=F32)


def mm_nt(a, b):
    return lax.dot_general(a, b, (((1,), (1,)), ((), ())), preferred_element_type=F32)


def split(x):
    high = x.astype(BF)
    return high, (x - high.astype(F32)).astype(BF)


def cat(*pieces):
    return jnp.concatenate(pieces, axis=1)


def stack(*pieces):
    return jnp.concatenate(pieces, axis=0)


def soft(scores):
    top = jnp.max(scores, axis=0, keepdims=True)
    raised = jnp.exp(scores - top)
    return raised * (1.0 / jnp.sum(raised, axis=0, keepdims=True))


def both_soft(scores):
    return stack(soft(scores), soft(-scores))


def soft_back(probs, upstream):
    half = probs.shape[0] // 2
    p, n = probs[:half], probs[half:]
    gp, gn = upstream[:half], upstream[half:]
    result = p * (gp - jnp.sum(p * gp, axis=0, keepdims=True))
    result = result - n * (gn - jnp.sum(n * gn, axis=0, keepdims=True))
    return result.astype(BF)


def causal_mask(core, tokens):
    own = tokens // 2
    shift = core * own
    rows = lax.broadcasted_iota(jnp.int32, (tokens, tokens), 0)
    cols = lax.broadcasted_iota(jnp.int32, (tokens, tokens), 1)
    rows = rows + jnp.where(rows < own, shift, -shift)
    cols = cols + jnp.where(cols < own, shift, -shift)
    return rows >= cols


def column(row):
    return jnp.broadcast_to(row, (8, row.shape[1])).T[:, :1]


def three_lanes(wide, order):
    lane = lax.broadcasted_iota(jnp.int32, wide.shape, 1)
    high = wide.astype(BF).astype(F32)
    parts = {"h": high, "l": wide - high}
    result = jnp.where(lane == 2, parts[order[2]], 0.0)
    result = jnp.where(lane == 1, parts[order[1]], result)
    return jnp.where(lane == 0, parts[order[0]], result).astype(BF)


def tokens_of(own_ref, got_ref):
    return stack(own_ref[...], got_ref[...].astype(BF))


def before_of(place, first, near, far, passed, passed_far, last):
    if first:
        return jnp.where(place == 2, passed[...], near[...] + passed_far[...])
    return jnp.where(place == 2, near[...] + far[...], last[...])


def key_kernel(
    n, i, info, k_ref, kg_ref, v_ref, vg_ref, w_ref, q_ref, c_ref,
    kp_ref, kb_ref, norm_ref, state_ref, qw_ref, cw_ref,
):
    group, width, dim = w_ref.shape
    keys = tokens_of(k_ref, kg_ref)
    values = tokens_of(v_ref, vg_ref)
    scores = mm_nt(w_ref[...].reshape(group * width, dim), keys)
    probs = stack(*[both_soft(scores[a : a + width]) for a in range(0, group * width, width)])
    features = probs.astype(BF)
    kp_ref[0] = probs
    kb_ref[0] = features
    norm_ref[0] = mm_nt(jnp.ones((16, keys.shape[0]), BF), features)[:1]
    state_ref[...] = mm(features, values)
    qw_ref[...] = q_ref[...].astype(F32)
    cw_ref[...] = c_ref[...].astype(F32)


def query_kernel(
    n, step, info, q_ref, qg_ref, c_ref, cg_ref, w_ref, kb_ref, pn_ref,
    qp_ref, qr_ref, wt_ref, state_ref,
):
    group, width, dim = w_ref.shape
    feats = 2 * width
    queries = tokens_of(q_ref, qg_ref)
    upstream = stack(c_ref[...].astype(F32), cg_ref[...])
    length = queries.shape[0]
    causal = causal_mask(info[2 * n], length)
    heads = range(group)
    cols = [slice(i * dim, (i + 1) * dim) for i in heads]
    rows = [slice(i * feats, (i + 1) * feats) for i in heads]
    scores = [mm_nt(w_ref[i], queries[:, cols[i]]) for i in heads]
    probs = [both_soft(x) for x in scores]
    query_t = [x.astype(BF) for x in probs]
    query_rows = [x.T for x in query_t]
    weights = [mm(query_rows[i], kb_ref[0, rows[i]]) for i in heads]
    weights = [jnp.where(causal, x, 0.0).astype(BF) for x in weights]
    norms = split(jnp.broadcast_to(pn_ref[0], (dim, group * feats)))
    ones = jnp.ones((dim, length), BF)
    den = [
        mm_nt(
            cat(weights[i], query_rows[i], query_rows[i]),
            cat(ones, norms[0][:, rows[i]], norms[1][:, rows[i]]),
        )
        for i in heads
    ]
    scaled = [(upstream[:, cols[i]] * (1.0 / den[i])).astype(BF) for i in heads]
    sums = [mm(query_t[i], scaled[i]) for i in heads]
    for i in heads:
        qp_ref[0, rows[i]] = probs[i]
        qr_ref[0, i] = query_rows[i]
        wt_ref[0, i] = weights[i]
    state_ref[...] = stack(*sums)


def attend_kernel(
    n, step, info, q_ref, qg_ref, c_ref, cg_ref, v_ref, vg_ref, kb_ref, qp_ref, qr_ref, wt_ref, pn_ref,
    near, far, passed, passed_far, last, att_ref, atg_ref, sn_ref, gk_ref, gq_ref,
):
    group, length, dim = qr_ref.shape[1:]
    feats = dim
    width = feats // 2
    own = length // 2
    heads = range(group)
    cols = [slice(i * dim, (i + 1) * dim) for i in heads]
    rows = [slice(i * feats, (i + 1) * feats) for i in heads]
    causal = causal_mask(info[2 * n], length)
    queries = tokens_of(q_ref, qg_ref)
    upstream = stack(c_ref[...].astype(F32), cg_ref[...])
    values = tokens_of(v_ref, vg_ref)
    high, low = split(before_of(info[2 * n + 1], step < n // 2, near, far, passed, passed_far, last))
    norm_wide = jnp.broadcast_to(column(pn_ref[0]), (group * feats, dim))
    norm_high, norm_low = split(norm_wide)
    norm_cols = three_lanes(norm_wide, "hhl")
    values_ones = cat(values, jnp.ones((length, dim), BF))
    query_rows = [qr_ref[0, i] for i in heads]
    both = [
        mm(
            cat(wt_ref[0, i], query_rows[i], query_rows[i]),
            stack(
                values_ones,
                cat(high[rows[i]], norm_high[rows[i]]),
                cat(low[rows[i]], norm_low[rows[i]]),
            ),
        )
        for i in heads
    ]
    numerator = [x[:, :dim] for x in both]
    inverse = [1.0 / x[:, dim:] for x in both]
    scaled_wide = [upstream[:, cols[i]] * inverse[i] for i in heads]
    scaled = [x.astype(BF) for x in scaled_wide]
    products = [cat(*split(-(scaled_wide[i] * inverse[i]) * numerator[i])) for i in heads]
    ones = jnp.ones((2 * dim, dim), BF)
    norm_grad = [mm(x, ones) for x in products]
    for i in heads:
        result = numerator[i] * inverse[i]
        att_ref[:, cols[i]] = result[:own].astype(BF)
        atg_ref[:, cols[i]] = result[own:]
        sn_ref[0, :, rows[i]] = jnp.sum(
            query_rows[i].astype(F32) * norm_grad[i], axis=0, keepdims=True
        )
    lanes = [three_lanes(x, "hlh") for x in norm_grad]
    lane = lax.broadcasted_iota(jnp.int32, (length, dim), 1)
    values_lanes = cat(values, jnp.where(lane < 2, 1.0, 0.0).astype(BF))
    mixed = [mm_nt(cat(scaled[i], lanes[i]), values_lanes) for i in heads]
    block = [jnp.where(causal, x, 0.0).astype(BF) for x in mixed]
    upstream_q = [
        mm_nt(
            cat(kb_ref[0, rows[i]], high[rows[i]], norm_cols[rows[i]], low[rows[i]]),
            cat(block[i], scaled[i], lanes[i], scaled[i]),
        )
        for i in heads
    ]
    probs = [qp_ref[0, r] for r in rows]
    back = [soft_back(probs[i], upstream_q[i]) for i in heads]
    for i in heads:
        gq_ref[i * width : (i + 1) * width] = mm(back[i], queries[:, cols[i]])
        gk_ref[0, rows[i]] = mm(probs[i].astype(BF), block[i])


def key_grad_kernel(
    n, step, info, k_ref, kg_ref, v_ref, vg_ref, kp_ref, gk_ref, sn_ref,
    near, far, passed, passed_far, last, out_ref,
):
    rows, length = kp_ref.shape[1:]
    feats = k_ref.shape[1]
    values = tokens_of(v_ref, vg_ref)
    state = cat(*split(before_of(info[2 * n + 2], step < n // 2, near, far, passed, passed_far, last)))
    upstream = gk_ref[0] + mm_nt(state, cat(values, values))
    upstream = upstream + jnp.broadcast_to(column(sn_ref[0]), (rows, length))
    back = [
        soft_back(kp_ref[0, a : a + feats], upstream[a : a + feats])
        for a in range(0, rows, feats)
    ]
    out_ref[...] = mm(stack(*back), tokens_of(k_ref, kg_ref))


def attended_kernel(n, i, info, x_ref, o_ref):
    o_ref[...] = x_ref[...].astype(BF)


def out_kernel(info, *refs):
    count = len(refs) // 2 - 1
    for out_ref, pieces in zip(refs[-2:], (refs[:count], refs[count:-2])):
        for i, ref in enumerate(pieces):
            out_ref[info[i]] = ref[...]


def core_swap(x):
    size = lax.axis_size("ctx")
    return lax.ppermute(x, "ctx", [(i, i ^ 1) for i in range(size)])


def chip_move(x, pairs):
    return lax.ppermute(x, "ctx", [(2 * a + c, 2 * b + c) for a, b in pairs for c in (0, 1)])


def after(values, *earlier):
    return lax.optimization_barrier((values, earlier))[0]


class Scan:
    def __init__(self, a, b, near, forward):
        self.chips = lax.axis_size("ctx") // 2
        chip = lax.axis_index("ctx") // 2
        self.forward = forward
        self.place = chip if forward else self.chips - 1 - chip
        self.a, self.b, self.payload = a, b, near

    def move(self, x, pairs):
        last = self.chips - 1
        turn = (lambda p: p) if self.forward else (lambda p: last - p)
        return chip_move(x, [(turn(p), turn(q)) for p, q in pairs])

    def first(self):
        if self.chips == 4:
            self.near = self.move(self.payload, [(0, 1), (1, 2), (2, 3)])
            self.far = self.move(self.b, [(0, 2)])

    def pass_on(self, *earlier):
        if self.chips == 4:
            a = after(self.a, *earlier) if earlier else self.a
            self.payload = a + self.near
            self.passed = self.move(self.payload, [(1, 2)])
            self.passed_far = self.move(self.payload, [(1, 3)])

    def finish(self, *earlier):
        if self.chips == 4:
            b = after(self.b, *earlier) if earlier else self.b
            self.payload = jnp.where(self.place == 2, b + self.near + self.far, b)
            last = self.move(self.payload, [(0, 1), (2, 3)])
            return self.near, self.far, self.passed, self.passed_far, last
        total = jnp.concatenate([self.a, self.b], axis=0)
        before = self.move(total, [(i, i + 1) for i in range(self.chips - 1)])
        step = 1
        while step < self.chips:
            pairs = [(i, i + step) for i in range(self.chips - step)]
            before = before + self.move(before, pairs)
            step *= 2
        rows = self.a.shape[0]
        zero = jnp.zeros_like(self.a)
        return before[:rows], zero, zero, zero, before[rows:]


def scan_norms(norm, chip, chips, forward, *earlier):
    base = jnp.zeros_like(norm)
    if earlier and chips <= 4:
        bits = range(1, chips)
        moved = [chip_move(norm, [(i, i ^ bit) for i in range(chips)]) for bit in bits]
        moved = after(moved, *earlier)
        for bit in bits:
            other = chip ^ bit
            base = base + jnp.where(other < chip if forward else other > chip, moved[bit - 1], 0.0)
        return base
    total = norm
    bit = 1
    while bit < chips:
        moved = chip_move(total, [(i, i ^ bit) for i in range(chips)])
        upper = (chip & bit) != 0 if forward else (chip & bit) == 0
        base = base + jnp.where(upper, moved, 0.0)
        total = total + moved
        bit *= 2
    return base


def sum_all(mine, chips, *earlier):
    dp = lax.axis_size("dp")
    share = len(mine) // dp
    rows = mine[0].shape[0]
    blocks = [
        jnp.concatenate(mine[k * share : (k + 1) * share]) if share > 1 else mine[k]
        for k in range(dp)
    ]
    got = [lax.ppermute(blocks[k], "dp", [(i, i ^ k) for i in range(dp)]) for k in range(1, dp)]
    if earlier:
        got = after(got, *earlier)
    total = blocks[0]
    for piece in got:
        total = total + piece
    bit = 1
    while bit < chips:
        total = total + chip_move(total, [(i, i ^ bit) for i in range(chips)])
        bit *= 2
    pieces = [total] + [
        lax.ppermute(total, "dp", [(i, i ^ k) for i in range(dp)]) for k in range(1, dp)
    ]
    pieces = pieces + [core_swap(x) for x in pieces]
    return [x[a : a + rows] if share > 1 else x for x in pieces for a in range(0, share * rows, rows)]


def shards(queries, key_tokens, value_tokens, cotangent, query_map, key_map):
    own = queries.shape[1]
    length = 2 * own
    head_count, dim, width = query_map.shape
    shared = key_tokens.shape[2] // dim
    group = head_count // shared
    feats = 2 * width
    n = shared // 2
    wide = group * feats
    queries = queries.reshape(own, head_count * dim)
    cotangent = cotangent.reshape(own, head_count * dim)
    keys = key_tokens.reshape(own, shared * dim)
    values = value_tokens.reshape(own, shared * dim)
    query_map = jnp.swapaxes(query_map, 1, 2)
    key_map = jnp.swapaxes(key_map, 1, 2)

    ctx = lax.axis_index("ctx")
    chips = lax.axis_size("ctx") // 2
    chip, core = ctx // 2, ctx % 2
    dp = lax.axis_size("dp")
    part = jnp.arange(n, dtype=jnp.int32) ^ (lax.axis_index("dp") * (n // dp))
    places = jnp.stack([core, chip, chips - 1 - chip]) if chips == 4 else jnp.stack([core, core * 0 + 3, core * 0 + 3])
    info = jnp.concatenate([part + n * core, part + n * (1 - core), places]).astype(jnp.int32)

    def spec(shape, index):
        return pl.BlockSpec(shape, index)

    def own_cols(cols):
        return spec((own, cols), lambda i, info: (0, info[i]))

    def other_cols(cols):
        return spec((own, cols), lambda i, info: (0, info[n + i]))

    def got_cols(cols):
        return spec((own, cols), lambda i, info: (0, i))

    def per_head(*shape):
        return spec((1,) + shape, lambda i, info: (i,) + (0,) * len(shape))

    def shape_of(*shape, dtype=F32):
        return jax.ShapeDtypeStruct((n,) + shape, dtype)

    def block(ref, spec, i, info):
        places = spec.index_map(i, info)
        return ref.at[
            tuple(
                pl.ds(p * size if isinstance(p, int) else pl.multiple_of(p * size, size), size)
                for p, size in zip(places, spec.block_shape)
            )
        ]

    in_hbm = [queries, cotangent, keys, values, query_map, key_map]

    def pinned(x):
        if any(x is y for y in in_hbm):
            return pltpu.with_memory_space_constraint(x, pltpu.HBM)
        return x

    def call(name, body, in_specs, out_specs, out_shape, aliases=None):
        in_specs = [x if isinstance(x, tuple) else (x, 0, n) for x in in_specs]
        kinds = [x.dtype for x in out_shape]
        results = {}
        for (spec_, which, _), kind in zip(out_specs, kinds):
            results[which] = (spec_.block_shape, kind)
        results = [results[k] for k in range(len(results))]
        extra = len(aliases or {})

        def kernel(info, *refs):
            count = len(in_specs) + extra
            ins, outs = refs[: len(in_specs)], refs[count : count + len(out_specs)]
            rest = refs[count + len(out_specs) :]
            in_bufs, out_bufs = rest[: len(in_specs)], rest[len(in_specs) : -2]
            in_sem, out_sem = rest[-2:]

            def incoming(i):
                return [
                    pltpu.make_async_copy(
                        block(ref, spec_, i, info), buf.at[i % period], in_sem.at[k, i]
                    )
                    for k, ((spec_, start, period), ref, buf) in enumerate(zip(in_specs, ins, in_bufs))
                    if start <= i < start + period
                ]

            def outgoing(i, act):
                for k, ((spec_, which, when), ref) in enumerate(zip(out_specs, outs)):
                    here = when(i, info)
                    if here is False:
                        continue
                    copy = pltpu.make_async_copy(
                        out_bufs[which].at[i], block(ref, spec_, i, info), out_sem.at[k, i]
                    )
                    if here is True:
                        act(copy)
                    else:
                        pl.when(here)(lambda copy=copy: act(copy))

            for i in range(n):
                for copy in incoming(i):
                    copy.start()
            for i in range(n):
                for copy in incoming(i):
                    copy.wait()
                blocks = [buf.at[i % period] for (_, _, period), buf in zip(in_specs, in_bufs)]
                body(n, i, info, *blocks, *[buf.at[i] for buf in out_bufs])
                outgoing(i, lambda copy: copy.start())
            for i in range(n):
                outgoing(i, lambda copy: copy.wait())

        def run(*arrays):
            anywhere = pl.BlockSpec(memory_space=pl.ANY)
            buffers = [
                pltpu.VMEM((period,) + tuple(x.block_shape), y.dtype)
                for (x, _, period), y in zip(in_specs, arrays)
            ] + [pltpu.VMEM((n,) + tuple(shape), kind) for shape, kind in results]
            return pl.pallas_call(
                kernel,
                name=name,
                out_shape=[pltpu.HBM(x.shape, x.dtype) for x in out_shape],
                in_specs=[pl.BlockSpec(memory_space=pltpu.SMEM)] + [anywhere] * len(arrays),
                out_specs=[anywhere] * len(out_shape),
                scratch_shapes=buffers
                + [
                    pltpu.SemaphoreType.DMA((len(in_specs), n)),
                    pltpu.SemaphoreType.DMA((len(out_specs), n)),
                ],
                input_output_aliases=aliases or {},
                compiler_params=pltpu.CompilerParams(vmem_limit_bytes=VMEM_LIMIT),
            )(info, *[pinned(x) for x in arrays])

        def remember(*arrays):
            made = run(*arrays)
            in_hbm.extend(made)
            return made

        return remember

    def spread(which):
        whole = spec((group * width, dim), lambda i, info: (0, 0))
        return [(whole, which, lambda i, info, k=k: i == k) for k in range(n)]

    def always(i, info):
        return True

    def each(*specs):
        return [(x, k, always) for k, x in enumerate(specs)]

    one, four = dim, group * dim
    map_spec = spec((group, width, dim), lambda i, info: (info[i], 0, 0))
    row_spec, row = per_head(1, wide), shape_of(1, wide)
    flat_spec, flat = per_head(wide, length), shape_of(wide, length)
    half = n // 2
    half_state = jax.ShapeDtypeStruct((half * wide, dim), F32)
    half_spec = spec((wide, dim), lambda i, info: (i % half, 0))
    moved_specs = [(half_spec, start, half) for start in (0, half, 0, 0, half)]

    def states(which, place):
        return [
            (half_spec, which, lambda i, info: i < half),
            (half_spec, which, lambda i, info: i >= half),
            (half_spec, which, lambda i, info: (info[2 * n + place] == 1) == (i >= half)),
        ]

    got_keys = spec((own, one), lambda i, info: (0, info[i] % n))
    got_values = spec((own, one), lambda i, info: (1, info[i] % n))
    half_cols = n * one
    packed = jnp.concatenate(
        [lax.dynamic_slice_in_dim(x, (1 - core) * half_cols, half_cols, axis=1) for x in (keys, values)]
    )
    swapped = core_swap(packed.astype(F32))
    keys_got = values_got = swapped

    wide_flat = jax.ShapeDtypeStruct((own, n * four), F32)
    key_probs, key_features, norm, a, b, near, *packed = call(
        "key_features",
        key_kernel,
        [own_cols(one), got_keys, own_cols(one), got_values, map_spec] + [other_cols(four)] * 2,
        each(flat_spec, flat_spec, row_spec)
        + states(3, 1)
        + [(got_cols(four), 4, always), (got_cols(four), 5, always)],
        [flat, shape_of(wide, length, dtype=BF), row] + [half_state] * 3 + [wide_flat] * 2,
    )(keys, keys_got, values, values_got, key_map, queries, cotangent)
    queries_got, cotangent_got = [core_swap(x) for x in packed]
    prefix_norm = scan_norms(norm, chip, chips, True)
    prefix = Scan(*after((a, b, near), prefix_norm), True)
    prefix.first()

    rows_spec = per_head(group, length, dim)
    rows_bf = shape_of(group, length, dim, dtype=BF)
    query_probs, query_rows, weights, a, b, near = call(
        "query_features",
        query_kernel,
        [own_cols(four), got_cols(four)] * 2 + [map_spec, flat_spec, row_spec],
        each(flat_spec, rows_spec, per_head(group, length, length)) + states(3, 2),
        [flat, rows_bf, shape_of(group, length, length, dtype=BF)] + [half_state] * 3,
    )(queries, queries_got, cotangent, cotangent_got, query_map, key_features, prefix_norm)
    suffix = Scan(a, b, near, False)
    suffix.first()
    prefix.pass_on(near)
    before = prefix.finish(prefix.payload)
    suffix.pass_on()
    before = after(before, suffix.payload)
    later = suffix.finish(suffix.payload)

    grad = jax.ShapeDtypeStruct((group * width, dim), F32)
    attended, attended_got, norm, key_up, *query_part = call(
        "attend",
        attend_kernel,
        [own_cols(four), got_cols(four)] * 2
        + [own_cols(one), got_values, flat_spec, flat_spec, rows_spec]
        + [per_head(group, length, length), row_spec]
        + moved_specs,
        each(own_cols(four), got_cols(four), row_spec, flat_spec) + spread(4),
        [
            jax.ShapeDtypeStruct((own, head_count * dim), BF),
            jax.ShapeDtypeStruct((own, n * four), F32),
            row,
            flat,
        ]
        + [grad] * n,
    )(
        queries, queries_got, cotangent, cotangent_got, values, values_got, key_features,
        query_probs, query_rows, weights, prefix_norm, *before,
    )
    suffix_norm = scan_norms(norm, chip, chips, False, *query_part)
    key_part = call(
        "key_grads",
        key_grad_kernel,
        [own_cols(one), got_keys, own_cols(one), got_values]
        + [flat_spec, flat_spec, row_spec]
        + moved_specs,
        spread(0),
        [grad] * n,
    )(keys, keys_got, values, values_got, key_probs, key_up, suffix_norm, *later)
    (attended,) = call(
        "attended",
        attended_kernel,
        [got_cols(four)],
        each(other_cols(four)),
        [jax.ShapeDtypeStruct((own, head_count * dim), BF)],
        aliases={2: 0},
    )(core_swap(after(attended_got, suffix_norm, *later)), attended)

    key_pieces = sum_all(key_part, chips, attended)
    query_pieces = sum_all(after(query_part, suffix_norm), chips, *key_part)
    whole = pl.BlockSpec(memory_space=pltpu.VMEM)
    sums = pl.pallas_call(
        out_kernel,
        name="sums_out",
        out_shape=[jax.ShapeDtypeStruct((shared, group * width, dim), F32)] * 2,
        in_specs=[pl.BlockSpec(memory_space=pltpu.SMEM)] + [whole] * (2 * shared),
        out_specs=[whole] * 2,
        compiler_params=pltpu.CompilerParams(vmem_limit_bytes=VMEM_LIMIT),
    )(info, *query_pieces, *key_pieces)
    query_grad, key_grad = [
        jnp.swapaxes(x.reshape(head_count, width, dim), 1, 2) for x in sums
    ]
    return attended.reshape(1, own, head_count * dim), query_grad, key_grad


def solution(mesh):
    in_specs = (
        P("dp", "ctx", None),
        P("dp", "ctx", None),
        P("dp", "ctx", None),
        P("dp", "ctx", None),
        P(),
        P(),
    )
    out_specs = (P("dp", "ctx", None), P(), P())
    return jax.shard_map(shards, mesh=mesh, in_specs=in_specs, out_specs=out_specs, check_vma=False)
```

```python
import jax
import jax.numpy as jnp
from jax import lax
from jax.experimental import pallas as pl
from jax.experimental.pallas import tpu as pltpu
from jax.sharding import PartitionSpec as P

BF = jnp.bfloat16
F32 = jnp.float32
VMEM_LIMIT = 40 * 1024 * 1024


def mm(a, b):
    return jnp.dot(a, b, preferred_element_type=F32)


def mm_nt(a, b):
    return lax.dot_general(a, b, (((1,), (1,)), ((), ())), preferred_element_type=F32)


def split(x):
    high = x.astype(BF)
    return high, (x - high.astype(F32)).astype(BF)


def cat(*pieces):
    return jnp.concatenate(pieces, axis=1)


def stack(*pieces):
    return jnp.concatenate(pieces, axis=0)


def soft(scores):
    top = jnp.max(scores, axis=0, keepdims=True)
    raised = jnp.exp(scores - top)
    return raised * (1.0 / jnp.sum(raised, axis=0, keepdims=True))


def both_soft(scores):
    return stack(soft(scores), soft(-scores))


def soft_back(probs, upstream):
    half = probs.shape[0] // 2
    p, n = probs[:half], probs[half:]
    gp, gn = upstream[:half], upstream[half:]
    result = p * (gp - jnp.sum(p * gp, axis=0, keepdims=True))
    result = result - n * (gn - jnp.sum(n * gn, axis=0, keepdims=True))
    return result.astype(BF)


def causal_mask(core, tokens):
    own = tokens // 2
    shift = core * own
    rows = lax.broadcasted_iota(jnp.int32, (tokens, tokens), 0)
    cols = lax.broadcasted_iota(jnp.int32, (tokens, tokens), 1)
    rows = rows + jnp.where(rows < own, shift, -shift)
    cols = cols + jnp.where(cols < own, shift, -shift)
    return rows >= cols


def column(row):
    return jnp.broadcast_to(row, (8, row.shape[1])).T[:, :1]


def three_lanes(wide, order):
    lane = lax.broadcasted_iota(jnp.int32, wide.shape, 1)
    high = wide.astype(BF).astype(F32)
    parts = {"h": high, "l": wide - high}
    result = jnp.where(lane == 2, parts[order[2]], 0.0)
    result = jnp.where(lane == 1, parts[order[1]], result)
    return jnp.where(lane == 0, parts[order[0]], result).astype(BF)


def tokens_of(own_ref, got_ref):
    return stack(own_ref[...], got_ref[...].astype(BF))


def before_of(place, first, near, far, passed, passed_far, last):
    if first:
        return jnp.where(place == 2, passed[...], near[...] + passed_far[...])
    return jnp.where(place == 2, near[...] + far[...], last[...])


def key_kernel(
    n, i, info, k_ref, kg_ref, v_ref, vg_ref, w_ref, q_ref, c_ref,
    kp_ref, kb_ref, norm_ref, state_ref, qw_ref, cw_ref,
):
    group, width, dim = w_ref.shape
    keys = tokens_of(k_ref, kg_ref)
    values = tokens_of(v_ref, vg_ref)
    scores = mm_nt(w_ref[...].reshape(group * width, dim), keys)
    yield
    probs = stack(*[both_soft(scores[a : a + width]) for a in range(0, group * width, width)])
    features = probs.astype(BF)
    yield
    kp_ref[0] = probs
    kb_ref[0] = features
    norm_ref[0] = mm_nt(jnp.ones((16, keys.shape[0]), BF), features)[:1]
    state_ref[...] = mm(features, values)
    qw_ref[...] = q_ref[...].astype(F32)
    cw_ref[...] = c_ref[...].astype(F32)


def query_kernel(
    n, step, info, q_ref, qg_ref, c_ref, cg_ref, w_ref, kb_ref, pn_ref,
    qp_ref, qr_ref, wt_ref, state_ref,
):
    group, width, dim = w_ref.shape
    feats = 2 * width
    queries = tokens_of(q_ref, qg_ref)
    upstream = stack(c_ref[...].astype(F32), cg_ref[...])
    length = queries.shape[0]
    causal = causal_mask(info[2 * n], length)
    heads = range(group)
    cols = [slice(i * dim, (i + 1) * dim) for i in heads]
    rows = [slice(i * feats, (i + 1) * feats) for i in heads]
    scores = [mm_nt(w_ref[i], queries[:, cols[i]]) for i in heads]
    yield
    probs = [both_soft(x) for x in scores]
    query_t = [x.astype(BF) for x in probs]
    query_rows = [x.T for x in query_t]
    yield
    weights = [mm(query_rows[i], kb_ref[0, rows[i]]) for i in heads]
    weights = [jnp.where(causal, x, 0.0).astype(BF) for x in weights]
    yield
    norms = split(jnp.broadcast_to(pn_ref[0], (dim, group * feats)))
    ones = jnp.ones((dim, length), BF)
    den = [
        mm_nt(
            cat(weights[i], query_rows[i], query_rows[i]),
            cat(ones, norms[0][:, rows[i]], norms[1][:, rows[i]]),
        )
        for i in heads
    ]
    yield
    scaled = [(upstream[:, cols[i]] * (1.0 / den[i])).astype(BF) for i in heads]
    yield
    sums = [mm(query_t[i], scaled[i]) for i in heads]
    for i in heads:
        qp_ref[0, rows[i]] = probs[i]
        qr_ref[0, i] = query_rows[i]
        wt_ref[0, i] = weights[i]
    state_ref[...] = stack(*sums)


def attend_kernel(
    n, step, info, q_ref, qg_ref, c_ref, cg_ref, v_ref, vg_ref, kb_ref, qp_ref, qr_ref, wt_ref, pn_ref,
    near, far, passed, passed_far, last, att_ref, atg_ref, sn_ref, gk_ref, gq_ref,
):
    group, length, dim = qr_ref.shape[1:]
    feats = dim
    width = feats // 2
    own = length // 2
    heads = range(group)
    cols = [slice(i * dim, (i + 1) * dim) for i in heads]
    rows = [slice(i * feats, (i + 1) * feats) for i in heads]
    causal = causal_mask(info[2 * n], length)
    queries = tokens_of(q_ref, qg_ref)
    upstream = stack(c_ref[...].astype(F32), cg_ref[...])
    values = tokens_of(v_ref, vg_ref)
    high, low = split(before_of(info[2 * n + 1], step < n // 2, near, far, passed, passed_far, last))
    norm_wide = jnp.broadcast_to(column(pn_ref[0]), (group * feats, dim))
    norm_high, norm_low = split(norm_wide)
    norm_cols = three_lanes(norm_wide, "hhl")
    values_ones = cat(values, jnp.ones((length, dim), BF))
    query_rows = [qr_ref[0, i] for i in heads]
    both = [
        mm(
            cat(wt_ref[0, i], query_rows[i], query_rows[i]),
            stack(
                values_ones,
                cat(high[rows[i]], norm_high[rows[i]]),
                cat(low[rows[i]], norm_low[rows[i]]),
            ),
        )
        for i in heads
    ]
    yield
    numerator = [x[:, :dim] for x in both]
    inverse = [1.0 / x[:, dim:] for x in both]
    scaled_wide = [upstream[:, cols[i]] * inverse[i] for i in heads]
    scaled = [x.astype(BF) for x in scaled_wide]
    products = [cat(*split(-(scaled_wide[i] * inverse[i]) * numerator[i])) for i in heads]
    ones = jnp.ones((2 * dim, dim), BF)
    yield
    norm_grad = [mm(x, ones) for x in products]
    yield
    for i in heads:
        result = numerator[i] * inverse[i]
        att_ref[:, cols[i]] = result[:own].astype(BF)
        atg_ref[:, cols[i]] = result[own:]
        sn_ref[0, :, rows[i]] = jnp.sum(
            query_rows[i].astype(F32) * norm_grad[i], axis=0, keepdims=True
        )
    lanes = [three_lanes(x, "hlh") for x in norm_grad]
    lane = lax.broadcasted_iota(jnp.int32, (length, dim), 1)
    values_lanes = cat(values, jnp.where(lane < 2, 1.0, 0.0).astype(BF))
    mixed = [mm_nt(cat(scaled[i], lanes[i]), values_lanes) for i in heads]
    yield
    block = [jnp.where(causal, x, 0.0).astype(BF) for x in mixed]
    yield
    upstream_q = [
        mm_nt(
            cat(kb_ref[0, rows[i]], high[rows[i]], norm_cols[rows[i]], low[rows[i]]),
            cat(block[i], scaled[i], lanes[i], scaled[i]),
        )
        for i in heads
    ]
    yield
    probs = [qp_ref[0, r] for r in rows]
    back = [soft_back(probs[i], upstream_q[i]) for i in heads]
    yield
    for i in heads:
        gq_ref[i * width : (i + 1) * width] = mm(back[i], queries[:, cols[i]])
        gk_ref[0, rows[i]] = mm(probs[i].astype(BF), block[i])


def key_grad_kernel(
    n, step, info, k_ref, kg_ref, v_ref, vg_ref, kp_ref, gk_ref, sn_ref,
    near, far, passed, passed_far, last, out_ref,
):
    rows, length = kp_ref.shape[1:]
    feats = k_ref.shape[1]
    values = tokens_of(v_ref, vg_ref)
    state = cat(*split(before_of(info[2 * n + 2], step < n // 2, near, far, passed, passed_far, last)))
    upstream = gk_ref[0] + mm_nt(state, cat(values, values))
    yield
    upstream = upstream + jnp.broadcast_to(column(sn_ref[0]), (rows, length))
    back = [
        soft_back(kp_ref[0, a : a + feats], upstream[a : a + feats])
        for a in range(0, rows, feats)
    ]
    yield
    out_ref[...] = mm(stack(*back), tokens_of(k_ref, kg_ref))


def attended_kernel(n, i, info, x_ref, o_ref):
    o_ref[...] = x_ref[...].astype(BF)
    yield


def out_kernel(info, *refs):
    count = len(refs) // 2 - 1
    for out_ref, pieces in zip(refs[-2:], (refs[:count], refs[count:-2])):
        for i, ref in enumerate(pieces):
            out_ref[info[i]] = ref[...]


def core_swap(x):
    size = lax.axis_size("ctx")
    return lax.ppermute(x, "ctx", [(i, i ^ 1) for i in range(size)])


def chip_move(x, pairs):
    return lax.ppermute(x, "ctx", [(2 * a + c, 2 * b + c) for a, b in pairs for c in (0, 1)])


def after(values, *earlier):
    return lax.optimization_barrier((values, earlier))[0]


class Scan:
    def __init__(self, a, b, near, forward):
        self.chips = lax.axis_size("ctx") // 2
        chip = lax.axis_index("ctx") // 2
        self.forward = forward
        self.place = chip if forward else self.chips - 1 - chip
        self.a, self.b, self.payload = a, b, near

    def move(self, x, pairs):
        last = self.chips - 1
        turn = (lambda p: p) if self.forward else (lambda p: last - p)
        return chip_move(x, [(turn(p), turn(q)) for p, q in pairs])

    def first(self):
        if self.chips == 4:
            self.near = self.move(self.payload, [(0, 1), (1, 2), (2, 3)])
            self.far = self.move(self.b, [(0, 2)])

    def pass_on(self, *earlier):
        if self.chips == 4:
            a = after(self.a, *earlier) if earlier else self.a
            self.payload = a + self.near
            self.passed = self.move(self.payload, [(1, 2)])
            self.passed_far = self.move(self.payload, [(1, 3)])

    def finish(self, *earlier):
        if self.chips == 4:
            b = after(self.b, *earlier) if earlier else self.b
            self.payload = jnp.where(self.place == 2, b + self.near + self.far, b)
            last = self.move(self.payload, [(0, 1), (2, 3)])
            return self.near, self.far, self.passed, self.passed_far, last
        total = jnp.concatenate([self.a, self.b], axis=0)
        before = self.move(total, [(i, i + 1) for i in range(self.chips - 1)])
        step = 1
        while step < self.chips:
            pairs = [(i, i + step) for i in range(self.chips - step)]
            before = before + self.move(before, pairs)
            step *= 2
        rows = self.a.shape[0]
        zero = jnp.zeros_like(self.a)
        return before[:rows], zero, zero, zero, before[rows:]


def scan_norms(norm, chip, chips, forward, *earlier):
    base = jnp.zeros_like(norm)
    moved = norm
    if earlier and chips <= 4:
        bits = range(1, chips)
        moved = [chip_move(norm, [(i, i ^ bit) for i in range(chips)]) for bit in bits]
        moved = after(moved, *earlier)
        for bit in bits:
            other = chip ^ bit
            base = base + jnp.where(other < chip if forward else other > chip, moved[bit - 1], 0.0)
        return base, moved[-1]
    total = norm
    bit = 1
    while bit < chips:
        moved = chip_move(total, [(i, i ^ bit) for i in range(chips)])
        upper = (chip & bit) != 0 if forward else (chip & bit) == 0
        base = base + jnp.where(upper, moved, 0.0)
        total = total + moved
        bit *= 2
    return base, moved


def sum_all(mine, chips, *earlier):
    dp = lax.axis_size("dp")
    share = len(mine) // dp
    rows = mine[0].shape[0]
    blocks = [
        jnp.concatenate(mine[k * share : (k + 1) * share]) if share > 1 else mine[k]
        for k in range(dp)
    ]
    got = [lax.ppermute(blocks[k], "dp", [(i, i ^ k) for i in range(dp)]) for k in range(1, dp)]
    if earlier:
        got = after(got, *earlier)
    total = blocks[0]
    for piece in got:
        total = total + piece
    bit = 1
    while bit < chips:
        total = total + chip_move(total, [(i, i ^ bit) for i in range(chips)])
        bit *= 2
    pieces = [total] + [
        lax.ppermute(total, "dp", [(i, i ^ k) for i in range(dp)]) for k in range(1, dp)
    ]
    pieces = pieces + [core_swap(x) for x in pieces]
    return [x[a : a + rows] if share > 1 else x for x in pieces for a in range(0, share * rows, rows)]


def shards(queries, key_tokens, value_tokens, cotangent, query_map, key_map):
    own = queries.shape[1]
    length = 2 * own
    head_count, dim, width = query_map.shape
    shared = key_tokens.shape[2] // dim
    group = head_count // shared
    feats = 2 * width
    n = shared // 2
    wide = group * feats
    queries = queries.reshape(own, head_count * dim)
    cotangent = cotangent.reshape(own, head_count * dim)
    keys = key_tokens.reshape(own, shared * dim)
    values = value_tokens.reshape(own, shared * dim)
    query_map = jnp.swapaxes(query_map, 1, 2)
    key_map = jnp.swapaxes(key_map, 1, 2)

    ctx = lax.axis_index("ctx")
    chips = lax.axis_size("ctx") // 2
    chip, core = ctx // 2, ctx % 2
    dp = lax.axis_size("dp")
    part = jnp.arange(n, dtype=jnp.int32) ^ (lax.axis_index("dp") * (n // dp))
    places = jnp.stack([core, chip, chips - 1 - chip]) if chips == 4 else jnp.stack([core, core * 0 + 3, core * 0 + 3])
    info = jnp.concatenate([part + n * core, part + n * (1 - core), places]).astype(jnp.int32)

    def spec(shape, index):
        return pl.BlockSpec(shape, index)

    def own_cols(cols):
        return spec((own, cols), lambda i, info: (0, info[i]))

    def other_cols(cols):
        return spec((own, cols), lambda i, info: (0, info[n + i]))

    def got_cols(cols):
        return spec((own, cols), lambda i, info: (0, i))

    def per_head(*shape):
        return spec((1,) + shape, lambda i, info: (i,) + (0,) * len(shape))

    def shape_of(*shape, dtype=F32):
        return jax.ShapeDtypeStruct((n,) + shape, dtype)

    def block(ref, spec, i, info):
        places = spec.index_map(i, info)
        return ref.at[
            tuple(
                pl.ds(p * size if isinstance(p, int) else pl.multiple_of(p * size, size), size)
                for p, size in zip(places, spec.block_shape)
            )
        ]

    in_hbm = [queries, cotangent, keys, values, query_map, key_map]

    def pinned(x):
        if any(x is y for y in in_hbm):
            return pltpu.with_memory_space_constraint(x, pltpu.HBM)
        return x

    def call(name, body, in_specs, out_specs, out_shape, aliases=None, side_by_side=1):
        in_specs = [x if isinstance(x, tuple) else (x, 0, n) for x in in_specs]
        kinds = [x.dtype for x in out_shape]
        results = {}
        for (spec_, which, _), kind in zip(out_specs, kinds):
            results[which] = (spec_.block_shape, kind)
        results = [results[k] for k in range(len(results))]
        extra = len(aliases or {})

        def kernel(info, *refs):
            count = len(in_specs) + extra
            ins, outs = refs[: len(in_specs)], refs[count : count + len(out_specs)]
            rest = refs[count + len(out_specs) :]
            in_bufs, out_bufs = rest[: len(in_specs)], rest[len(in_specs) : -2]
            in_sem, out_sem = rest[-2:]

            def incoming(i):
                return [
                    pltpu.make_async_copy(
                        block(ref, spec_, i, info), buf.at[i % period], in_sem.at[k, i]
                    )
                    for k, ((spec_, start, period), ref, buf) in enumerate(zip(in_specs, ins, in_bufs))
                    if start <= i < start + period
                ]

            def outgoing(i, act):
                for k, ((spec_, which, when), ref) in enumerate(zip(out_specs, outs)):
                    here = when(i, info)
                    if here is False:
                        continue
                    copy = pltpu.make_async_copy(
                        out_bufs[which].at[i], block(ref, spec_, i, info), out_sem.at[k, i]
                    )
                    if here is True:
                        act(copy)
                    else:
                        pl.when(here)(lambda copy=copy: act(copy))

            for i in range(n):
                for copy in incoming(i):
                    copy.start()
            for first in range(0, n, side_by_side):
                steps = range(first, first + side_by_side)
                for i in steps:
                    for copy in incoming(i):
                        copy.wait()
                running = []
                for i in steps:
                    blocks = [buf.at[i % period] for (_, _, period), buf in zip(in_specs, in_bufs)]
                    running.append(body(n, i, info, *blocks, *[buf.at[i] for buf in out_bufs]))
                while running:
                    running = [x for x in running if next(x, True) is None]
                for i in steps:
                    outgoing(i, lambda copy: copy.start())
            for i in range(n):
                outgoing(i, lambda copy: copy.wait())

        def run(*arrays):
            anywhere = pl.BlockSpec(memory_space=pl.ANY)
            buffers = [
                pltpu.VMEM((period,) + tuple(x.block_shape), y.dtype)
                for (x, _, period), y in zip(in_specs, arrays)
            ] + [pltpu.VMEM((n,) + tuple(shape), kind) for shape, kind in results]
            return pl.pallas_call(
                kernel,
                name=name,
                out_shape=[pltpu.HBM(x.shape, x.dtype) for x in out_shape],
                in_specs=[pl.BlockSpec(memory_space=pltpu.SMEM)] + [anywhere] * len(arrays),
                out_specs=[anywhere] * len(out_shape),
                scratch_shapes=buffers
                + [
                    pltpu.SemaphoreType.DMA((len(in_specs), n)),
                    pltpu.SemaphoreType.DMA((len(out_specs), n)),
                ],
                input_output_aliases=aliases or {},
                compiler_params=pltpu.CompilerParams(vmem_limit_bytes=VMEM_LIMIT),
            )(info, *[pinned(x) for x in arrays])

        def remember(*arrays):
            made = run(*arrays)
            in_hbm.extend(made)
            return made

        return remember

    def spread(which):
        whole = spec((group * width, dim), lambda i, info: (0, 0))
        return [(whole, which, lambda i, info, k=k: i == k) for k in range(n)]

    def always(i, info):
        return True

    def each(*specs):
        return [(x, k, always) for k, x in enumerate(specs)]

    one, four = dim, group * dim
    map_spec = spec((group, width, dim), lambda i, info: (info[i], 0, 0))
    row_spec, row = per_head(1, wide), shape_of(1, wide)
    flat_spec, flat = per_head(wide, length), shape_of(wide, length)
    half = n // 2
    half_state = jax.ShapeDtypeStruct((half * wide, dim), F32)
    half_spec = spec((wide, dim), lambda i, info: (i % half, 0))
    moved_specs = [(half_spec, start, half) for start in (0, half, 0, 0, half)]

    def states(which, place):
        return [
            (half_spec, which, lambda i, info: i < half),
            (half_spec, which, lambda i, info: i >= half),
            (half_spec, which, lambda i, info: (info[2 * n + place] == 1) == (i >= half)),
        ]

    got_keys = spec((own, one), lambda i, info: (0, info[i] % n))
    got_values = spec((own, one), lambda i, info: (1, info[i] % n))
    half_cols = n * one
    packed = jnp.concatenate(
        [lax.dynamic_slice_in_dim(x, (1 - core) * half_cols, half_cols, axis=1) for x in (keys, values)]
    )
    swapped = core_swap(packed.astype(F32))
    keys_got = values_got = swapped

    wide_flat = jax.ShapeDtypeStruct((own, n * four), F32)
    key_probs, key_features, norm, a, b, near, *packed = call(
        "key_features",
        key_kernel,
        [own_cols(one), got_keys, own_cols(one), got_values, map_spec] + [other_cols(four)] * 2,
        each(flat_spec, flat_spec, row_spec)
        + states(3, 1)
        + [(got_cols(four), 4, always), (got_cols(four), 5, always)],
        [flat, shape_of(wide, length, dtype=BF), row] + [half_state] * 3 + [wide_flat] * 2,
    )(keys, keys_got, values, values_got, key_map, queries, cotangent)
    queries_got, cotangent_got = [core_swap(x) for x in packed]
    prefix_norm, norm_moved = scan_norms(norm, chip, chips, True)
    prefix = Scan(*after((a, b, near), norm_moved), True)
    prefix.first()

    rows_spec = per_head(group, length, dim)
    rows_bf = shape_of(group, length, dim, dtype=BF)
    query_probs, query_rows, weights, a, b, near = call(
        "query_features",
        query_kernel,
        [own_cols(four), got_cols(four)] * 2 + [map_spec, flat_spec, row_spec],
        each(flat_spec, rows_spec, per_head(group, length, length)) + states(3, 2),
        [flat, rows_bf, shape_of(group, length, length, dtype=BF)] + [half_state] * 3,
        side_by_side=2,
    )(queries, queries_got, cotangent, cotangent_got, query_map, key_features, prefix_norm)
    suffix = Scan(a, b, near, False)
    suffix.first()
    prefix.pass_on(near)
    before = prefix.finish(prefix.payload)
    suffix.pass_on()
    before = after(before, suffix.payload)
    later = suffix.finish(suffix.payload)

    grad = jax.ShapeDtypeStruct((group * width, dim), F32)
    attended, attended_got, norm, key_up, *query_part = call(
        "attend",
        attend_kernel,
        [own_cols(four), got_cols(four)] * 2
        + [own_cols(one), got_values, flat_spec, flat_spec, rows_spec]
        + [per_head(group, length, length), row_spec]
        + moved_specs,
        each(own_cols(four), got_cols(four), row_spec, flat_spec) + spread(4),
        [
            jax.ShapeDtypeStruct((own, head_count * dim), BF),
            jax.ShapeDtypeStruct((own, n * four), F32),
            row,
            flat,
        ]
        + [grad] * n,
    )(
        queries, queries_got, cotangent, cotangent_got, values, values_got, key_features,
        query_probs, query_rows, weights, prefix_norm, *before,
    )
    suffix_norm, _ = scan_norms(norm, chip, chips, False, *query_part)
    key_part = call(
        "key_grads",
        key_grad_kernel,
        [own_cols(one), got_keys, own_cols(one), got_values]
        + [flat_spec, flat_spec, row_spec]
        + moved_specs,
        spread(0),
        [grad] * n,
        side_by_side=2,
    )(keys, keys_got, values, values_got, key_probs, key_up, suffix_norm, *later)
    (attended,) = call(
        "attended",
        attended_kernel,
        [got_cols(four)],
        each(other_cols(four)),
        [jax.ShapeDtypeStruct((own, head_count * dim), BF)],
        aliases={2: 0},
    )(core_swap(after(attended_got, suffix_norm, *later)), attended)

    key_pieces = sum_all(key_part, chips, attended)
    query_pieces = sum_all(after(query_part, suffix_norm), chips, *key_part)
    whole = pl.BlockSpec(memory_space=pltpu.VMEM)
    sums = pl.pallas_call(
        out_kernel,
        name="sums_out",
        out_shape=[jax.ShapeDtypeStruct((shared, group * width, dim), F32)] * 2,
        in_specs=[pl.BlockSpec(memory_space=pltpu.SMEM)] + [whole] * (2 * shared),
        out_specs=[whole] * 2,
        compiler_params=pltpu.CompilerParams(vmem_limit_bytes=VMEM_LIMIT),
    )(info, *query_pieces, *key_pieces)
    query_grad, key_grad = [
        jnp.swapaxes(x.reshape(head_count, width, dim), 1, 2) for x in sums
    ]
    return attended.reshape(1, own, head_count * dim), query_grad, key_grad


def solution(mesh):
    in_specs = (
        P("dp", "ctx", None),
        P("dp", "ctx", None),
        P("dp", "ctx", None),
        P("dp", "ctx", None),
        P(),
        P(),
    )
    out_specs = (P("dp", "ctx", None), P(), P())
    return jax.shard_map(shards, mesh=mesh, in_specs=in_specs, out_specs=out_specs, check_vma=False)
```

```python
import jax
import jax.numpy as jnp
from jax import lax
from jax.experimental import pallas as pl
from jax.experimental.pallas import tpu as pltpu
from jax.sharding import PartitionSpec as P

BF = jnp.bfloat16
F32 = jnp.float32
VMEM_LIMIT = 40 * 1024 * 1024


def mm(a, b):
    return jnp.dot(a, b, preferred_element_type=F32)


def mm_nt(a, b):
    return lax.dot_general(a, b, (((1,), (1,)), ((), ())), preferred_element_type=F32)


def split(x):
    high = x.astype(BF)
    return high, (x - high.astype(F32)).astype(BF)


def cat(*pieces):
    return jnp.concatenate(pieces, axis=1)


def stack(*pieces):
    return jnp.concatenate(pieces, axis=0)


def soft(scores):
    top = jnp.max(scores, axis=0, keepdims=True)
    raised = jnp.exp(scores - top)
    return raised * (1.0 / jnp.sum(raised, axis=0, keepdims=True))


def both_soft(scores):
    return stack(soft(scores), soft(-scores))


def soft_back(probs, upstream):
    half = probs.shape[0] // 2
    p, n = probs[:half].astype(F32), probs[half:].astype(F32)
    gp, gn = upstream[:half], upstream[half:]
    mean_p = jnp.sum(p * gp, axis=0, keepdims=True) / jnp.sum(p, axis=0, keepdims=True)
    mean_n = jnp.sum(n * gn, axis=0, keepdims=True) / jnp.sum(n, axis=0, keepdims=True)
    return (p * (gp - mean_p) - n * (gn - mean_n)).astype(BF)


def causal_mask(core, tokens):
    own = tokens // 2
    shift = core * own
    rows = lax.broadcasted_iota(jnp.int32, (tokens, tokens), 0)
    cols = lax.broadcasted_iota(jnp.int32, (tokens, tokens), 1)
    rows = rows + jnp.where(rows < own, shift, -shift)
    cols = cols + jnp.where(cols < own, shift, -shift)
    return rows >= cols


def column(row):
    return jnp.broadcast_to(row, (8, row.shape[1])).T[:, :1]


def three_lanes(wide, order):
    lane = lax.broadcasted_iota(jnp.int32, wide.shape, 1)
    high = wide.astype(BF).astype(F32)
    parts = {"h": high, "l": wide - high}
    result = jnp.where(lane == 2, parts[order[2]], 0.0)
    result = jnp.where(lane == 1, parts[order[1]], result)
    return jnp.where(lane == 0, parts[order[0]], result).astype(BF)


def tokens_of(own_ref, got_ref):
    return stack(own_ref[...], got_ref[...].astype(BF))


def before_of(place, first, near, far, passed, passed_far, last):
    if first:
        return jnp.where(place == 2, passed[...], near[...] + passed_far[...])
    return jnp.where(place == 2, near[...] + far[...], last[...])


def key_kernel(
    n, i, info, k_ref, kg_ref, v_ref, vg_ref, w_ref, q_ref, c_ref,
    kb_ref, norm_ref, state_ref, qw_ref, cw_ref,
):
    group, width, dim = w_ref.shape
    keys = tokens_of(k_ref, kg_ref)
    values = tokens_of(v_ref, vg_ref)
    scores = mm_nt(w_ref[...].reshape(group * width, dim), keys)
    probs = stack(*[both_soft(scores[a : a + width]) for a in range(0, group * width, width)])
    features = probs.astype(BF)
    kb_ref[0] = features
    norm_ref[0] = mm_nt(jnp.ones((16, keys.shape[0]), BF), features)[:1]
    state_ref[...] = mm(features, values)
    qw_ref[...] = q_ref[...].astype(F32)
    cw_ref[...] = c_ref[...].astype(F32)


def query_kernel(
    n, step, info, q_ref, qg_ref, c_ref, cg_ref, w_ref, kb_ref, pn_ref,
    qp_ref, qr_ref, wt_ref, state_ref,
):
    group, width, dim = w_ref.shape
    feats = 2 * width
    queries = tokens_of(q_ref, qg_ref)
    upstream = stack(c_ref[...].astype(F32), cg_ref[...])
    length = queries.shape[0]
    causal = causal_mask(info[2 * n], length)
    heads = range(group)
    cols = [slice(i * dim, (i + 1) * dim) for i in heads]
    rows = [slice(i * feats, (i + 1) * feats) for i in heads]
    scores = [mm_nt(w_ref[i], queries[:, cols[i]]) for i in heads]
    probs = [both_soft(x) for x in scores]
    query_t = [x.astype(BF) for x in probs]
    query_rows = [x.T for x in query_t]
    weights = [mm(query_rows[i], kb_ref[0, rows[i]]) for i in heads]
    weights = [jnp.where(causal, x, 0.0).astype(BF) for x in weights]
    norms = split(jnp.broadcast_to(pn_ref[0], (dim, group * feats)))
    ones = jnp.ones((dim, length), BF)
    den = [
        mm_nt(
            cat(weights[i], query_rows[i], query_rows[i]),
            cat(ones, norms[0][:, rows[i]], norms[1][:, rows[i]]),
        )
        for i in heads
    ]
    scaled = [(upstream[:, cols[i]] * (1.0 / den[i])).astype(BF) for i in heads]
    sums = [mm(query_t[i], scaled[i]) for i in heads]
    for i in heads:
        qp_ref[0, rows[i]] = query_t[i]
        qr_ref[0, i] = query_rows[i]
        wt_ref[0, i] = weights[i]
    state_ref[...] = stack(*sums)


def attend_kernel(
    n, step, info, q_ref, qg_ref, c_ref, cg_ref, v_ref, vg_ref, kb_ref, qp_ref, qr_ref, wt_ref, pn_ref,
    near, far, passed, passed_far, last, att_ref, atg_ref, sn_ref, gk_ref, gq_ref,
):
    group, length, dim = qr_ref.shape[1:]
    feats = dim
    width = feats // 2
    own = length // 2
    heads = range(group)
    cols = [slice(i * dim, (i + 1) * dim) for i in heads]
    rows = [slice(i * feats, (i + 1) * feats) for i in heads]
    causal = causal_mask(info[2 * n], length)
    queries = tokens_of(q_ref, qg_ref)
    upstream = stack(c_ref[...].astype(F32), cg_ref[...])
    values = tokens_of(v_ref, vg_ref)
    high, low = split(before_of(info[2 * n + 1], step < n // 2, near, far, passed, passed_far, last))
    norm_wide = jnp.broadcast_to(column(pn_ref[0]), (group * feats, dim))
    norm_high, norm_low = split(norm_wide)
    norm_cols = three_lanes(norm_wide, "hhl")
    values_ones = cat(values, jnp.ones((length, dim), BF))
    query_rows = [qr_ref[0, i] for i in heads]
    both = [
        mm(
            cat(wt_ref[0, i], query_rows[i], query_rows[i]),
            stack(
                values_ones,
                cat(high[rows[i]], norm_high[rows[i]]),
                cat(low[rows[i]], norm_low[rows[i]]),
            ),
        )
        for i in heads
    ]
    numerator = [x[:, :dim] for x in both]
    inverse = [1.0 / x[:, dim:] for x in both]
    scaled_wide = [upstream[:, cols[i]] * inverse[i] for i in heads]
    scaled = [x.astype(BF) for x in scaled_wide]
    products = [cat(*split(-(scaled_wide[i] * inverse[i]) * numerator[i])) for i in heads]
    ones = jnp.ones((2 * dim, dim), BF)
    norm_grad = [mm(x, ones) for x in products]
    for i in heads:
        result = numerator[i] * inverse[i]
        att_ref[:, cols[i]] = result[:own].astype(BF)
        atg_ref[:, cols[i]] = result[own:]
        sn_ref[0, :, rows[i]] = jnp.sum(
            query_rows[i].astype(F32) * norm_grad[i], axis=0, keepdims=True
        )
    lanes = [three_lanes(x, "hlh") for x in norm_grad]
    lane = lax.broadcasted_iota(jnp.int32, (length, dim), 1)
    values_lanes = cat(values, jnp.where(lane < 2, 1.0, 0.0).astype(BF))
    mixed = [mm_nt(cat(scaled[i], lanes[i]), values_lanes) for i in heads]
    block = [jnp.where(causal, x, 0.0).astype(BF) for x in mixed]
    upstream_q = [
        mm_nt(
            cat(kb_ref[0, rows[i]], high[rows[i]], norm_cols[rows[i]], low[rows[i]]),
            cat(block[i], scaled[i], lanes[i], scaled[i]),
        )
        for i in heads
    ]
    probs = [qp_ref[0, r] for r in rows]
    back = [soft_back(probs[i], upstream_q[i]) for i in heads]
    for i in heads:
        gq_ref[i * width : (i + 1) * width] = mm(back[i], queries[:, cols[i]])
        gk_ref[0, rows[i]] = mm(probs[i], block[i])


def key_grad_kernel(
    n, step, info, k_ref, kg_ref, v_ref, vg_ref, kp_ref, gk_ref, sn_ref,
    near, far, passed, passed_far, last, out_ref,
):
    rows, length = kp_ref.shape[1:]
    feats = k_ref.shape[1]
    values = tokens_of(v_ref, vg_ref)
    state = cat(*split(before_of(info[2 * n + 2], step < n // 2, near, far, passed, passed_far, last)))
    upstream = gk_ref[0] + mm_nt(state, cat(values, values))
    upstream = upstream + jnp.broadcast_to(column(sn_ref[0]), (rows, length))
    back = [
        soft_back(kp_ref[0, a : a + feats], upstream[a : a + feats])
        for a in range(0, rows, feats)
    ]
    out_ref[...] = mm(stack(*back), tokens_of(k_ref, kg_ref))


def attended_kernel(n, i, info, x_ref, o_ref):
    o_ref[...] = x_ref[...].astype(BF)


def out_kernel(info, *refs):
    count = len(refs) // 2 - 1
    for out_ref, pieces in zip(refs[-2:], (refs[:count], refs[count:-2])):
        for i, ref in enumerate(pieces):
            out_ref[info[i]] = ref[...]


def core_swap(x):
    size = lax.axis_size("ctx")
    return lax.ppermute(x, "ctx", [(i, i ^ 1) for i in range(size)])


def chip_move(x, pairs):
    return lax.ppermute(x, "ctx", [(2 * a + c, 2 * b + c) for a, b in pairs for c in (0, 1)])


def after(values, *earlier):
    return lax.optimization_barrier((values, earlier))[0]


class Scan:
    def __init__(self, a, b, near, forward):
        self.chips = lax.axis_size("ctx") // 2
        chip = lax.axis_index("ctx") // 2
        self.forward = forward
        self.place = chip if forward else self.chips - 1 - chip
        self.a, self.b, self.payload = a, b, near

    def move(self, x, pairs):
        last = self.chips - 1
        turn = (lambda p: p) if self.forward else (lambda p: last - p)
        return chip_move(x, [(turn(p), turn(q)) for p, q in pairs])

    def first(self):
        if self.chips == 4:
            self.near = self.move(self.payload, [(0, 1), (1, 2), (2, 3)])
            self.far = self.move(self.b, [(0, 2)])

    def pass_on(self, *earlier):
        if self.chips == 4:
            a = after(self.a, *earlier) if earlier else self.a
            self.payload = a + self.near
            self.passed = self.move(self.payload, [(1, 2)])
            self.passed_far = self.move(self.payload, [(1, 3)])

    def finish(self, *earlier):
        if self.chips == 4:
            b = after(self.b, *earlier) if earlier else self.b
            self.payload = jnp.where(self.place == 2, b + self.near + self.far, b)
            last = self.move(self.payload, [(0, 1), (2, 3)])
            return self.near, self.far, self.passed, self.passed_far, last
        total = jnp.concatenate([self.a, self.b], axis=0)
        before = self.move(total, [(i, i + 1) for i in range(self.chips - 1)])
        step = 1
        while step < self.chips:
            pairs = [(i, i + step) for i in range(self.chips - step)]
            before = before + self.move(before, pairs)
            step *= 2
        rows = self.a.shape[0]
        zero = jnp.zeros_like(self.a)
        return before[:rows], zero, zero, zero, before[rows:]


def scan_norms(norm, chip, chips, forward, *earlier):
    base = jnp.zeros_like(norm)
    if earlier and chips <= 4:
        bits = range(1, chips)
        moved = [chip_move(norm, [(i, i ^ bit) for i in range(chips)]) for bit in bits]
        moved = after(moved, *earlier)
        for bit in bits:
            other = chip ^ bit
            base = base + jnp.where(other < chip if forward else other > chip, moved[bit - 1], 0.0)
        return base
    total = norm
    bit = 1
    while bit < chips:
        moved = chip_move(total, [(i, i ^ bit) for i in range(chips)])
        upper = (chip & bit) != 0 if forward else (chip & bit) == 0
        base = base + jnp.where(upper, moved, 0.0)
        total = total + moved
        bit *= 2
    return base


def sum_all(mine, chips, *earlier):
    dp = lax.axis_size("dp")
    share = len(mine) // dp
    rows = mine[0].shape[0]
    blocks = [
        jnp.concatenate(mine[k * share : (k + 1) * share]) if share > 1 else mine[k]
        for k in range(dp)
    ]
    got = [lax.ppermute(blocks[k], "dp", [(i, i ^ k) for i in range(dp)]) for k in range(1, dp)]
    if earlier:
        got = after(got, *earlier)
    total = blocks[0]
    for piece in got:
        total = total + piece
    bit = 1
    while bit < chips:
        total = total + chip_move(total, [(i, i ^ bit) for i in range(chips)])
        bit *= 2
    pieces = [total] + [
        lax.ppermute(total, "dp", [(i, i ^ k) for i in range(dp)]) for k in range(1, dp)
    ]
    pieces = pieces + [core_swap(x) for x in pieces]
    return [x[a : a + rows] if share > 1 else x for x in pieces for a in range(0, share * rows, rows)]


def shards(queries, key_tokens, value_tokens, cotangent, query_map, key_map):
    own = queries.shape[1]
    length = 2 * own
    head_count, dim, width = query_map.shape
    shared = key_tokens.shape[2] // dim
    group = head_count // shared
    feats = 2 * width
    n = shared // 2
    wide = group * feats
    queries = queries.reshape(own, head_count * dim)
    cotangent = cotangent.reshape(own, head_count * dim)
    keys = key_tokens.reshape(own, shared * dim)
    values = value_tokens.reshape(own, shared * dim)
    query_map = jnp.swapaxes(query_map, 1, 2)
    key_map = jnp.swapaxes(key_map, 1, 2)

    ctx = lax.axis_index("ctx")
    chips = lax.axis_size("ctx") // 2
    chip, core = ctx // 2, ctx % 2
    dp = lax.axis_size("dp")
    part = jnp.arange(n, dtype=jnp.int32) ^ (lax.axis_index("dp") * (n // dp))
    places = jnp.stack([core, chip, chips - 1 - chip]) if chips == 4 else jnp.stack([core, core * 0 + 3, core * 0 + 3])
    info = jnp.concatenate([part + n * core, part + n * (1 - core), places]).astype(jnp.int32)

    def spec(shape, index):
        return pl.BlockSpec(shape, index)

    def own_cols(cols):
        return spec((own, cols), lambda i, info: (0, info[i]))

    def other_cols(cols):
        return spec((own, cols), lambda i, info: (0, info[n + i]))

    def got_cols(cols):
        return spec((own, cols), lambda i, info: (0, i))

    def per_head(*shape):
        return spec((1,) + shape, lambda i, info: (i,) + (0,) * len(shape))

    def shape_of(*shape, dtype=F32):
        return jax.ShapeDtypeStruct((n,) + shape, dtype)

    def block(ref, spec, i, info):
        places = spec.index_map(i, info)
        return ref.at[
            tuple(
                pl.ds(p * size if isinstance(p, int) else pl.multiple_of(p * size, size), size)
                for p, size in zip(places, spec.block_shape)
            )
        ]

    in_hbm = [queries, cotangent, keys, values, query_map, key_map]

    def pinned(x):
        if any(x is y for y in in_hbm):
            return pltpu.with_memory_space_constraint(x, pltpu.HBM)
        return x

    def call(name, body, in_specs, out_specs, out_shape, aliases=None):
        in_specs = [x if isinstance(x, tuple) else (x, 0, n) for x in in_specs]
        kinds = [x.dtype for x in out_shape]
        results = {}
        for (spec_, which, _), kind in zip(out_specs, kinds):
            results[which] = (spec_.block_shape, kind)
        results = [results[k] for k in range(len(results))]
        extra = len(aliases or {})

        def kernel(info, *refs):
            count = len(in_specs) + extra
            ins, outs = refs[: len(in_specs)], refs[count : count + len(out_specs)]
            rest = refs[count + len(out_specs) :]
            in_bufs, out_bufs = rest[: len(in_specs)], rest[len(in_specs) : -2]
            in_sem, out_sem = rest[-2:]

            def incoming(i):
                return [
                    pltpu.make_async_copy(
                        block(ref, spec_, i, info), buf.at[i % period], in_sem.at[k, i]
                    )
                    for k, ((spec_, start, period), ref, buf) in enumerate(zip(in_specs, ins, in_bufs))
                    if start <= i < start + period
                ]

            def outgoing(i, act):
                for k, ((spec_, which, when), ref) in enumerate(zip(out_specs, outs)):
                    here = when(i, info)
                    if here is False:
                        continue
                    copy = pltpu.make_async_copy(
                        out_bufs[which].at[i], block(ref, spec_, i, info), out_sem.at[k, i]
                    )
                    if here is True:
                        act(copy)
                    else:
                        pl.when(here)(lambda copy=copy: act(copy))

            for i in range(n):
                for copy in incoming(i):
                    copy.start()
            for i in range(n):
                for copy in incoming(i):
                    copy.wait()
                blocks = [buf.at[i % period] for (_, _, period), buf in zip(in_specs, in_bufs)]
                body(n, i, info, *blocks, *[buf.at[i] for buf in out_bufs])
                outgoing(i, lambda copy: copy.start())
            for i in range(n):
                outgoing(i, lambda copy: copy.wait())

        def run(*arrays):
            anywhere = pl.BlockSpec(memory_space=pl.ANY)
            buffers = [
                pltpu.VMEM((period,) + tuple(x.block_shape), y.dtype)
                for (x, _, period), y in zip(in_specs, arrays)
            ] + [pltpu.VMEM((n,) + tuple(shape), kind) for shape, kind in results]
            return pl.pallas_call(
                kernel,
                name=name,
                out_shape=[pltpu.HBM(x.shape, x.dtype) for x in out_shape],
                in_specs=[pl.BlockSpec(memory_space=pltpu.SMEM)] + [anywhere] * len(arrays),
                out_specs=[anywhere] * len(out_shape),
                scratch_shapes=buffers
                + [
                    pltpu.SemaphoreType.DMA((len(in_specs), n)),
                    pltpu.SemaphoreType.DMA((len(out_specs), n)),
                ],
                input_output_aliases=aliases or {},
                compiler_params=pltpu.CompilerParams(vmem_limit_bytes=VMEM_LIMIT),
            )(info, *[pinned(x) for x in arrays])

        def remember(*arrays):
            made = run(*arrays)
            in_hbm.extend(made)
            return made

        return remember

    def spread(which):
        whole = spec((group * width, dim), lambda i, info: (0, 0))
        return [(whole, which, lambda i, info, k=k: i == k) for k in range(n)]

    def always(i, info):
        return True

    def each(*specs):
        return [(x, k, always) for k, x in enumerate(specs)]

    one, four = dim, group * dim
    map_spec = spec((group, width, dim), lambda i, info: (info[i], 0, 0))
    row_spec, row = per_head(1, wide), shape_of(1, wide)
    flat_spec, flat = per_head(wide, length), shape_of(wide, length)
    half = n // 2
    half_state = jax.ShapeDtypeStruct((half * wide, dim), F32)
    half_spec = spec((wide, dim), lambda i, info: (i % half, 0))
    moved_specs = [(half_spec, start, half) for start in (0, half, 0, 0, half)]

    def states(which, place):
        return [
            (half_spec, which, lambda i, info: i < half),
            (half_spec, which, lambda i, info: i >= half),
            (half_spec, which, lambda i, info: (info[2 * n + place] == 1) == (i >= half)),
        ]

    got_keys = spec((own, one), lambda i, info: (0, info[i] % n))
    got_values = spec((own, one), lambda i, info: (1, info[i] % n))
    half_cols = n * one
    packed = jnp.concatenate(
        [lax.dynamic_slice_in_dim(x, (1 - core) * half_cols, half_cols, axis=1) for x in (keys, values)]
    )
    swapped = core_swap(packed.astype(F32))
    keys_got = values_got = swapped

    flat_bf = shape_of(wide, length, dtype=BF)
    wide_flat = jax.ShapeDtypeStruct((own, n * four), F32)
    key_features, norm, a, b, near, *packed = call(
        "key_features",
        key_kernel,
        [own_cols(one), got_keys, own_cols(one), got_values, map_spec] + [other_cols(four)] * 2,
        each(flat_spec, row_spec)
        + states(2, 1)
        + [(got_cols(four), 3, always), (got_cols(four), 4, always)],
        [flat_bf, row] + [half_state] * 3 + [wide_flat] * 2,
    )(keys, keys_got, values, values_got, key_map, queries, cotangent)
    queries_got, cotangent_got = [core_swap(x) for x in packed]
    prefix_norm = scan_norms(norm, chip, chips, True)
    prefix = Scan(*after((a, b, near), prefix_norm), True)
    prefix.first()

    rows_spec = per_head(group, length, dim)
    rows_bf = shape_of(group, length, dim, dtype=BF)
    query_probs, query_rows, weights, a, b, near = call(
        "query_features",
        query_kernel,
        [own_cols(four), got_cols(four)] * 2 + [map_spec, flat_spec, row_spec],
        each(flat_spec, rows_spec, per_head(group, length, length)) + states(3, 2),
        [flat_bf, rows_bf, shape_of(group, length, length, dtype=BF)] + [half_state] * 3,
    )(queries, queries_got, cotangent, cotangent_got, query_map, key_features, prefix_norm)
    suffix = Scan(a, b, near, False)
    suffix.first()
    prefix.pass_on(near)
    before = prefix.finish(prefix.payload)
    suffix.pass_on()
    before = after(before, suffix.payload)
    later = suffix.finish(suffix.payload)

    grad = jax.ShapeDtypeStruct((group * width, dim), F32)
    attended, attended_got, norm, key_up, *query_part = call(
        "attend",
        attend_kernel,
        [own_cols(four), got_cols(four)] * 2
        + [own_cols(one), got_values, flat_spec, flat_spec, rows_spec]
        + [per_head(group, length, length), row_spec]
        + moved_specs,
        each(own_cols(four), got_cols(four), row_spec, flat_spec) + spread(4),
        [
            jax.ShapeDtypeStruct((own, head_count * dim), BF),
            jax.ShapeDtypeStruct((own, n * four), F32),
            row,
            flat,
        ]
        + [grad] * n,
    )(
        queries, queries_got, cotangent, cotangent_got, values, values_got, key_features,
        query_probs, query_rows, weights, prefix_norm, *before,
    )
    suffix_norm = scan_norms(norm, chip, chips, False, *query_part)
    key_part = call(
        "key_grads",
        key_grad_kernel,
        [own_cols(one), got_keys, own_cols(one), got_values]
        + [flat_spec, flat_spec, row_spec]
        + moved_specs,
        spread(0),
        [grad] * n,
    )(keys, keys_got, values, values_got, key_features, key_up, suffix_norm, *later)
    (attended,) = call(
        "attended",
        attended_kernel,
        [got_cols(four)],
        each(other_cols(four)),
        [jax.ShapeDtypeStruct((own, head_count * dim), BF)],
        aliases={2: 0},
    )(core_swap(after(attended_got, suffix_norm, *later)), attended)

    key_pieces = sum_all(key_part, chips, attended)
    query_pieces = sum_all(after(query_part, suffix_norm), chips, *key_part)
    whole = pl.BlockSpec(memory_space=pltpu.VMEM)
    sums = pl.pallas_call(
        out_kernel,
        name="sums_out",
        out_shape=[jax.ShapeDtypeStruct((shared, group * width, dim), F32)] * 2,
        in_specs=[pl.BlockSpec(memory_space=pltpu.SMEM)] + [whole] * (2 * shared),
        out_specs=[whole] * 2,
        compiler_params=pltpu.CompilerParams(vmem_limit_bytes=VMEM_LIMIT),
    )(info, *query_pieces, *key_pieces)
    query_grad, key_grad = [
        jnp.swapaxes(x.reshape(head_count, width, dim), 1, 2) for x in sums
    ]
    return attended.reshape(1, own, head_count * dim), query_grad, key_grad


def solution(mesh):
    in_specs = (
        P("dp", "ctx", None),
        P("dp", "ctx", None),
        P("dp", "ctx", None),
        P("dp", "ctx", None),
        P(),
        P(),
    )
    out_specs = (P("dp", "ctx", None), P(), P())
    return jax.shard_map(shards, mesh=mesh, in_specs=in_specs, out_specs=out_specs, check_vma=False)
```
